32 devices in a mesh: parts: 2 (over y), src: 4 (over z), tgt: 2 (over x), rep: 2 (over core).
Axes of the slice: x: 2, y: 2, z: 4, core: 2. Of those that a mesh axis runs over, the one named last changes fastest.
Arguments:
- acts: bfloat16 [1024, 4096], P(('parts', 'rep'), 'src'), parts along dimension 0, may hold values from -6 to 6
- enc_w: bfloat16 [4096, 1024], P('src', 'tgt'), may hold values from -0.09375 to 0.09375
- enc_b: float32 [1024], P('tgt'), may hold values from -3 to 3
- dec_w: bfloat16 [2, 2, 512, 4096], P(None, None, 'src', 'tgt'), may hold values from -0.375 to 0.375
- dec_b: float32 [2, 4096], P(None, 'tgt'), may hold values from -2 to 2
- targets: bfloat16 [2, 1024, 4096], P(None, ('parts', 'rep', 'src'), 'tgt'), parts along dimension 1, may hold values from -3 to 3
- active: int32 [8, 8], P(('parts', 'rep')), parts along dimension 0, may hold values from -1 to 7, as said below
Outputs:
- error: bfloat16 [2, 1024, 4096], P(None, ('parts', 'rep', 'src'), 'tgt'), parts along dimension 1
The draws below stay inside these ranges and needn't reach their ends.
There are 2 independent parts, one for each index of `parts`. The reference program is written for one: setup_inputs(seed, part) draws one part's arguments, and reference() takes and returns one part's arrays. A program takes and returns all parts, laid end to end along the dimension named above; an argument that names none is the same for every part. Nothing has to cross between parts.
Inputs may be any that keep to these rules, and one draw needn't show every extreme that they name: `active`: each row lists distinct blocks in ascending order, then -1 in the empty slots. In each aligned group of 2 tiles (the tiles of one token half) a block is listed by at most 2 tiles, and some block by exactly 2.
All inputs are finite; a program needn't handle non-finite values.
Results may differ from the reference program's by a relative error of at most 0.015.
Values may be sent and summed in bfloat16 or wider, within the bound.
No kernel may reach another device: no remote copies, remote signals or barrier semaphores. Data moves between devices by JAX's collectives and lax.ppermute only.
A program may use at most 64 MiB of HBM per device.

```python
import jax
import jax.numpy as jnp
from jax import lax

D = 4096
BLK = 128
TL = 2
TILE = 128
M_TILE = 2
TOK_DEV = 256
LAT = 1024
SUB = 512
TGRP = 2
NBLK = 8
K_ACT = 8
TOKENS = 512
TILES = 4
N_SRC = 4


def draw_active(key, part):
    key = jax.random.fold_in(key, 7)
    per_group = TOK_DEV // TILE
    groups = TILES // per_group
    key_count, key_full, key_order = jax.random.split(key, 3)
    counts = jax.random.randint(key_count, (groups, NBLK), 0, M_TILE + 1)
    fullest = jax.random.randint(key_full, (groups, 1), 0, NBLK)
    counts = jnp.where(jnp.arange(NBLK)[None, :] == fullest, M_TILE, counts)
    scores = jax.random.randint(key_order, (groups, NBLK, per_group), 0, 1 << 20) * per_group + jnp.arange(per_group)[None, None, :]
    places = jnp.argsort(jnp.argsort(scores, axis=2), axis=2)
    chosen = places < counts[:, :, None]
    flags = jnp.transpose(chosen, (0, 2, 1)).reshape(TILES, NBLK)
    ranked = jnp.where(flags, jnp.arange(NBLK)[None, :], NBLK + jnp.arange(NBLK)[None, :])
    ordered = jnp.sort(ranked, axis=1)
    return jnp.where(ordered < NBLK, ordered, -1).astype(jnp.int32)[:, :K_ACT]


def levels(key, extent, pieces, smallest, top_value):
    level = 1.0
    for position, parts in pieces:
        draws = jax.random.uniform(jax.random.fold_in(jax.random.fold_in(key, 6), position), (parts,), jnp.float32, smallest / len(pieces), top_value / len(pieces))
        level = level * jnp.repeat(jnp.exp(draws), extent[position] // parts).reshape((-1,) + (1,) * (len(extent) - 1 - position))
    return level


def gaussian(rng, extent, scale, reach, pieces=(), kind=jnp.bfloat16):
    result = scale * jax.random.normal(rng, extent, jnp.float32)
    if pieces:
        result = result * levels(rng, extent, pieces, -0.22, 0.18)
    return jnp.clip(result, -reach, reach).astype(kind)


def setup_inputs(seed: int = 0, part: int = 0) -> dict:
    key_list = jax.random.split(jax.random.key(seed), 8)
    own_keys = jax.random.split(jax.random.fold_in(key_list[7], part), 8)
    return {
        "acts": gaussian(own_keys[0], (TOKENS, D), 1.0, 6.0, ((0, 2), (1, 4))),
        "enc_w": gaussian(key_list[1], (D, LAT), D ** -0.5, 0.09375, ((0, 4), (1, 2))),
        "enc_b": gaussian(key_list[2], (LAT,), 0.5, 3.0, ((0, 2),), jnp.float32),
        "dec_w": gaussian(key_list[3], (TL, TGRP, SUB, D), (LAT // 4) ** -0.5, 0.375, ((2, 4), (3, 2))),
        "dec_b": gaussian(key_list[4], (TL, D), 0.3, 2.0, ((1, 2),), jnp.float32),
        "targets": gaussian(own_keys[5], (TL, TOKENS, D), 0.5, 3.0, ((1, 8), (2, 2))),
        "active": draw_active(jax.random.fold_in(jax.random.fold_in(key_list[7], part), 71), part),
    }


def reference(acts, enc_w, enc_b, dec_w, dec_b, targets, active):
    width = D // N_SRC

    def enc_step(total, group):
        columns = lax.dynamic_slice_in_dim(acts, group * width, width, 1)
        weights = lax.dynamic_slice_in_dim(enc_w, group * width, width, 0)
        term = jnp.dot(columns, weights, preferred_element_type=jnp.float32).astype(jnp.bfloat16)
        term = lax.optimization_barrier(term)
        return total + term.astype(jnp.float32), None

    summed, _ = lax.scan(enc_step, jnp.zeros((TOKENS, LAT), jnp.float32), jnp.arange(N_SRC, dtype=jnp.int32))
    pre = summed + enc_b[None, :]
    listed = jnp.any(active[:, :, None] == jnp.arange(NBLK, dtype=jnp.int32)[None, None, :], axis=1)
    live = jnp.repeat(jnp.repeat(listed.astype(jnp.float32), TILE, axis=0), BLK, axis=1)
    codes = (live * jnp.maximum(pre, 0.0)).astype(jnp.bfloat16)
    grouped = codes.reshape(TOKENS, TGRP, N_SRC, BLK)

    def dec_step(total, group):
        piece = lax.dynamic_slice_in_dim(grouped, group, 1, 2).reshape(TOKENS, TGRP * BLK)
        weights = lax.dynamic_slice_in_dim(dec_w, group * BLK, BLK, 2).reshape(TL, TGRP * BLK, D)
        terms = jnp.stack([jnp.dot(piece, weights[layer], preferred_element_type=jnp.float32) for layer in range(TL)])
        terms = lax.optimization_barrier(terms.astype(jnp.bfloat16))
        return total + terms.astype(jnp.float32), None

    decoded, _ = lax.scan(dec_step, jnp.zeros((TL, TOKENS, D), jnp.float32), jnp.arange(N_SRC, dtype=jnp.int32))
    return (decoded + dec_b[:, None, :] - targets.astype(jnp.float32)).astype(jnp.bfloat16)
```

```python
import functools

import jax
import jax.numpy as jnp
from jax import lax
from jax.experimental import pallas as pl
from jax.experimental.pallas import tpu as pltpu
from jax.sharding import PartitionSpec as P

VMEM_BYTES = 32 * 1024 * 1024


def encode_kernel(n, acts_ref, w_ref, *out_refs):
    src = lax.axis_index("src")
    width = w_ref.shape[1] // (n // 2)
    for k in range(n):
        dest = lax.rem(src + k, n)
        rows = acts_ref[:, lax.rem(dest, 2)]
        rows = rows.reshape(rows.shape[0] * rows.shape[1], rows.shape[2])
        columns = pl.ds(pl.multiple_of((dest // 2) * width, width), width)
        out_refs[k][...] = jnp.dot(
            rows, w_ref[:, columns], preferred_element_type=jnp.float32
        ).astype(jnp.bfloat16)


def codes_kernel(n, share, tile_rows, active_ref, bias_ref, *refs):
    term_refs, out_ref = refs[:-1], refs[-1]
    src = lax.axis_index("src")
    tgt = lax.axis_index("tgt")
    parity, half = lax.rem(src, 2), src // 2
    block = out_ref.shape[2] // 2
    pre = term_refs[0][...].astype(jnp.float32)
    for ref in term_refs[1:]:
        pre = pre + ref[...].astype(jnp.float32)
    tiles, slots = active_ref.shape
    for piece in range(2):
        columns = slice(piece * block, (piece + 1) * block)
        bias = bias_ref[pl.ds(half * 2 + piece, 1), :]
        wanted = tgt * n + half * 2 + piece
        flags = []
        for tile in range(tiles):
            flags.append(
                lax.fori_loop(
                    0,
                    slots,
                    lambda i, total: total + (active_ref[tile, i] == wanted).astype(jnp.int32),
                    jnp.int32(0),
                    unroll=slots <= 16,
                )
            )
        for group in range(n // 2):
            tile = ((group * 2 + parity) * share) // tile_rows
            flag = flags[0]
            for i in range(1, tiles):
                flag = jnp.where(tile == i, flags[i], flag)
            live = jnp.where(flag > 0, 1.0, 0.0).astype(jnp.float32)
            rows = slice(group * share, (group + 1) * share)
            value = live * jnp.maximum(pre[rows, columns] + bias, 0.0)
            out_ref[group, :, columns] = value.astype(jnp.bfloat16)


def gather_rows(n, groups, lhs_ref, code_refs, group):
    src = lax.axis_index("src")
    tgt = lax.axis_index("tgt")
    rep = lax.axis_index("rep")
    parity = lax.rem(src, 2)
    block = code_refs[0].shape[2] // 2
    for place in range(2 * groups):
        if place < groups:
            wanted, piece = place, parity
        else:
            side = (place - groups) // (groups // 2)
            owner = rep if side == 0 else 1 - rep
            wanted = owner * (groups // 2) + (place - groups) % (groups // 2)
            piece = 1 - parity
        offset = lax.rem(tgt - wanted + groups, groups)
        columns = pl.ds(pl.multiple_of(piece * block, block), block)
        for k in range(groups):

            @pl.when(offset == k)
            def _():
                lhs_ref[:, place * block : (place + 1) * block] = code_refs[k][group, :, columns]


def product(groups, lhs_ref, own_ref, got_ref, swapped_ref):
    block = own_ref.shape[-2]
    own = own_ref[...].reshape(groups * block, own_ref.shape[-1])
    got = got_ref[...].reshape(groups // 2 * block, own_ref.shape[-1])
    swapped = swapped_ref[...].reshape(groups // 2 * block, own_ref.shape[-1])
    edge, last = groups * block, groups * block * 3 // 2
    total = jnp.dot(lhs_ref[:, :edge], own, preferred_element_type=jnp.float32)
    total += jnp.dot(lhs_ref[:, edge:last], got, preferred_element_type=jnp.float32)
    total += jnp.dot(lhs_ref[:, last:], swapped, preferred_element_type=jnp.float32)
    return total


def send_kernel(n, groups, step, own_ref, got_ref, swapped_ref, *refs):
    code_refs, out_ref, lhs_ref = refs[:-2], refs[-2], refs[-1]

    @pl.when(pl.program_id(0) == 0)
    def _():
        group = lax.rem(lax.axis_index("src") // 2 + step, n // 2)
        gather_rows(n, groups, lhs_ref, code_refs, group)

    out_ref[...] = product(groups, lhs_ref, own_ref, got_ref, swapped_ref).astype(jnp.bfloat16)


def keep_kernel(n, groups, own_ref, got_ref, swapped_ref, bias_ref, target_ref, *refs):
    code_refs, out_ref, lhs_ref = refs[:-2], refs[-2], refs[-1]

    @pl.when(pl.program_id(0) == 0)
    def _():
        gather_rows(n, groups, lhs_ref, code_refs, lax.axis_index("src") // 2)

    total = product(groups, lhs_ref, own_ref, got_ref, swapped_ref)
    out_ref[...] = total + bias_ref[...] - target_ref[0].astype(jnp.float32)


def add_kernel(layers, *refs):
    out_ref = refs[-1]
    per_layer = (len(refs) - 1) // layers
    for layer in range(layers):
        mine = refs[layer * per_layer : (layer + 1) * per_layer]
        total = mine[0][...]
        for ref in mine[1:]:
            total = total + ref[...].astype(jnp.float32)
        out_ref[layer] = total.astype(jnp.bfloat16)


def body(acts, enc_w, enc_b, dec_w, dec_b, targets, active):
    n = lax.axis_size("src")
    rep = lax.axis_index("rep")
    rows, features = acts.shape
    layers, groups, block, cols = dec_w.shape
    share = rows // n
    half = n // 2
    tile_rows = rows // active.shape[0]
    pair = [(i, i ^ 1) for i in range(n)]
    params = pltpu.CompilerParams(vmem_limit_bytes=VMEM_BYTES)
    vmem = pl.BlockSpec(memory_space=pltpu.VMEM)
    smem = pl.BlockSpec(memory_space=pltpu.SMEM)

    got, swapped = [], []
    for layer in range(layers):
        part = lax.dynamic_slice_in_dim(dec_w[layer], rep * (groups // 2), groups // 2, 0)
        got.append(lax.ppermute(part, "src", pair))
        swapped.append(lax.ppermute(got[-1], "rep", [(0, 1), (1, 0)]))

    term_shape = jax.ShapeDtypeStruct((half * share, 2 * block), jnp.bfloat16)
    terms = pl.pallas_call(
        functools.partial(encode_kernel, n),
        out_shape=[term_shape] * n,
        in_specs=[vmem, vmem],
        out_specs=[vmem] * n,
        compiler_params=params,
        cost_estimate=pl.CostEstimate(
            flops=2 * rows * features * groups * block * 0 + 2 * rows * features * enc_w.shape[1],
            bytes_accessed=(acts.size + enc_w.size) * 2,
            transcendentals=0,
        ),
        name="encode",
    )(acts.reshape(half, 2, share, features), enc_w)
    arrived = [terms[0]]
    for k in range(1, n):
        arrived.append(lax.ppermute(terms[k], "src", [(i, (i + k) % n) for i in range(n)]))

    codes = [
        pl.pallas_call(
            functools.partial(codes_kernel, n, share, tile_rows),
            out_shape=jax.ShapeDtypeStruct((half, share, 2 * block), jnp.bfloat16),
            in_specs=[smem, vmem] + [vmem] * n,
            out_specs=vmem,
            compiler_params=params,
            name="codes",
        )(active, enc_b.reshape(n, block), *arrived)
    ]
    for k in range(1, groups):
        codes.append(
            lax.ppermute(codes[0], "tgt", [(i, (i + k) % groups) for i in range(groups)])
        )

    width = min(cols, 512)
    lhs = pltpu.VMEM((share, 2 * groups * block), jnp.bfloat16)
    cost = pl.CostEstimate(
        flops=2 * share * 2 * groups * block * cols,
        bytes_accessed=2 * groups * block * cols * 2,
        transcendentals=0,
    )

    def weight_specs(layer):
        return [
            pl.BlockSpec((1, groups, block, width), lambda j: (layer, 0, 0, j)),
            pl.BlockSpec((groups // 2, block, width), lambda j: (0, 0, j)),
            pl.BlockSpec((groups // 2, block, width), lambda j: (0, 0, j)),
        ]

    block_spec = pl.BlockSpec((share, width), lambda j: (0, j))
    sums = []
    for layer in range(layers):
        received = []
        for step in range(1, half):
            term = pl.pallas_call(
                functools.partial(send_kernel, n, groups, step),
                grid=(cols // width,),
                out_shape=jax.ShapeDtypeStruct((share, cols), jnp.bfloat16),
                in_specs=weight_specs(layer) + [vmem] * groups,
                out_specs=block_spec,
                scratch_shapes=[lhs],
                compiler_params=params,
                cost_estimate=cost,
                name="decode_send",
            )(dec_w, got[layer], swapped[layer], *codes)
            perm = [(i, (i + 2 * step) % n) for i in range(n)]
            received.append(lax.ppermute(term, "src", perm))
        sums.append(received)

    operands = []
    for layer in range(layers):
        kept = pl.pallas_call(
            functools.partial(keep_kernel, n, groups),
            grid=(cols // width,),
            out_shape=jax.ShapeDtypeStruct((share, cols), jnp.float32),
            in_specs=weight_specs(layer)
            + [
                pl.BlockSpec((1, width), lambda j: (0, j)),
                pl.BlockSpec((1, share, width), lambda j, layer=layer: (layer, 0, j)),
            ]
            + [vmem] * groups,
            out_specs=block_spec,
            scratch_shapes=[lhs],
            compiler_params=params,
            cost_estimate=cost,
            name="decode_keep",
        )(dec_w, got[layer], swapped[layer], dec_b[layer : layer + 1], targets, *codes)
        operands += [kept] + sums[layer]

    return pl.pallas_call(
        functools.partial(add_kernel, layers),
        out_shape=jax.ShapeDtypeStruct((layers, share, cols), jnp.bfloat16),
        in_specs=[vmem] * len(operands),
        out_specs=vmem,
        compiler_params=params,
        name="add",
    )(*operands)


def solution(mesh):
    in_specs = (
        P(("parts", "rep"), "src"),
        P("src", "tgt"),
        P("tgt"),
        P(None, None, "src", "tgt"),
        P(None, "tgt"),
        P(None, ("parts", "rep", "src"), "tgt"),
        P(("parts", "rep"), None),
    )
    out_specs = P(None, ("parts", "rep", "src"), "tgt")
    return jax.shard_map(body, mesh=mesh, in_specs=in_specs, out_specs=out_specs, check_vma=False)
```

```python
import functools

import jax
import jax.numpy as jnp
from jax import lax
from jax.experimental import pallas as pl
from jax.experimental.pallas import tpu as pltpu
from jax.sharding import PartitionSpec as P

VMEM_BYTES = 32 * 1024 * 1024
ENCODE_VMEM_BYTES = 60 * 1024 * 1024


def encode_kernel(n, acts_hbm, w_hbm, dec_hbm, terms_ref, *refs):
    part_refs, (acts_ref, w_ref, part_sems, acts_sems, w_sems) = refs[:-5], refs[-5:]
    cut = part_refs[0].shape[-1]
    half = n // 2
    width = w_ref.shape[1] // half
    copies_w = []
    for i in range(half):
        columns = slice(i * width, (i + 1) * width)
        copies_w.append(
            pltpu.make_async_copy(w_hbm.at[:, columns], w_ref.at[:, columns], w_sems.at[i])
        )
    copies_acts = [
        pltpu.make_async_copy(acts_hbm.at[:, i], acts_ref.at[i], acts_sems.at[i]) for i in range(2)
    ]
    mine = pl.ds(pl.multiple_of(lax.axis_index("rep") * cut, cut), cut)
    copies_part = [
        pltpu.make_async_copy(dec_hbm.at[i, :, :, mine], ref, part_sems.at[i])
        for i, ref in enumerate(part_refs)
    ]
    copies_acts[0].start()
    copies_w[0].start()
    copies_acts[1].start()
    for copy in copies_w[1:] + copies_part:
        copy.start()
    for i in range(half):
        copies_w[i].wait()
        for parity in range(2):
            if i == 0:
                copies_acts[parity].wait()
            rows = acts_ref[parity]
            rows = rows.reshape(rows.shape[0] * rows.shape[1], rows.shape[2])
            terms_ref[i * 2 + parity] = jnp.dot(
                rows, w_ref[:, i * width : (i + 1) * width], preferred_element_type=jnp.float32
            ).astype(jnp.bfloat16)
    for copy in copies_part:
        copy.wait()


def codes_kernel(n, share, tile_rows, active_ref, bias_ref, terms_ref, out_ref):
    src = lax.axis_index("src")
    tgt = lax.axis_index("tgt")
    parity, half = lax.rem(src, 2), src // 2
    block = out_ref.shape[2] // 2
    pre = terms_ref[0].astype(jnp.float32)
    for i in range(1, n):
        pre = pre + terms_ref[i].astype(jnp.float32)
    tiles, slots = active_ref.shape
    for piece in range(2):
        columns = slice(piece * block, (piece + 1) * block)
        bias = bias_ref[pl.ds(half * 2 + piece, 1), :]
        wanted = tgt * n + half * 2 + piece
        flags = []
        for tile in range(tiles):
            flags.append(
                lax.fori_loop(
                    0,
                    slots,
                    lambda i, total: total + (active_ref[tile, i] == wanted).astype(jnp.int32),
                    jnp.int32(0),
                    unroll=slots <= 16,
                )
            )
        for group in range(n // 2):
            tile = ((group * 2 + parity) * share) // tile_rows
            flag = flags[0]
            for i in range(1, tiles):
                flag = jnp.where(tile == i, flags[i], flag)
            live = jnp.where(flag > 0, 1.0, 0.0).astype(jnp.float32)
            rows = slice(group * share, (group + 1) * share)
            value = live * jnp.maximum(pre[rows, columns] + bias, 0.0)
            out_ref[group, :, columns] = value.astype(jnp.bfloat16)


def decode_kernel(n, groups, own_ref, got_ref, *refs):
    half = n // 2
    code_refs, out_refs, lhs_ref = refs[: 2 * groups], refs[-2 * half - 1 : -1], refs[-1]
    src, tgt = lax.axis_index("src"), lax.axis_index("tgt")
    parity = lax.rem(src, 2)
    share, block = code_refs[0].shape[1], code_refs[0].shape[2] // 2
    depth = groups * block
    for k in range(groups):
        place = lax.rem(tgt - k + groups, groups)
        for side in range(2):
            piece = parity if side == 0 else 1 - parity
            piece = pl.ds(pl.multiple_of(piece * block, block), block)
            columns = pl.ds(pl.multiple_of((side * groups + place) * block, block), block)
            for j in range(half):
                group = lax.rem(src // 2 + j, half)
                for r in range(2):
                    rows = slice((2 * j + r) * share, (2 * j + r + 1) * share)
                    lhs_ref[rows, columns] = code_refs[2 * k + r][group, :, piece]
    own = own_ref[...].reshape(depth, own_ref.shape[2])
    got = got_ref[...].reshape(depth, own_ref.shape[2])
    total = jnp.dot(lhs_ref[:, :depth], own, preferred_element_type=jnp.float32)
    total += jnp.dot(lhs_ref[:, depth:], got, preferred_element_type=jnp.float32)
    for i, ref in enumerate(out_refs):
        ref[...] = total[i * share : (i + 1) * share].astype(ref.dtype)


def add_kernel(layers, bias_ref, target_ref, *refs):
    out_ref = refs[-1]
    each = (len(refs) - 1) // (2 * layers)
    cut = refs[0].shape[1]
    rep = lax.axis_index("rep")
    for layer in range(layers):
        for side in range(2):
            core = rep if side == 0 else 1 - rep
            columns = pl.ds(pl.multiple_of(core * cut, cut), cut)
            total = bias_ref[layer : layer + 1, columns]
            total = total - target_ref[layer, :, columns].astype(jnp.float32)
            first = (layer * 2 + side) * each
            for ref in refs[first : first + each]:
                total = total + ref[...].astype(jnp.float32)
            out_ref[layer, :, columns] = total.astype(jnp.bfloat16)


def body(acts, enc_w, enc_b, dec_w, dec_b, targets, active):
    n = lax.axis_size("src")
    rows, features = acts.shape
    layers, groups, block, cols = dec_w.shape
    share = rows // n
    half = n // 2
    cut = cols // 2
    tile_rows = rows // active.shape[0]
    pair = [(i, i ^ 1) for i in range(n)]
    params = pltpu.CompilerParams(vmem_limit_bytes=VMEM_BYTES)
    vmem = pl.BlockSpec(memory_space=pltpu.VMEM)
    smem = pl.BlockSpec(memory_space=pltpu.SMEM)
    anywhere = pl.BlockSpec(memory_space=pl.ANY)
    cost = pl.CostEstimate(flops=0, bytes_accessed=0, transcendentals=0)

    def shape(*extent, kind=jnp.bfloat16):
        return jax.ShapeDtypeStruct(extent, kind)

    terms, *parts = pl.pallas_call(
        functools.partial(encode_kernel, n),
        out_shape=[shape(n, half * share, 2 * block)] + [shape(groups, block, cut)] * layers,
        in_specs=[anywhere] * 3,
        out_specs=[vmem] * (1 + layers),
        scratch_shapes=[
            pltpu.VMEM((2, half, share, features), jnp.bfloat16),
            pltpu.VMEM(enc_w.shape, jnp.bfloat16),
            pltpu.SemaphoreType.DMA((layers,)),
            pltpu.SemaphoreType.DMA((2,)),
            pltpu.SemaphoreType.DMA((half,)),
        ],
        compiler_params=pltpu.CompilerParams(vmem_limit_bytes=ENCODE_VMEM_BYTES),
        cost_estimate=cost,
        name="encode",
    )(acts.reshape(half, 2, share, features), enc_w, dec_w)
    got = [lax.ppermute(part, "src", pair) for part in parts]
    terms = lax.all_to_all(terms, "src", 0, 0, tiled=True)

    own = pl.pallas_call(
        functools.partial(codes_kernel, n, share, tile_rows),
        out_shape=shape(half, share, 2 * block),
        in_specs=[smem, vmem, vmem],
        out_specs=vmem,
        compiler_params=params,
        cost_estimate=cost,
        name="codes",
    )(active, enc_b.reshape(n, block), terms)
    codes = []
    for k in range(groups):
        for r in range(2):
            perm = [
                (i * 2 + c, (i + k) % groups * 2 + (c ^ r)) for i in range(groups) for c in range(2)
            ]
            codes.append(lax.ppermute(own, ("tgt", "rep"), perm) if k + r else own)

    sums, after = [], []
    for layer in range(layers):
        kinds = [jnp.float32] + [jnp.bfloat16] * (2 * half - 1)
        terms = pl.pallas_call(
            functools.partial(decode_kernel, n, groups),
            out_shape=[shape(share, cut, kind=kind) for kind in kinds],
            in_specs=[vmem] * (2 + 2 * groups) + [anywhere] * len(after),
            out_specs=[vmem] * (2 * half),
            scratch_shapes=[pltpu.VMEM((rows, 2 * groups * block), jnp.bfloat16)],
            compiler_params=params,
            cost_estimate=cost,
            name="decode",
        )(parts[layer], got[layer], *codes, *after)
        after = [terms[0]]
        for r in range(2):
            for j in range(half):
                perm = [
                    (i * 2 + c, (i + 2 * j) % n * 2 + (c ^ r)) for i in range(n) for c in range(2)
                ]
                term = terms[2 * j + r]
                sums.append(lax.ppermute(term, ("src", "rep"), perm) if j + r else term)

    return pl.pallas_call(
        functools.partial(add_kernel, layers),
        out_shape=shape(layers, share, cols),
        in_specs=[vmem] * (2 + len(sums)),
        out_specs=vmem,
        compiler_params=params,
        cost_estimate=cost,
        name="add",
    )(dec_b, targets, *sums)


def solution(mesh):
    in_specs = (
        P(("parts", "rep"), "src"),
        P("src", "tgt"),
        P("tgt"),
        P(None, None, "src", "tgt"),
        P(None, "tgt"),
        P(None, ("parts", "rep", "src"), "tgt"),
        P(("parts", "rep"), None),
    )
    out_specs = P(None, ("parts", "rep", "src"), "tgt")
    return jax.shard_map(body, mesh=mesh, in_specs=in_specs, out_specs=out_specs, check_vma=False)
```

```python
import functools

import jax
import jax.numpy as jnp
from jax import lax
from jax.experimental import pallas as pl
from jax.experimental.pallas import tpu as pltpu
from jax.sharding import PartitionSpec as P

VMEM_BYTES = 32 * 1024 * 1024
ENCODE_VMEM_BYTES = 60 * 1024 * 1024
LANES = 128
SHARES = (4, 4)


def cut_columns(columns):
    tiles = columns // LANES
    pieces, start = [], 0
    for i, eighths in enumerate(SHARES):
        stop = min(tiles, start + -(-tiles * eighths // 8))
        stop = tiles if i == len(SHARES) - 1 else stop
        if stop > start:
            pieces.append((start * LANES, (stop - start) * LANES))
        start = stop
    return pieces


def part_copies(piece, dec_hbm, part_ref, sems):
    layers, groups, _, cols = dec_hbm.shape
    start = pl.multiple_of(lax.axis_index("rep") * (cols // 2) + piece[0], LANES)
    copies = []
    for layer in range(layers):
        for group in range(groups):
            source = dec_hbm.at[layer, group, :, pl.ds(start, piece[1])]
            copies.append(
                pltpu.make_async_copy(
                    source, part_ref.at[layer, group], sems.at[layer * groups + group]
                )
            )
            copies[-1].start()
    return copies


def encode_kernel(
    n, piece, acts_hbm, w_hbm, dec_hbm, terms_ref, part_ref, acts_ref, w_ref, part_sems, acts_sems, w_sems
):
    half = n // 2
    width = w_ref.shape[1] // half
    depth = w_ref.shape[0] // 4
    copies_w, copies_acts = [], []
    for i in range(half):
        columns = slice(i * width, (i + 1) * width)
        for j in range(4):
            rows = slice(j * depth, (j + 1) * depth)
            copies_w.append(
                pltpu.make_async_copy(
                    w_hbm.at[rows, columns], w_ref.at[rows, columns], w_sems.at[i * 4 + j]
                )
            )
    for i in range(2):
        for j in range(half):
            copies_acts.append(
                pltpu.make_async_copy(
                    acts_hbm.at[j, i], acts_ref.at[i, j], acts_sems.at[i * half + j]
                )
            )
    for copy in copies_w[:4] + copies_acts + copies_w[4:]:
        copy.start()
    copies_part = part_copies(piece, dec_hbm, part_ref, part_sems)
    for i in range(half):
        for copy in copies_w[i * 4 : i * 4 + 4]:
            copy.wait()
        for parity in range(2):
            if i == 0:
                for copy in copies_acts[parity * half : (parity + 1) * half]:
                    copy.wait()
            rows = acts_ref[parity]
            rows = rows.reshape(rows.shape[0] * rows.shape[1], rows.shape[2])
            terms_ref[i * 2 + parity] = jnp.dot(
                rows, w_ref[:, i * width : (i + 1) * width], preferred_element_type=jnp.float32
            ).astype(jnp.bfloat16)
    for copy in copies_part:
        copy.wait()


def codes_kernel(n, share, tile_rows, piece, active_ref, bias_ref, terms_ref, *refs):
    copies_part = []
    if piece is None:
        (out_ref,) = refs
    else:
        dec_hbm, out_ref, part_ref, part_sems = refs
        copies_part = part_copies(piece, dec_hbm, part_ref, part_sems)
    src = lax.axis_index("src")
    tgt = lax.axis_index("tgt")
    parity, half = lax.rem(src, 2), src // 2
    block = out_ref.shape[2] // 2
    pre = terms_ref[0].astype(jnp.float32)
    for i in range(1, n):
        pre = pre + terms_ref[i].astype(jnp.float32)
    tiles, slots = active_ref.shape
    for piece in range(2):
        columns = slice(piece * block, (piece + 1) * block)
        bias = bias_ref[pl.ds(half * 2 + piece, 1), :]
        wanted = tgt * n + half * 2 + piece
        flags = []
        for tile in range(tiles):
            flags.append(
                lax.fori_loop(
                    0,
                    slots,
                    lambda i, total: total + (active_ref[tile, i] == wanted).astype(jnp.int32),
                    jnp.int32(0),
                    unroll=slots <= 16,
                )
            )
        for group in range(n // 2):
            tile = ((group * 2 + parity) * share) // tile_rows
            flag = flags[0]
            for i in range(1, tiles):
                flag = jnp.where(tile == i, flags[i], flag)
            live = jnp.where(flag > 0, 1.0, 0.0).astype(jnp.float32)
            rows = slice(group * share, (group + 1) * share)
            value = live * jnp.maximum(pre[rows, columns] + bias, 0.0)
            out_ref[group, :, columns] = value.astype(jnp.bfloat16)
    for copy in copies_part:
        copy.wait()


def decode_kernel(n, piece, later, dec_hbm, got_hbm, *refs):
    half = n // 2
    layers, groups, block, _ = dec_hbm.shape
    code_refs, refs = refs[: 2 * groups], refs[2 * groups :]
    out_refs, refs = refs[-5 - 2 * half - (later is not None) :][: 2 * half], refs[-5 - (later is not None) :]
    own_ref, got_ref, lhs_ref, sems, part_sems = refs[-5:]
    copies = part_copies(piece, dec_hbm, own_ref, sems)
    for layer in range(layers):
        for group in range(groups):
            copies.append(
                pltpu.make_async_copy(
                    got_hbm.at[layer, group],
                    got_ref.at[layer, group],
                    sems.at[(layers + layer) * groups + group],
                )
            )
            copies[-1].start()
    copies_part = []
    if later is not None:
        copies_part = part_copies(later, dec_hbm, refs[0], part_sems)
    src, tgt = lax.axis_index("src"), lax.axis_index("tgt")
    parity = lax.rem(src, 2)
    share = code_refs[0].shape[1]
    depth, width = groups * block, piece[1]
    for k in range(groups):
        place = lax.rem(tgt - k + groups, groups)
        for side in range(2):
            latents = parity if side == 0 else 1 - parity
            latents = pl.ds(pl.multiple_of(latents * block, block), block)
            columns = pl.ds(pl.multiple_of((side * groups + place) * block, block), block)
            for j in range(half):
                group = lax.rem(src // 2 + j, half)
                for r in range(2):
                    rows = slice((2 * j + r) * share, (2 * j + r + 1) * share)
                    lhs_ref[rows, columns] = code_refs[2 * k + r][group, :, latents]
    for copy in copies:
        copy.wait()
    for layer in range(layers):
        own = own_ref[layer].reshape(depth, width)
        got = got_ref[layer].reshape(depth, width)
        total = jnp.dot(lhs_ref[:, :depth], own, preferred_element_type=jnp.float32)
        total += jnp.dot(lhs_ref[:, depth:], got, preferred_element_type=jnp.float32)
        for i, ref in enumerate(out_refs):
            ref[layer] = total[i * share : (i + 1) * share].astype(ref.dtype)
    for copy in copies_part:
        copy.wait()


def add_kernel(n, pieces, bias_ref, target_ref, *refs):
    out_hbm, out_ref, sems = refs[-3:]
    half = n // 2
    layers, _, cols = target_ref.shape
    rep = lax.axis_index("rep")
    copies = []
    for i, (first, width) in enumerate(pieces):
        for side in range(2):
            core = rep if side == 0 else 1 - rep
            columns = pl.ds(pl.multiple_of(core * (cols // 2) + first, LANES), width)
            mine = refs[(2 * i + side) * half : (2 * i + side + 1) * half]
            for layer in range(layers):
                total = bias_ref[layer : layer + 1, columns]
                total = total - target_ref[layer, :, columns].astype(jnp.float32)
                for ref in mine:
                    total = total + ref[layer].astype(jnp.float32)
                out_ref[layer, :, columns] = total.astype(jnp.bfloat16)
                copies.append(
                    pltpu.make_async_copy(
                        out_ref.at[layer, :, columns],
                        out_hbm.at[layer, :, columns],
                        sems.at[(2 * i + side) * layers + layer],
                    )
                )
                copies[-1].start()
    for copy in copies:
        copy.wait()


def body(acts, enc_w, enc_b, dec_w, dec_b, targets, active):
    n = lax.axis_size("src")
    rows, features = acts.shape
    layers, groups, block, cols = dec_w.shape
    share = rows // n
    half = n // 2
    pieces = cut_columns(cols // 2)
    tile_rows = rows // active.shape[0]
    pair = [(i, i ^ 1) for i in range(n)]
    params = pltpu.CompilerParams(vmem_limit_bytes=VMEM_BYTES)
    vmem = pl.BlockSpec(memory_space=pltpu.VMEM)
    smem = pl.BlockSpec(memory_space=pltpu.SMEM)
    anywhere = pl.BlockSpec(memory_space=pl.ANY)
    cost = pl.CostEstimate(flops=0, bytes_accessed=0, transcendentals=0)
    part_sems = pltpu.SemaphoreType.DMA((layers * groups,))

    def shape(*extent, kind=jnp.bfloat16):
        return jax.ShapeDtypeStruct(extent, kind)

    def part_shapes(i):
        return [shape(layers, groups, block, pieces[i][1])] if i < len(pieces) else []

    terms, part = pl.pallas_call(
        functools.partial(encode_kernel, n, pieces[0]),
        out_shape=[shape(n, half * share, 2 * block)] + part_shapes(0),
        in_specs=[anywhere] * 3,
        out_specs=[vmem] * 2,
        scratch_shapes=[
            pltpu.VMEM((2, half, share, features), jnp.bfloat16),
            pltpu.VMEM(enc_w.shape, jnp.bfloat16),
            part_sems,
            pltpu.SemaphoreType.DMA((2 * half,)),
            pltpu.SemaphoreType.DMA((4 * half,)),
        ],
        compiler_params=pltpu.CompilerParams(vmem_limit_bytes=ENCODE_VMEM_BYTES),
        cost_estimate=cost,
        name="encode",
    )(acts.reshape(half, 2, share, features), enc_w, dec_w)
    got = [lax.ppermute(part, "src", pair)]
    terms = lax.all_to_all(terms, "src", 0, 0, tiled=True)

    more = len(pieces) > 1
    own, *part = pl.pallas_call(
        functools.partial(codes_kernel, n, share, tile_rows, pieces[1] if more else None),
        out_shape=[shape(half, share, 2 * block)] + part_shapes(1),
        in_specs=[smem, vmem, vmem] + [anywhere] * more,
        out_specs=[vmem] * (1 + more),
        scratch_shapes=[part_sems] * more,
        compiler_params=params,
        cost_estimate=cost,
        name="codes",
    )(active, enc_b.reshape(n, block), terms, *[dec_w] * more)
    got += [lax.ppermute(value, "src", pair) for value in part]
    codes = []
    for k in range(groups):
        for r in range(2):
            perm = [
                (i * 2 + c, (i + k) % groups * 2 + (c ^ r)) for i in range(groups) for c in range(2)
            ]
            codes.append(lax.ppermute(own, ("tgt", "rep"), perm) if k + r else own)

    sums, after = [], []
    for i, piece in enumerate(pieces):
        later = pieces[i + 2] if i + 2 < len(pieces) else None
        width = piece[1]
        shapes = [shape(layers, share, width)] * (2 * half)
        shapes[0] = shape(layers, share, width, kind=jnp.float32)
        shapes += part_shapes(i + 2)
        terms = pl.pallas_call(
            functools.partial(decode_kernel, n, piece, later),
            out_shape=shapes,
            in_specs=[anywhere] * 2 + [vmem] * (2 * groups) + [anywhere] * len(after),
            out_specs=[vmem] * len(shapes),
            scratch_shapes=[
                pltpu.VMEM((layers, groups, block, width), jnp.bfloat16),
                pltpu.VMEM((layers, groups, block, width), jnp.bfloat16),
                pltpu.VMEM((rows, 2 * groups * block), jnp.bfloat16),
                pltpu.SemaphoreType.DMA((2 * layers * groups,)),
                part_sems,
            ],
            compiler_params=params,
            cost_estimate=cost,
            name="decode",
        )(dec_w, got[i], *codes, *after)
        after = [terms[0]]
        got += [lax.ppermute(value, "src", pair) for value in terms[2 * half :]]
        for r in range(2):
            for j in range(half):
                perm = [
                    (d * 2 + c, (d + 2 * j) % n * 2 + (c ^ r)) for d in range(n) for c in range(2)
                ]
                term = terms[2 * j + r]
                sums.append(lax.ppermute(term, ("src", "rep"), perm) if j + r else term)

    return pl.pallas_call(
        functools.partial(add_kernel, n, pieces),
        out_shape=shape(layers, share, cols),
        in_specs=[vmem] * (2 + len(sums)),
        out_specs=anywhere,
        scratch_shapes=[
            pltpu.VMEM((layers, share, cols), jnp.bfloat16),
            pltpu.SemaphoreType.DMA((2 * len(pieces) * layers,)),
        ],
        compiler_params=params,
        cost_estimate=cost,
        name="add",
    )(dec_b, targets, *sums)


def solution(mesh):
    in_specs = (
        P(("parts", "rep"), "src"),
        P("src", "tgt"),
        P("tgt"),
        P(None, None, "src", "tgt"),
        P(None, "tgt"),
        P(None, ("parts", "rep", "src"), "tgt"),
        P(("parts", "rep"), None),
    )
    out_specs = P(None, ("parts", "rep", "src"), "tgt")
    return jax.shard_map(body, mesh=mesh, in_specs=in_specs, out_specs=out_specs, check_vma=False)
```

```python
import functools

import jax
import jax.numpy as jnp
from jax import lax
from jax.experimental import pallas as pl
from jax.experimental.pallas import tpu as pltpu
from jax.sharding import PartitionSpec as P

VMEM_BYTES = 32 * 1024 * 1024
LANES = 128
SHARES = (4, 4)


def cut_columns(columns):
    tiles = columns // LANES
    pieces, start = [], 0
    for i, eighths in enumerate(SHARES):
        stop = min(tiles, start + -(-tiles * eighths // 8))
        stop = tiles if i == len(SHARES) - 1 else stop
        if stop > start:
            pieces.append((start * LANES, (stop - start) * LANES))
        start = stop
    return pieces


def part_copies(piece, dec_hbm, part_ref, sems):
    layers, groups, _, cols = dec_hbm.shape
    start = pl.multiple_of(lax.axis_index("rep") * (cols // 2) + piece[0], LANES)
    copies = []
    for layer in range(layers):
        for group in range(groups):
            source = dec_hbm.at[layer, group, :, pl.ds(start, piece[1])]
            copies.append(
                pltpu.make_async_copy(
                    source, part_ref.at[layer, group], sems.at[layer * groups + group]
                )
            )
            copies[-1].start()
    return copies


def encode_kernel(n, pieces, acts_hbm, w_hbm, dec_hbm, *refs):
    term_refs, part_refs, refs = refs[:n], refs[n : n + len(pieces)], refs[n + len(pieces) :]
    acts_ref, w_ref, part_sems, acts_sems, w_sems = refs
    half = n // 2
    width = w_ref.shape[1] // half
    depth = w_ref.shape[0] // 8
    copies = []
    for i in range(2):
        for j in range(half):
            copies.append(
                pltpu.make_async_copy(
                    acts_hbm.at[j, i], acts_ref.at[i, j], acts_sems.at[i * half + j]
                )
            )
    for i in range(8):
        rows = slice(i * depth, (i + 1) * depth)
        copies.append(pltpu.make_async_copy(w_hbm.at[rows], w_ref.at[rows], w_sems.at[i]))
    for copy in copies:
        copy.start()
    for copy in copies:
        copy.wait()
    copies_part = []
    for i, piece in enumerate(pieces):
        copies_part += part_copies(piece, dec_hbm, part_refs[i], part_sems.at[i])
    src = lax.axis_index("src")
    for k in range(n):
        dest = lax.rem(src + k, n)
        rows = acts_ref[lax.rem(dest, 2)]
        rows = rows.reshape(rows.shape[0] * rows.shape[1], rows.shape[2])
        columns = pl.ds(pl.multiple_of((dest // 2) * width, width), width)
        term_refs[k][...] = jnp.dot(
            rows, w_ref[:, columns], preferred_element_type=jnp.float32
        ).astype(jnp.bfloat16)
    for copy in copies_part:
        copy.wait()


def codes_kernel(n, share, tile_rows, active_ref, bias_ref, *refs):
    term_refs, out_ref = refs[:n], refs[n + (len(refs) - n - 1) // 2]
    src = lax.axis_index("src")
    tgt = lax.axis_index("tgt")
    parity, half = lax.rem(src, 2), src // 2
    block = out_ref.shape[2] // 2
    pre = term_refs[0][...].astype(jnp.float32)
    for ref in term_refs[1:]:
        pre = pre + ref[...].astype(jnp.float32)
    tiles, slots = active_ref.shape
    for piece in range(2):
        columns = slice(piece * block, (piece + 1) * block)
        bias = bias_ref[pl.ds(half * 2 + piece, 1), :]
        wanted = tgt * n + half * 2 + piece
        flags = []
        for tile in range(tiles):
            flags.append(
                lax.fori_loop(
                    0,
                    slots,
                    lambda i, total: total + (active_ref[tile, i] == wanted).astype(jnp.int32),
                    jnp.int32(0),
                    unroll=slots <= 16,
                )
            )
        for group in range(n // 2):
            tile = ((group * 2 + parity) * share) // tile_rows
            flag = flags[0]
            for i in range(1, tiles):
                flag = jnp.where(tile == i, flags[i], flag)
            live = jnp.where(flag > 0, 1.0, 0.0).astype(jnp.float32)
            rows = slice(group * share, (group + 1) * share)
            value = live * jnp.maximum(pre[rows, columns] + bias, 0.0)
            out_ref[group, :, columns] = value.astype(jnp.bfloat16)


def decode_kernel(n, own_ref, got_ref, *refs):
    half = n // 2
    layers, groups, block, width = own_ref.shape
    code_refs, out_refs, lhs_ref = refs[: 2 * groups], refs[-2 * half - 1 : -1], refs[-1]
    src, tgt = lax.axis_index("src"), lax.axis_index("tgt")
    parity = lax.rem(src, 2)
    share = code_refs[0].shape[1]
    depth = groups * block
    for k in range(groups):
        place = lax.rem(tgt - k + groups, groups)
        for side in range(2):
            latents = parity if side == 0 else 1 - parity
            latents = pl.ds(pl.multiple_of(latents * block, block), block)
            columns = pl.ds(pl.multiple_of((side * groups + place) * block, block), block)
            for j in range(half):
                group = lax.rem(src // 2 + j, half)
                for r in range(2):
                    rows = slice((2 * j + r) * share, (2 * j + r + 1) * share)
                    lhs_ref[rows, columns] = code_refs[2 * k + r][group, :, latents]
    for layer in range(layers):
        own = own_ref[layer].reshape(depth, width)
        got = got_ref[layer].reshape(depth, width)
        total = jnp.dot(lhs_ref[:, :depth], own, preferred_element_type=jnp.float32)
        total += jnp.dot(lhs_ref[:, depth:], got, preferred_element_type=jnp.float32)
        for i, ref in enumerate(out_refs):
            ref[layer] = total[i * share : (i + 1) * share].astype(ref.dtype)


def add_kernel(n, pieces, bias_ref, target_ref, *refs):
    out_hbm, out_ref, sems = refs[-3:]
    half = n // 2
    layers, _, cols = target_ref.shape
    rep = lax.axis_index("rep")
    copies = []
    for i, (first, width) in enumerate(pieces):
        for side in range(2):
            core = rep if side == 0 else 1 - rep
            columns = pl.ds(pl.multiple_of(core * (cols // 2) + first, LANES), width)
            mine = refs[(2 * i + side) * half : (2 * i + side + 1) * half]
            for layer in range(layers):
                total = bias_ref[layer : layer + 1, columns]
                total = total - target_ref[layer, :, columns].astype(jnp.float32)
                for ref in mine:
                    total = total + ref[layer].astype(jnp.float32)
                out_ref[layer, :, columns] = total.astype(jnp.bfloat16)
                copies.append(
                    pltpu.make_async_copy(
                        out_ref.at[layer, :, columns],
                        out_hbm.at[layer, :, columns],
                        sems.at[(2 * i + side) * layers + layer],
                    )
                )
                copies[-1].start()
    for copy in copies:
        copy.wait()


def body(acts, enc_w, enc_b, dec_w, dec_b, targets, active):
    n = lax.axis_size("src")
    rows, features = acts.shape
    layers, groups, block, cols = dec_w.shape
    share = rows // n
    half = n // 2
    pieces = cut_columns(cols // 2)
    tile_rows = rows // active.shape[0]
    pair = [(i, i ^ 1) for i in range(n)]
    params = pltpu.CompilerParams(vmem_limit_bytes=VMEM_BYTES)
    vmem = pl.BlockSpec(memory_space=pltpu.VMEM)
    smem = pl.BlockSpec(memory_space=pltpu.SMEM)
    anywhere = pl.BlockSpec(memory_space=pl.ANY)
    cost = pl.CostEstimate(flops=0, bytes_accessed=0, transcendentals=0)

    acts, enc_w, dec_w = (
        pltpu.with_memory_space_constraint(value, pltpu.HBM)
        for value in (acts.reshape(half, 2, share, features), enc_w, dec_w)
    )

    def shape(*extent, kind=jnp.bfloat16):
        return jax.ShapeDtypeStruct(extent, kind)

    results = pl.pallas_call(
        functools.partial(encode_kernel, n, pieces),
        out_shape=[shape(half * share, 2 * block)] * n
        + [shape(layers, groups, block, width) for _, width in pieces],
        in_specs=[anywhere] * 3,
        out_specs=[vmem] * (n + len(pieces)),
        scratch_shapes=[
            pltpu.VMEM((2, half, share, features), jnp.bfloat16),
            pltpu.VMEM(enc_w.shape, jnp.bfloat16),
            pltpu.SemaphoreType.DMA((len(pieces), layers * groups)),
            pltpu.SemaphoreType.DMA((2 * half,)),
            pltpu.SemaphoreType.DMA((8,)),
        ],
        compiler_params=params,
        cost_estimate=cost,
        name="encode",
    )(acts, enc_w, dec_w)
    terms, parts = list(results[:n]), results[n:]
    for k in range(1, n):
        terms[k] = lax.ppermute(terms[k], "src", [(i, (i + k) % n) for i in range(n)])
    own, *late = pl.pallas_call(
        functools.partial(codes_kernel, n, share, tile_rows),
        out_shape=[shape(half, share, 2 * block)]
        + [jax.ShapeDtypeStruct(part.shape, part.dtype) for part in parts[1:]],
        in_specs=[smem] + [vmem] * (1 + n) + [anywhere] * (len(parts) - 1),
        out_specs=[vmem] + [anywhere] * (len(parts) - 1),
        input_output_aliases={2 + n + i: 1 + i for i in range(len(parts) - 1)},
        compiler_params=params,
        cost_estimate=cost,
        name="codes",
    )(active, enc_b.reshape(n, block), *terms, *parts[1:])
    parts = [parts[0], *late]
    got = [lax.ppermute(part, "src", pair) for part in parts]
    codes = []
    for k in range(groups):
        for r in range(2):
            perm = [
                (i * 2 + c, (i + k) % groups * 2 + (c ^ r)) for i in range(groups) for c in range(2)
            ]
            codes.append(lax.ppermute(own, ("tgt", "rep"), perm) if k + r else own)

    sums, after = [], []
    for i, piece in enumerate(pieces):
        shapes = [shape(layers, share, piece[1])] * (2 * half)
        shapes[0] = shape(layers, share, piece[1], kind=jnp.float32)
        terms = pl.pallas_call(
            functools.partial(decode_kernel, n),
            out_shape=shapes,
            in_specs=[vmem] * (2 + 2 * groups) + [anywhere] * len(after),
            out_specs=[vmem] * len(shapes),
            scratch_shapes=[pltpu.VMEM((rows, 2 * groups * block), jnp.bfloat16)],
            compiler_params=params,
            cost_estimate=cost,
            name="decode",
        )(parts[i], got[i], *codes, *after)
        after = [terms[0]]
        for r in range(2):
            for j in range(half):
                perm = [
                    (d * 2 + c, (d + 2 * j) % n * 2 + (c ^ r)) for d in range(n) for c in range(2)
                ]
                term = terms[2 * j + r]
                sums.append(lax.ppermute(term, ("src", "rep"), perm) if j + r else term)

    return pl.pallas_call(
        functools.partial(add_kernel, n, pieces),
        out_shape=shape(layers, share, cols),
        in_specs=[vmem] * (2 + len(sums)),
        out_specs=anywhere,
        scratch_shapes=[
            pltpu.VMEM((layers, share, cols), jnp.bfloat16),
            pltpu.SemaphoreType.DMA((2 * len(pieces) * layers,)),
        ],
        compiler_params=params,
        cost_estimate=cost,
        name="add",
    )(dec_b, targets, *sums)


def solution(mesh):
    in_specs = (
        P(("parts", "rep"), "src"),
        P("src", "tgt"),
        P("tgt"),
        P(None, None, "src", "tgt"),
        P(None, "tgt"),
        P(None, ("parts", "rep", "src"), "tgt"),
        P(("parts", "rep"), None),
    )
    out_specs = P(None, ("parts", "rep", "src"), "tgt")
    return jax.shard_map(body, mesh=mesh, in_specs=in_specs, out_specs=out_specs, check_vma=False)
```

```python
import functools

import jax
import jax.numpy as jnp
from jax import lax
from jax.experimental import pallas as pl
from jax.experimental.pallas import tpu as pltpu
from jax.sharding import PartitionSpec as P

VMEM_BYTES = 32 * 1024 * 1024
LANES = 128
SHARES = (5, 3)


def cut_columns(columns):
    tiles = columns // LANES
    pieces, start = [], 0
    for i, eighths in enumerate(SHARES):
        stop = min(tiles, start + -(-tiles * eighths // 8))
        stop = tiles if i == len(SHARES) - 1 else stop
        if stop > start:
            pieces.append((start * LANES, (stop - start) * LANES))
        start = stop
    return pieces


def part_copies(piece, layer, dec_hbm, part_ref, sems):
    groups, cols = dec_hbm.shape[1], dec_hbm.shape[3]
    start = pl.multiple_of(lax.axis_index("rep") * (cols // 2) + piece[0], LANES)
    copies = []
    for group in range(groups):
        source = dec_hbm.at[layer, group, :, pl.ds(start, piece[1])]
        copies.append(pltpu.make_async_copy(source, part_ref.at[group], sems.at[group]))
        copies[-1].start()
    return copies


def encode_kernel(n, pieces, acts_hbm, w_hbm, dec_hbm, *refs):
    layers = dec_hbm.shape[0]
    term_refs, part_refs, refs = refs[:n], refs[n:-5], refs[-5:]
    acts_ref, w_ref, part_sems, acts_sems, w_sems = refs
    half = n // 2
    width = w_ref.shape[1] // half
    depth = w_ref.shape[0] // 8
    copies = []
    for i in range(2):
        for j in range(half):
            copies.append(
                pltpu.make_async_copy(
                    acts_hbm.at[j, i], acts_ref.at[i, j], acts_sems.at[i * half + j]
                )
            )
    for i in range(8):
        rows = slice(i * depth, (i + 1) * depth)
        copies.append(pltpu.make_async_copy(w_hbm.at[rows], w_ref.at[rows], w_sems.at[i]))
    for copy in copies:
        copy.start()
    for copy in copies:
        copy.wait()
    copies_part = []
    for i, piece in enumerate(pieces):
        for layer in range(layers):
            ref = part_refs[layer] if i == 0 else part_refs[layers + i - 1].at[layer]
            copies_part += part_copies(piece, layer, dec_hbm, ref, part_sems.at[i, layer])
    src = lax.axis_index("src")
    for k in range(n):
        dest = lax.rem(src + k, n)
        rows = acts_ref[lax.rem(dest, 2)]
        rows = rows.reshape(rows.shape[0] * rows.shape[1], rows.shape[2])
        columns = pl.ds(pl.multiple_of((dest // 2) * width, width), width)
        term_refs[k][...] = jnp.dot(
            rows, w_ref[:, columns], preferred_element_type=jnp.float32
        ).astype(jnp.bfloat16)
    for copy in copies_part:
        copy.wait()


def codes_kernel(n, share, tile_rows, active_ref, bias_ref, *refs):
    term_refs, out_ref = refs[:n], refs[n]
    src = lax.axis_index("src")
    tgt = lax.axis_index("tgt")
    parity, half = lax.rem(src, 2), src // 2
    block = out_ref.shape[2] // 2
    pre = term_refs[0][...].astype(jnp.float32)
    for ref in term_refs[1:]:
        pre = pre + ref[...].astype(jnp.float32)
    tiles, slots = active_ref.shape
    for piece in range(2):
        columns = slice(piece * block, (piece + 1) * block)
        bias = bias_ref[pl.ds(half * 2 + piece, 1), :]
        wanted = tgt * n + half * 2 + piece
        flags = []
        for tile in range(tiles):
            flags.append(
                lax.fori_loop(
                    0,
                    slots,
                    lambda i, total: total + (active_ref[tile, i] == wanted).astype(jnp.int32),
                    jnp.int32(0),
                    unroll=slots <= 16,
                )
            )
        for group in range(n // 2):
            tile = ((group * 2 + parity) * share) // tile_rows
            flag = flags[0]
            for i in range(1, tiles):
                flag = jnp.where(tile == i, flags[i], flag)
            live = jnp.where(flag > 0, 1.0, 0.0).astype(jnp.float32)
            rows = slice(group * share, (group + 1) * share)
            value = live * jnp.maximum(pre[rows, columns] + bias, 0.0)
            out_ref[group, :, columns] = value.astype(jnp.bfloat16)


def decode_kernel(n, layers, *refs):
    half = n // 2
    count = 1 if len(refs[0].shape) == 4 else layers
    own_refs, got_refs, refs = refs[:count], refs[count : 2 * count], refs[2 * count :]
    groups, block, width = own_refs[0].shape[-3:]
    code_refs, out_refs, lhs_ref = refs[: 2 * groups], refs[-2 * half - 1 : -1], refs[-1]
    src, tgt = lax.axis_index("src"), lax.axis_index("tgt")
    parity = lax.rem(src, 2)
    share = code_refs[0].shape[1]
    depth = groups * block
    for k in range(groups):
        place = lax.rem(tgt - k + groups, groups)
        for side in range(2):
            latents = parity if side == 0 else 1 - parity
            latents = pl.ds(pl.multiple_of(latents * block, block), block)
            columns = pl.ds(pl.multiple_of((side * groups + place) * block, block), block)
            for j in range(half):
                group = lax.rem(src // 2 + j, half)
                for r in range(2):
                    rows = slice((2 * j + r) * share, (2 * j + r + 1) * share)
                    lhs_ref[rows, columns] = code_refs[2 * k + r][group, :, latents]
    for layer in range(layers):
        own = (own_refs[layer][...] if count > 1 else own_refs[0][layer]).reshape(depth, width)
        got = (got_refs[layer][...] if count > 1 else got_refs[0][layer]).reshape(depth, width)
        total = jnp.dot(lhs_ref[:, :depth], own, preferred_element_type=jnp.float32)
        total += jnp.dot(lhs_ref[:, depth:], got, preferred_element_type=jnp.float32)
        for i, ref in enumerate(out_refs):
            ref[layer] = total[i * share : (i + 1) * share].astype(ref.dtype)


def add_kernel(n, pieces, bias_ref, target_ref, *refs):
    out_hbm, out_ref, sems = refs[-3:]
    half = n // 2
    layers, _, cols = target_ref.shape
    rep = lax.axis_index("rep")
    copies = []
    for i, (first, width) in enumerate(pieces):
        for side in range(2):
            core = rep if side == 0 else 1 - rep
            columns = pl.ds(pl.multiple_of(core * (cols // 2) + first, LANES), width)
            mine = refs[(2 * i + side) * half : (2 * i + side + 1) * half]
            for layer in range(layers):
                total = bias_ref[layer : layer + 1, columns]
                total = total - target_ref[layer, :, columns].astype(jnp.float32)
                for ref in mine:
                    total = total + ref[layer].astype(jnp.float32)
                out_ref[layer, :, columns] = total.astype(jnp.bfloat16)
                copies.append(
                    pltpu.make_async_copy(
                        out_ref.at[layer, :, columns],
                        out_hbm.at[layer, :, columns],
                        sems.at[(2 * i + side) * layers + layer],
                    )
                )
                copies[-1].start()
    for copy in copies:
        copy.wait()


def body(acts, enc_w, enc_b, dec_w, dec_b, targets, active):
    n = lax.axis_size("src")
    rows, features = acts.shape
    layers, groups, block, cols = dec_w.shape
    share = rows // n
    half = n // 2
    pieces = cut_columns(cols // 2)
    tile_rows = rows // active.shape[0]
    pair = [(i, i ^ 1) for i in range(n)]
    params = pltpu.CompilerParams(vmem_limit_bytes=VMEM_BYTES)
    vmem = pl.BlockSpec(memory_space=pltpu.VMEM)
    smem = pl.BlockSpec(memory_space=pltpu.SMEM)
    anywhere = pl.BlockSpec(memory_space=pl.ANY)
    cost = pl.CostEstimate(flops=0, bytes_accessed=0, transcendentals=0)

    acts, enc_w, dec_w = (
        pltpu.with_memory_space_constraint(value, pltpu.HBM)
        for value in (acts.reshape(half, 2, share, features), enc_w, dec_w)
    )

    def shape(*extent, kind=jnp.bfloat16):
        return jax.ShapeDtypeStruct(extent, kind)

    results = pl.pallas_call(
        functools.partial(encode_kernel, n, pieces),
        out_shape=[shape(half * share, 2 * block)] * n
        + [shape(groups, block, pieces[0][1])] * layers
        + [shape(layers, groups, block, width) for _, width in pieces[1:]],
        in_specs=[anywhere] * 3,
        out_specs=[vmem] * (n + layers + len(pieces) - 1),
        scratch_shapes=[
            pltpu.VMEM((2, half, share, features), jnp.bfloat16),
            pltpu.VMEM(enc_w.shape, jnp.bfloat16),
            pltpu.SemaphoreType.DMA((len(pieces), layers, groups)),
            pltpu.SemaphoreType.DMA((2 * half,)),
            pltpu.SemaphoreType.DMA((8,)),
        ],
        compiler_params=params,
        cost_estimate=cost,
        name="encode",
    )(acts, enc_w, dec_w)
    terms, parts = list(results[:n]), results[n:]
    for k in range(1, n):
        terms[k] = lax.ppermute(terms[k], "src", [(i, (i + k) % n) for i in range(n)])
    early, late = parts[:layers], parts[layers:]
    own = pl.pallas_call(
        functools.partial(codes_kernel, n, share, tile_rows),
        out_shape=shape(half, share, 2 * block),
        in_specs=[smem] + [vmem] * (1 + n),
        out_specs=vmem,
        compiler_params=params,
        cost_estimate=cost,
        name="codes",
    )(active, enc_b.reshape(n, block), *terms)
    codes = []
    for k in range(groups):
        for r in range(2):
            perm = [
                (i * 2 + c, (i + k) % groups * 2 + (c ^ r)) for i in range(groups) for c in range(2)
            ]
            codes.append(lax.ppermute(own, ("tgt", "rep"), perm) if k + r else own)

    def hold(value, after):
        return pl.pallas_call(
            lambda *refs: None,
            out_shape=jax.ShapeDtypeStruct(value.shape, value.dtype),
            in_specs=[anywhere] * 2,
            out_specs=anywhere,
            input_output_aliases={0: 0},
            compiler_params=params,
            cost_estimate=cost,
            name="hold",
        )(value, after)

    parts = [early] + [[hold(part, codes[1])] for part in late]
    got = [[lax.ppermute(part, "src", pair) for part in piece] for piece in parts]

    sums, after = [], []
    for i, piece in enumerate(pieces):
        shapes = [shape(layers, share, piece[1])] * (2 * half)
        shapes[0] = shape(layers, share, piece[1], kind=jnp.float32)
        terms = pl.pallas_call(
            functools.partial(decode_kernel, n, layers),
            out_shape=shapes,
            in_specs=[vmem] * (2 * len(parts[i]) + 2 * groups) + [anywhere] * len(after),
            out_specs=[vmem] * len(shapes),
            scratch_shapes=[pltpu.VMEM((rows, 2 * groups * block), jnp.bfloat16)],
            compiler_params=params,
            cost_estimate=cost,
            name="decode",
        )(*parts[i], *got[i], *codes, *after)
        after = [terms[0]]
        for r in range(2):
            for j in range(half):
                perm = [
                    (d * 2 + c, (d + 2 * j) % n * 2 + (c ^ r)) for d in range(n) for c in range(2)
                ]
                term = terms[2 * j + r]
                sums.append(lax.ppermute(term, ("src", "rep"), perm) if j + r else term)

    return pl.pallas_call(
        functools.partial(add_kernel, n, pieces),
        out_shape=shape(layers, share, cols),
        in_specs=[vmem] * (2 + len(sums)),
        out_specs=anywhere,
        scratch_shapes=[
            pltpu.VMEM((layers, share, cols), jnp.bfloat16),
            pltpu.SemaphoreType.DMA((2 * len(pieces) * layers,)),
        ],
        compiler_params=params,
        cost_estimate=cost,
        name="add",
    )(dec_b, targets, *sums)


def solution(mesh):
    in_specs = (
        P(("parts", "rep"), "src"),
        P("src", "tgt"),
        P("tgt"),
        P(None, None, "src", "tgt"),
        P(None, "tgt"),
        P(None, ("parts", "rep", "src"), "tgt"),
        P(("parts", "rep"), None),
    )
    out_specs = P(None, ("parts", "rep", "src"), "tgt")
    return jax.shard_map(body, mesh=mesh, in_specs=in_specs, out_specs=out_specs, check_vma=False)
```

```python
import functools

import jax
import jax.numpy as jnp
from jax import lax
from jax.experimental import pallas as pl
from jax.experimental.pallas import tpu as pltpu
from jax.sharding import PartitionSpec as P

VMEM_BYTES = 32 * 1024 * 1024
LANES = 128
FIRST = 7


def cut_pieces(layers, columns):
    tiles = columns // LANES
    first = -(-tiles * FIRST // 8)
    pieces = [((layer,), 0, first * LANES) for layer in range(layers)]
    if first < tiles:
        pieces.append((tuple(range(layers)), first * LANES, (tiles - first) * LANES))
    return pieces


def part_copies(piece, dec_hbm, part_ref, sems):
    layers, first, width = piece
    groups, cols = dec_hbm.shape[1], dec_hbm.shape[3]
    start = pl.multiple_of(lax.axis_index("rep") * (cols // 2) + first, LANES)
    copies = []
    for i, layer in enumerate(layers):
        for group in range(groups):
            source = dec_hbm.at[layer, group, :, pl.ds(start, width)]
            sem = sems.at[i * groups + group]
            copies.append(pltpu.make_async_copy(source, part_ref.at[i, group], sem))
            copies[-1].start()
    return copies


def encode_kernel(n, pieces, acts_hbm, w_hbm, dec_hbm, *refs):
    term_refs, part_refs, refs = refs[:n], refs[n:-5], refs[-5:]
    acts_ref, w_ref, part_sems, acts_sems, w_sems = refs
    half = n // 2
    width = w_ref.shape[1] // half
    depth = w_ref.shape[0] // 8
    copies = []
    for i in range(2):
        for j in range(half):
            copies.append(
                pltpu.make_async_copy(
                    acts_hbm.at[j, i], acts_ref.at[i, j], acts_sems.at[i * half + j]
                )
            )
    for i in range(8):
        rows = slice(i * depth, (i + 1) * depth)
        copies.append(pltpu.make_async_copy(w_hbm.at[rows], w_ref.at[rows], w_sems.at[i]))
    for copy in copies:
        copy.start()
    for copy in copies:
        copy.wait()
    copies_part = []
    for i, piece in enumerate(pieces):
        copies_part += part_copies(piece, dec_hbm, part_refs[i], part_sems.at[i])
    src = lax.axis_index("src")
    for k in range(n):
        dest = lax.rem(src + k, n)
        rows = acts_ref[lax.rem(dest, 2)]
        rows = rows.reshape(rows.shape[0] * rows.shape[1], rows.shape[2])
        columns = pl.ds(pl.multiple_of((dest // 2) * width, width), width)
        term_refs[k][...] = jnp.dot(
            rows, w_ref[:, columns], preferred_element_type=jnp.float32
        ).astype(jnp.bfloat16)
    for copy in copies_part:
        copy.wait()


def codes_kernel(n, share, tile_rows, active_ref, bias_ref, *refs):
    term_refs, out_ref = refs[:n], refs[n]
    src = lax.axis_index("src")
    tgt = lax.axis_index("tgt")
    parity, half = lax.rem(src, 2), src // 2
    block = out_ref.shape[2] // 2
    pre = term_refs[0][...].astype(jnp.float32)
    for ref in term_refs[1:]:
        pre = pre + ref[...].astype(jnp.float32)
    tiles, slots = active_ref.shape
    for piece in range(2):
        columns = slice(piece * block, (piece + 1) * block)
        bias = bias_ref[pl.ds(half * 2 + piece, 1), :]
        wanted = tgt * n + half * 2 + piece
        flags = []
        for tile in range(tiles):
            flags.append(
                lax.fori_loop(
                    0,
                    slots,
                    lambda i, total: total + (active_ref[tile, i] == wanted).astype(jnp.int32),
                    jnp.int32(0),
                    unroll=slots <= 16,
                )
            )
        for group in range(n // 2):
            tile = ((group * 2 + parity) * share) // tile_rows
            flag = flags[0]
            for i in range(1, tiles):
                flag = jnp.where(tile == i, flags[i], flag)
            live = jnp.where(flag > 0, 1.0, 0.0).astype(jnp.float32)
            rows = slice(group * share, (group + 1) * share)
            value = live * jnp.maximum(pre[rows, columns] + bias, 0.0)
            out_ref[group, :, columns] = value.astype(jnp.bfloat16)


def decode_kernel(n, own_ref, got_ref, *refs):
    half = n // 2
    layers, groups, block, width = own_ref.shape
    code_refs, out_refs, lhs_ref = refs[: 2 * groups], refs[-2 * half - 1 : -1], refs[-1]
    src, tgt = lax.axis_index("src"), lax.axis_index("tgt")
    parity = lax.rem(src, 2)
    share = code_refs[0].shape[1]
    depth = groups * block
    for k in range(groups):
        place = lax.rem(tgt - k + groups, groups)
        for side in range(2):
            latents = parity if side == 0 else 1 - parity
            latents = pl.ds(pl.multiple_of(latents * block, block), block)
            columns = pl.ds(pl.multiple_of((side * groups + place) * block, block), block)
            for j in range(half):
                group = lax.rem(src // 2 + j, half)
                for r in range(2):
                    rows = slice((2 * j + r) * share, (2 * j + r + 1) * share)
                    lhs_ref[rows, columns] = code_refs[2 * k + r][group, :, latents]
    for layer in range(layers):
        own = own_ref[layer].reshape(depth, width)
        got = got_ref[layer].reshape(depth, width)
        total = jnp.dot(lhs_ref[:, :depth], own, preferred_element_type=jnp.float32)
        total += jnp.dot(lhs_ref[:, depth:], got, preferred_element_type=jnp.float32)
        for i, ref in enumerate(out_refs):
            ref[layer] = total[i * share : (i + 1) * share].astype(ref.dtype)


def add_kernel(n, pieces, chained, bias_ref, target_ref, *refs):
    out_hbm, out_ref, sems = refs[-3:]
    half = n // 2
    cols = target_ref.shape[2]
    rep = lax.axis_index("rep")
    copies = []
    for i, (layers, first, width) in enumerate(pieces):
        for side in range(2):
            core = rep if side == 0 else 1 - rep
            columns = pl.ds(pl.multiple_of(core * (cols // 2) + first, LANES), width)
            mine = refs[(2 * i + side) * half : (2 * i + side + 1) * half]
            for j, layer in enumerate(layers):
                total = bias_ref[layer : layer + 1, columns]
                total = total - target_ref[layer, :, columns].astype(jnp.float32)
                for ref in mine:
                    total = total + ref[j].astype(jnp.float32)
                out_ref[layer, :, columns] = total.astype(jnp.bfloat16)
                copies.append(
                    pltpu.make_async_copy(
                        out_ref.at[layer, :, columns],
                        out_hbm.at[layer, :, columns],
                        sems.at[len(copies)],
                    )
                )
                copies[-1].start()
    for copy in copies:
        copy.wait()


def body(acts, enc_w, enc_b, dec_w, dec_b, targets, active):
    n = lax.axis_size("src")
    rows, features = acts.shape
    layers, groups, block, cols = dec_w.shape
    share = rows // n
    half = n // 2
    pieces = cut_pieces(layers, cols // 2)
    tile_rows = rows // active.shape[0]
    pair = [(i, i ^ 1) for i in range(n)]
    params = pltpu.CompilerParams(vmem_limit_bytes=VMEM_BYTES)
    vmem = pl.BlockSpec(memory_space=pltpu.VMEM)
    smem = pl.BlockSpec(memory_space=pltpu.SMEM)
    anywhere = pl.BlockSpec(memory_space=pl.ANY)
    cost = pl.CostEstimate(flops=0, bytes_accessed=0, transcendentals=0)

    acts, enc_w, dec_w = (
        pltpu.with_memory_space_constraint(value, pltpu.HBM)
        for value in (acts.reshape(half, 2, share, features), enc_w, dec_w)
    )

    def shape(*extent, kind=jnp.bfloat16):
        return jax.ShapeDtypeStruct(extent, kind)

    results = pl.pallas_call(
        functools.partial(encode_kernel, n, pieces),
        out_shape=[shape(half * share, 2 * block)] * n
        + [shape(len(which), groups, block, width) for which, _, width in pieces],
        in_specs=[anywhere] * 3,
        out_specs=[vmem] * (n + len(pieces)),
        scratch_shapes=[
            pltpu.VMEM((2, half, share, features), jnp.bfloat16),
            pltpu.VMEM(enc_w.shape, jnp.bfloat16),
            pltpu.SemaphoreType.DMA((len(pieces), layers * groups)),
            pltpu.SemaphoreType.DMA((2 * half,)),
            pltpu.SemaphoreType.DMA((8,)),
        ],
        compiler_params=params,
        cost_estimate=cost,
        name="encode",
    )(acts, enc_w, dec_w)
    terms, parts = list(results[:n]), list(results[n:])
    for k in range(1, n):
        terms[k] = lax.ppermute(terms[k], "src", [(i, (i + k) % n) for i in range(n)])
    own = pl.pallas_call(
        functools.partial(codes_kernel, n, share, tile_rows),
        out_shape=shape(half, share, 2 * block),
        in_specs=[smem] + [vmem] * (1 + n),
        out_specs=vmem,
        compiler_params=params,
        cost_estimate=cost,
        name="codes",
    )(active, enc_b.reshape(n, block), *terms)
    codes = []
    for k in range(groups):
        for r in range(2):
            perm = [
                (i * 2 + c, (i + k) % groups * 2 + (c ^ r)) for i in range(groups) for c in range(2)
            ]
            codes.append(lax.ppermute(own, ("tgt", "rep"), perm) if k + r else own)

    def hold(value, after):
        return pl.pallas_call(
            lambda *refs: None,
            out_shape=jax.ShapeDtypeStruct(value.shape, value.dtype),
            in_specs=[anywhere] * 2,
            out_specs=anywhere,
            input_output_aliases={0: 0},
            compiler_params=params,
            cost_estimate=cost,
            name="hold",
        )(value, after)

    def add(some, out):
        chained = [] if out is None else [out]
        operands = [value for i in some for value in sums[i]]
        return pl.pallas_call(
            functools.partial(add_kernel, n, [pieces[i] for i in some], len(chained)),
            out_shape=shape(layers, share, cols),
            in_specs=[vmem] * (2 + len(operands)) + [anywhere] * len(chained),
            out_specs=anywhere,
            scratch_shapes=[
                pltpu.VMEM((layers, share, cols), jnp.bfloat16),
                pltpu.SemaphoreType.DMA((2 * len(some) * layers,)),
            ],
            input_output_aliases={2 + len(operands): 0} if chained else {},
            compiler_params=params,
            cost_estimate=cost,
            name="add",
        )(dec_b, targets, *operands, *chained)

    parts[1:layers] = [hold(part, codes[1]) for part in parts[1:layers]]
    got = [lax.ppermute(part, "src", pair) for part in parts[:layers]]
    sums, after, out = [], [], None
    for i, (which, _, width) in enumerate(pieces):
        if i == layers:
            out = add([0], None)
            after.append(out)
        shapes = [shape(len(which), share, width)] * (2 * half)
        shapes[0] = shape(len(which), share, width, kind=jnp.float32)
        terms = pl.pallas_call(
            functools.partial(decode_kernel, n),
            out_shape=shapes,
            in_specs=[vmem] * (2 + 2 * groups) + [anywhere] * len(after),
            out_specs=[vmem] * len(shapes),
            scratch_shapes=[pltpu.VMEM((rows, 2 * groups * block), jnp.bfloat16)],
            compiler_params=params,
            cost_estimate=cost,
            name="decode",
        )(parts[i], got[i], *codes, *after)
        after = [terms[0]]
        if i == 0:
            for part in parts[layers:]:
                got.append(lax.ppermute(hold(part, terms[0]), "src", pair))
        sums.append([])
        for r in range(2):
            for j in range(half):
                perm = [
                    (d * 2 + c, (d + 2 * j) % n * 2 + (c ^ r)) for d in range(n) for c in range(2)
                ]
                term = terms[2 * j + r]
                sums[i].append(lax.ppermute(term, ("src", "rep"), perm) if j + r else term)
    rest = range(0 if out is None else 1, len(pieces))
    return add(list(rest), out)


def solution(mesh):
    in_specs = (
        P(("parts", "rep"), "src"),
        P("src", "tgt"),
        P("tgt"),
        P(None, None, "src", "tgt"),
        P(None, "tgt"),
        P(None, ("parts", "rep", "src"), "tgt"),
        P(("parts", "rep"), None),
    )
    out_specs = P(None, ("parts", "rep", "src"), "tgt")
    return jax.shard_map(body, mesh=mesh, in_specs=in_specs, out_specs=out_specs, check_vma=False)
```

```python
import functools

import jax
import jax.numpy as jnp
from jax import lax
from jax.experimental import pallas as pl
from jax.experimental.pallas import tpu as pltpu
from jax.sharding import PartitionSpec as P

VMEM_BYTES = 32 * 1024 * 1024
LANES = 128
FIRST = 4


def cut_pieces(layers, columns):
    tiles = columns // LANES
    first = -(-tiles * FIRST // 8)
    every = tuple(range(layers))
    return [
        (every, start * LANES, (stop - start) * LANES)
        for start, stop in ((0, first), (first, tiles))
        if stop > start
    ]


def part_copies(piece, dec_hbm, part_ref, sems):
    layers, first, width = piece
    groups, cols = dec_hbm.shape[1], dec_hbm.shape[3]
    start = pl.multiple_of(lax.axis_index("rep") * (cols // 2) + first, LANES)
    copies = []
    for i, layer in enumerate(layers):
        for group in range(groups):
            source = dec_hbm.at[layer, group, :, pl.ds(start, width)]
            sem = sems.at[i * groups + group]
            copies.append(pltpu.make_async_copy(source, part_ref.at[i, group], sem))
            copies[-1].start()
    return copies


def encode_kernel(n, pieces, acts_hbm, w_hbm, dec_hbm, *refs):
    term_refs, part_refs, refs = refs[:n], refs[n:-5], refs[-5:]
    acts_ref, w_ref, part_sems, acts_sems, w_sems = refs
    half = n // 2
    width = w_ref.shape[1] // half
    depth = w_ref.shape[0] // 8
    copies = []
    for i in range(2):
        for j in range(half):
            copies.append(
                pltpu.make_async_copy(
                    acts_hbm.at[j, i], acts_ref.at[i, j], acts_sems.at[i * half + j]
                )
            )
    for i in range(8):
        rows = slice(i * depth, (i + 1) * depth)
        copies.append(pltpu.make_async_copy(w_hbm.at[rows], w_ref.at[rows], w_sems.at[i]))
    for copy in copies:
        copy.start()
    for copy in copies:
        copy.wait()
    copies_part = []
    for i, piece in enumerate(pieces):
        if i == 0:
            piece = ((lax.axis_index("parts"),), *piece[1:])
        copies_part += part_copies(piece, dec_hbm, part_refs[i], part_sems.at[i])
    src = lax.axis_index("src")
    for k in range(n):
        dest = lax.rem(src + k, n)
        rows = acts_ref[lax.rem(dest, 2)]
        rows = rows.reshape(rows.shape[0] * rows.shape[1], rows.shape[2])
        columns = pl.ds(pl.multiple_of((dest // 2) * width, width), width)
        term_refs[k][...] = jnp.dot(
            rows, w_ref[:, columns], preferred_element_type=jnp.float32
        ).astype(jnp.bfloat16)
    for copy in copies_part:
        copy.wait()


def codes_kernel(n, share, tile_rows, piece, active_ref, bias_ref, *refs):
    term_refs, (dec_hbm, out_ref, part_ref, part_sems) = refs[:n], refs[n:]
    copies_part = part_copies(piece, dec_hbm, part_ref, part_sems)
    src = lax.axis_index("src")
    tgt = lax.axis_index("tgt")
    parity, half = lax.rem(src, 2), src // 2
    block = out_ref.shape[2] // 2
    pre = term_refs[0][...].astype(jnp.float32)
    for ref in term_refs[1:]:
        pre = pre + ref[...].astype(jnp.float32)
    tiles, slots = active_ref.shape
    for piece in range(2):
        columns = slice(piece * block, (piece + 1) * block)
        bias = bias_ref[pl.ds(half * 2 + piece, 1), :]
        wanted = tgt * n + half * 2 + piece
        flags = []
        for tile in range(tiles):
            flags.append(
                lax.fori_loop(
                    0,
                    slots,
                    lambda i, total: total + (active_ref[tile, i] == wanted).astype(jnp.int32),
                    jnp.int32(0),
                    unroll=slots <= 16,
                )
            )
        for group in range(n // 2):
            tile = ((group * 2 + parity) * share) // tile_rows
            flag = flags[0]
            for i in range(1, tiles):
                flag = jnp.where(tile == i, flags[i], flag)
            live = jnp.where(flag > 0, 1.0, 0.0).astype(jnp.float32)
            rows = slice(group * share, (group + 1) * share)
            value = live * jnp.maximum(pre[rows, columns] + bias, 0.0)
            out_ref[group, :, columns] = value.astype(jnp.bfloat16)
    for copy in copies_part:
        copy.wait()


def decode_kernel(n, shared, own_ref, *refs):
    half = n // 2
    layers, groups, block, width = own_ref.shape
    got_refs, refs = refs[: 1 + shared], refs[1 + shared :]
    code_refs, out_refs, lhs_ref = refs[: 2 * groups], refs[-2 * half - 1 : -1], refs[-1]
    src, tgt = lax.axis_index("src"), lax.axis_index("tgt")
    parity = lax.rem(src, 2)
    share = code_refs[0].shape[1]
    depth = groups * block
    for k in range(groups):
        place = lax.rem(tgt - k + groups, groups)
        for side in range(2):
            latents = parity if side == 0 else 1 - parity
            latents = pl.ds(pl.multiple_of(latents * block, block), block)
            columns = pl.ds(pl.multiple_of((side * groups + place) * block, block), block)
            for j in range(half):
                group = lax.rem(src // 2 + j, half)
                for r in range(2):
                    rows = slice((2 * j + r) * share, (2 * j + r + 1) * share)
                    lhs_ref[rows, columns] = code_refs[2 * k + r][group, :, latents]
    for i in range(layers):
        layer = lax.rem(lax.axis_index("parts") + i, layers) if shared else i
        own = own_ref[layer].reshape(depth, width)
        got = (got_refs[i][0] if shared else got_refs[0][i]).reshape(depth, width)
        total = jnp.dot(lhs_ref[:, :depth], own, preferred_element_type=jnp.float32)
        total += jnp.dot(lhs_ref[:, depth:], got, preferred_element_type=jnp.float32)
        for j, ref in enumerate(out_refs):
            ref[layer] = total[j * share : (j + 1) * share].astype(ref.dtype)


def add_kernel(n, pieces, bias_ref, target_ref, *refs):
    out_hbm, out_ref, sems = refs[-3:]
    half = n // 2
    cols = target_ref.shape[2]
    rep = lax.axis_index("rep")
    copies = []
    for i, (layers, first, width) in enumerate(pieces):
        for side in range(2):
            core = rep if side == 0 else 1 - rep
            columns = pl.ds(pl.multiple_of(core * (cols // 2) + first, LANES), width)
            mine = refs[(2 * i + side) * half : (2 * i + side + 1) * half]
            for j, layer in enumerate(layers):
                total = bias_ref[layer : layer + 1, columns]
                total = total - target_ref[layer, :, columns].astype(jnp.float32)
                for ref in mine:
                    total = total + ref[j].astype(jnp.float32)
                out_ref[layer, :, columns] = total.astype(jnp.bfloat16)
                copies.append(
                    pltpu.make_async_copy(
                        out_ref.at[layer, :, columns],
                        out_hbm.at[layer, :, columns],
                        sems.at[len(copies)],
                    )
                )
                copies[-1].start()
    for copy in copies:
        copy.wait()


def body(acts, enc_w, enc_b, dec_w, dec_b, targets, active):
    n = lax.axis_size("src")
    rows, features = acts.shape
    layers, groups, block, cols = dec_w.shape
    share = rows // n
    half = n // 2
    pieces = cut_pieces(layers, cols // 2)
    tile_rows = rows // active.shape[0]
    pair = [(i, i ^ 1) for i in range(n)]
    params = pltpu.CompilerParams(vmem_limit_bytes=VMEM_BYTES)
    vmem = pl.BlockSpec(memory_space=pltpu.VMEM)
    smem = pl.BlockSpec(memory_space=pltpu.SMEM)
    anywhere = pl.BlockSpec(memory_space=pl.ANY)
    cost = pl.CostEstimate(flops=0, bytes_accessed=0, transcendentals=0)

    acts, enc_w, dec_w = (
        pltpu.with_memory_space_constraint(value, pltpu.HBM)
        for value in (acts.reshape(half, 2, share, features), enc_w, dec_w)
    )

    def shape(*extent, kind=jnp.bfloat16):
        return jax.ShapeDtypeStruct(extent, kind)

    results = pl.pallas_call(
        functools.partial(encode_kernel, n, pieces),
        out_shape=[shape(half * share, 2 * block)] * n
        + [
            shape(1 if i == 0 else layers, groups, block, width)
            for i, (_, _, width) in enumerate(pieces)
        ],
        in_specs=[anywhere] * 3,
        out_specs=[vmem] * (n + len(pieces)),
        scratch_shapes=[
            pltpu.VMEM((2, half, share, features), jnp.bfloat16),
            pltpu.VMEM(enc_w.shape, jnp.bfloat16),
            pltpu.SemaphoreType.DMA((len(pieces), layers * groups)),
            pltpu.SemaphoreType.DMA((2 * half,)),
            pltpu.SemaphoreType.DMA((8,)),
        ],
        compiler_params=params,
        cost_estimate=cost,
        name="encode",
    )(acts, enc_w, dec_w)
    terms, parts = list(results[:n]), list(results[n:])
    for k in range(1, n):
        terms[k] = lax.ppermute(terms[k], "src", [(i, (i + k) % n) for i in range(n)])
    own, own_part = pl.pallas_call(
        functools.partial(codes_kernel, n, share, tile_rows, pieces[0]),
        out_shape=[
            shape(half, share, 2 * block),
            shape(layers, groups, block, pieces[0][2]),
        ],
        in_specs=[smem] + [vmem] * (1 + n) + [anywhere],
        out_specs=[vmem] * 2,
        scratch_shapes=[pltpu.SemaphoreType.DMA((layers * groups,))],
        compiler_params=params,
        cost_estimate=cost,
        name="codes",
    )(active, enc_b.reshape(n, block), *terms, dec_w)
    codes = []
    for k in range(groups):
        for r in range(2):
            perm = [
                (i * 2 + c, (i + k) % groups * 2 + (c ^ r)) for i in range(groups) for c in range(2)
            ]
            codes.append(lax.ppermute(own, ("tgt", "rep"), perm) if k + r else own)

    def hold(value, after):
        return pl.pallas_call(
            lambda *refs: None,
            out_shape=jax.ShapeDtypeStruct(value.shape, value.dtype),
            in_specs=[anywhere] * 2,
            out_specs=anywhere,
            input_output_aliases={0: 0},
            compiler_params=params,
            cost_estimate=cost,
            name="hold",
        )(value, after)

    got = [[lax.ppermute(parts[0], "src", pair)]]
    got[0].append(lax.ppermute(got[0][0], "parts", [(0, 1), (1, 0)]))
    for part in parts[1:]:
        got.append([lax.ppermute(hold(part, codes[1]), "src", pair)])
    parts[0] = own_part
    sums, after = [], []
    for i, (_, _, width) in enumerate(pieces):
        shapes = [shape(layers, share, width)] * (2 * half)
        shapes[0] = shape(layers, share, width, kind=jnp.float32)
        terms = pl.pallas_call(
            functools.partial(decode_kernel, n, i == 0),
            out_shape=shapes,
            in_specs=[vmem] * (1 + len(got[i]) + 2 * groups) + [anywhere] * len(after),
            out_specs=[vmem] * len(shapes),
            scratch_shapes=[pltpu.VMEM((rows, 2 * groups * block), jnp.bfloat16)],
            compiler_params=params,
            cost_estimate=cost,
            name="decode",
        )(parts[i], *got[i], *codes, *after)
        after = [terms[0]]
        for r in range(2):
            for j in range(half):
                perm = [
                    (d * 2 + c, (d + 2 * j) % n * 2 + (c ^ r)) for d in range(n) for c in range(2)
                ]
                term = terms[2 * j + r]
                sums.append(lax.ppermute(term, ("src", "rep"), perm) if j + r else term)

    return pl.pallas_call(
        functools.partial(add_kernel, n, pieces),
        out_shape=shape(layers, share, cols),
        in_specs=[vmem] * (2 + len(sums)),
        out_specs=anywhere,
        scratch_shapes=[
            pltpu.VMEM((layers, share, cols), jnp.bfloat16),
            pltpu.SemaphoreType.DMA((2 * len(pieces) * layers,)),
        ],
        compiler_params=params,
        cost_estimate=cost,
        name="add",
    )(dec_b, targets, *sums)


def solution(mesh):
    in_specs = (
        P(("parts", "rep"), "src"),
        P("src", "tgt"),
        P("tgt"),
        P(None, None, "src", "tgt"),
        P(None, "tgt"),
        P(None, ("parts", "rep", "src"), "tgt"),
        P(("parts", "rep"), None),
    )
    out_specs = P(None, ("parts", "rep", "src"), "tgt")
    return jax.shard_map(body, mesh=mesh, in_specs=in_specs, out_specs=out_specs, check_vma=False)
```

```python
import functools

import jax
import jax.numpy as jnp
from jax import lax
from jax.experimental import pallas as pl
from jax.experimental.pallas import tpu as pltpu
from jax.sharding import PartitionSpec as P

VMEM_BYTES = 32 * 1024 * 1024
LANES = 128
SHARES = (3, 3, 2)


def cut_pieces(layers, columns):
    tiles = columns // LANES
    pieces, start = [], 0
    for i, eighths in enumerate(SHARES):
        stop = tiles if i + 1 == len(SHARES) else min(tiles, start + -(-tiles * eighths // 8))
        if stop > start:
            pieces.append((tuple(range(layers)), start * LANES, (stop - start) * LANES))
        start = stop
    return pieces


def part_copies(piece, dec_hbm, part_ref, sems):
    layers, first, width = piece
    groups, cols = dec_hbm.shape[1], dec_hbm.shape[3]
    start = pl.multiple_of(lax.axis_index("rep") * (cols // 2) + first, LANES)
    copies = []
    for i, layer in enumerate(layers):
        for group in range(groups):
            source = dec_hbm.at[layer, group, :, pl.ds(start, width)]
            sem = sems.at[i * groups + group]
            copies.append(pltpu.make_async_copy(source, part_ref.at[i, group], sem))
            copies[-1].start()
    return copies


def encode_kernel(n, pieces, acts_hbm, w_hbm, dec_hbm, *refs):
    term_refs, part_refs, refs = refs[:n], refs[n:-5], refs[-5:]
    acts_ref, w_ref, part_sems, acts_sems, w_sems = refs
    half = n // 2
    width = w_ref.shape[1] // half
    depth = w_ref.shape[0] // 8
    copies = []
    for i in range(2):
        for j in range(half):
            copies.append(
                pltpu.make_async_copy(
                    acts_hbm.at[j, i], acts_ref.at[i, j], acts_sems.at[i * half + j]
                )
            )
    for i in range(8):
        rows = slice(i * depth, (i + 1) * depth)
        copies.append(pltpu.make_async_copy(w_hbm.at[rows], w_ref.at[rows], w_sems.at[i]))
    for copy in copies:
        copy.start()
    for copy in copies:
        copy.wait()
    copies_part = []
    for i, piece in enumerate(pieces):
        if i == 0:
            piece = ((lax.axis_index("parts"),), *piece[1:])
        copies_part += part_copies(piece, dec_hbm, part_refs[i], part_sems.at[i])
    src = lax.axis_index("src")
    for k in range(n):
        dest = lax.rem(src + k, n)
        rows = acts_ref[lax.rem(dest, 2)]
        rows = rows.reshape(rows.shape[0] * rows.shape[1], rows.shape[2])
        columns = pl.ds(pl.multiple_of((dest // 2) * width, width), width)
        term_refs[k][...] = jnp.dot(
            rows, w_ref[:, columns], preferred_element_type=jnp.float32
        ).astype(jnp.bfloat16)
    for copy in copies_part:
        copy.wait()


def codes_kernel(n, share, tile_rows, active_ref, bias_ref, *refs):
    term_refs, out_ref = refs[:n], refs[n]
    src = lax.axis_index("src")
    tgt = lax.axis_index("tgt")
    parity, half = lax.rem(src, 2), src // 2
    block = out_ref.shape[2] // 2
    pre = term_refs[0][...].astype(jnp.float32)
    for ref in term_refs[1:]:
        pre = pre + ref[...].astype(jnp.float32)
    tiles, slots = active_ref.shape
    for piece in range(2):
        columns = slice(piece * block, (piece + 1) * block)
        bias = bias_ref[pl.ds(half * 2 + piece, 1), :]
        wanted = tgt * n + half * 2 + piece
        flags = []
        for tile in range(tiles):
            flags.append(
                lax.fori_loop(
                    0,
                    slots,
                    lambda i, total: total + (active_ref[tile, i] == wanted).astype(jnp.int32),
                    jnp.int32(0),
                    unroll=slots <= 16,
                )
            )
        for group in range(n // 2):
            tile = ((group * 2 + parity) * share) // tile_rows
            flag = flags[0]
            for i in range(1, tiles):
                flag = jnp.where(tile == i, flags[i], flag)
            live = jnp.where(flag > 0, 1.0, 0.0).astype(jnp.float32)
            rows = slice(group * share, (group + 1) * share)
            value = live * jnp.maximum(pre[rows, columns] + bias, 0.0)
            out_ref[group, :, columns] = value.astype(jnp.bfloat16)


def decode_kernel(n, piece, shared, dec_ref, *refs):
    half = n // 2
    layers, groups, block, cols = dec_ref.shape
    _, first, width = piece
    got_refs, refs = refs[: 1 + shared], refs[1 + shared :]
    code_refs, out_refs, lhs_ref = refs[: 2 * groups], refs[-2 * half - 1 : -1], refs[-1]
    src, tgt = lax.axis_index("src"), lax.axis_index("tgt")
    parity = lax.rem(src, 2)
    share = code_refs[0].shape[1]
    depth = groups * block
    for k in range(groups):
        place = lax.rem(tgt - k + groups, groups)
        for side in range(2):
            latents = parity if side == 0 else 1 - parity
            latents = pl.ds(pl.multiple_of(latents * block, block), block)
            columns = pl.ds(pl.multiple_of((side * groups + place) * block, block), block)
            for j in range(half):
                group = lax.rem(src // 2 + j, half)
                for r in range(2):
                    rows = slice((2 * j + r) * share, (2 * j + r + 1) * share)
                    lhs_ref[rows, columns] = code_refs[2 * k + r][group, :, latents]
    start = pl.multiple_of(lax.axis_index("rep") * (cols // 2) + first, LANES)
    for i in range(layers):
        layer = lax.rem(lax.axis_index("parts") + i, layers) if shared else i
        own = dec_ref[layer, :, :, pl.ds(start, width)].reshape(depth, width)
        got = (got_refs[i][0] if shared else got_refs[0][i]).reshape(depth, width)
        total = jnp.dot(lhs_ref[:, :depth], own, preferred_element_type=jnp.float32)
        total += jnp.dot(lhs_ref[:, depth:], got, preferred_element_type=jnp.float32)
        for j, ref in enumerate(out_refs):
            ref[layer] = total[j * share : (j + 1) * share].astype(ref.dtype)


def add_kernel(n, pieces, bias_ref, target_ref, *refs):
    out_hbm, out_ref, sems = refs[-3:]
    half = n // 2
    cols = target_ref.shape[2]
    rep = lax.axis_index("rep")
    copies = []
    for i, (layers, first, width) in enumerate(pieces):
        for side in range(2):
            core = rep if side == 0 else 1 - rep
            columns = pl.ds(pl.multiple_of(core * (cols // 2) + first, LANES), width)
            mine = refs[(2 * i + side) * half : (2 * i + side + 1) * half]
            for j, layer in enumerate(layers):
                total = bias_ref[layer : layer + 1, columns]
                total = total - target_ref[layer, :, columns].astype(jnp.float32)
                for ref in mine:
                    total = total + ref[j].astype(jnp.float32)
                out_ref[layer, :, columns] = total.astype(jnp.bfloat16)
                copies.append(
                    pltpu.make_async_copy(
                        out_ref.at[layer, :, columns],
                        out_hbm.at[layer, :, columns],
                        sems.at[len(copies)],
                    )
                )
                copies[-1].start()
    for copy in copies:
        copy.wait()


def body(acts, enc_w, enc_b, dec_w, dec_b, targets, active):
    n = lax.axis_size("src")
    rows, features = acts.shape
    layers, groups, block, cols = dec_w.shape
    share = rows // n
    half = n // 2
    pieces = cut_pieces(layers, cols // 2)
    tile_rows = rows // active.shape[0]
    pair = [(i, i ^ 1) for i in range(n)]
    params = pltpu.CompilerParams(vmem_limit_bytes=VMEM_BYTES)
    vmem = pl.BlockSpec(memory_space=pltpu.VMEM)
    smem = pl.BlockSpec(memory_space=pltpu.SMEM)
    anywhere = pl.BlockSpec(memory_space=pl.ANY)
    cost = pl.CostEstimate(flops=0, bytes_accessed=0, transcendentals=0)

    dec_rows = dec_w
    acts, enc_w, dec_w = (
        pltpu.with_memory_space_constraint(value, pltpu.HBM)
        for value in (acts.reshape(half, 2, share, features), enc_w, dec_w)
    )

    def shape(*extent, kind=jnp.bfloat16):
        return jax.ShapeDtypeStruct(extent, kind)

    results = pl.pallas_call(
        functools.partial(encode_kernel, n, pieces),
        out_shape=[shape(half * share, 2 * block)] * n
        + [
            shape(1 if i == 0 else layers, groups, block, width)
            for i, (_, _, width) in enumerate(pieces)
        ],
        in_specs=[anywhere] * 3,
        out_specs=[vmem] * (n + len(pieces)),
        scratch_shapes=[
            pltpu.VMEM((2, half, share, features), jnp.bfloat16),
            pltpu.VMEM(enc_w.shape, jnp.bfloat16),
            pltpu.SemaphoreType.DMA((len(pieces), layers * groups)),
            pltpu.SemaphoreType.DMA((2 * half,)),
            pltpu.SemaphoreType.DMA((8,)),
        ],
        compiler_params=params,
        cost_estimate=cost,
        name="encode",
    )(acts, enc_w, dec_w)
    terms, parts = list(results[:n]), list(results[n:])
    for k in range(1, n):
        terms[k] = lax.ppermute(terms[k], "src", [(i, (i + k) % n) for i in range(n)])
    own = pl.pallas_call(
        functools.partial(codes_kernel, n, share, tile_rows),
        out_shape=shape(half, share, 2 * block),
        in_specs=[smem] + [vmem] * (1 + n),
        out_specs=vmem,
        compiler_params=params,
        cost_estimate=cost,
        name="codes",
    )(active, enc_b.reshape(n, block), *terms)
    codes = []
    for k in range(groups):
        for r in range(2):
            perm = [
                (i * 2 + c, (i + k) % groups * 2 + (c ^ r)) for i in range(groups) for c in range(2)
            ]
            codes.append(lax.ppermute(own, ("tgt", "rep"), perm) if k + r else own)

    def hold(value, after):
        return pl.pallas_call(
            lambda *refs: None,
            out_shape=jax.ShapeDtypeStruct(value.shape, value.dtype),
            in_specs=[anywhere] * 2,
            out_specs=anywhere,
            input_output_aliases={0: 0},
            compiler_params=params,
            cost_estimate=cost,
            name="hold",
        )(value, after)

    got = [[lax.ppermute(parts[0], "src", pair)]]
    got[0].append(lax.ppermute(got[0][0], "parts", [(0, 1), (1, 0)]))
    if len(pieces) > 1:
        got.append([lax.ppermute(hold(parts[1], own), "src", pair)])
    def add(some, begun):
        operands = [value for i in some for value in sums[i]]
        return pl.pallas_call(
            functools.partial(add_kernel, n, [pieces[i] for i in some]),
            out_shape=shape(layers, share, cols),
            in_specs=[vmem] * (2 + len(operands)) + [anywhere] * len(begun),
            out_specs=anywhere,
            scratch_shapes=[
                pltpu.VMEM((layers, share, cols), jnp.bfloat16),
                pltpu.SemaphoreType.DMA((2 * len(some) * layers,)),
            ],
            input_output_aliases={2 + len(operands): 0} if begun else {},
            compiler_params=params,
            cost_estimate=cost,
            name="add",
        )(dec_b, targets, *operands, *begun)

    sums, after, begun = [], [], []
    for i, (_, _, width) in enumerate(pieces):
        if i == 2:
            begun = [add([0], [])]
            after.append(begun[0])
        shapes = [shape(layers, share, width)] * (2 * half)
        shapes[0] = shape(layers, share, width, kind=jnp.float32)
        terms = pl.pallas_call(
            functools.partial(decode_kernel, n, pieces[i], i == 0),
            out_shape=shapes,
            in_specs=[vmem] * (1 + len(got[i]) + 2 * groups) + [anywhere] * len(after),
            out_specs=[vmem] * len(shapes),
            scratch_shapes=[pltpu.VMEM((rows, 2 * groups * block), jnp.bfloat16)],
            compiler_params=params,
            cost_estimate=cost,
            name="decode",
        )(dec_rows, *got[i], *codes, *after)
        after = [terms[0]]
        if i == 0:
            for part in parts[2:]:
                got.append([lax.ppermute(hold(part, own), "src", pair)])
        sums.append([])
        for r in range(2):
            for j in range(half):
                perm = [
                    (d * 2 + c, (d + 2 * j) % n * 2 + (c ^ r)) for d in range(n) for c in range(2)
                ]
                term = terms[2 * j + r]
                sums[i].append(lax.ppermute(term, ("src", "rep"), perm) if j + r else term)

    return add(list(range(len(begun), len(pieces))), begun)


def solution(mesh):
    in_specs = (
        P(("parts", "rep"), "src"),
        P("src", "tgt"),
        P("tgt"),
        P(None, None, "src", "tgt"),
        P(None, "tgt"),
        P(None, ("parts", "rep", "src"), "tgt"),
        P(("parts", "rep"), None),
    )
    out_specs = P(None, ("parts", "rep", "src"), "tgt")
    return jax.shard_map(body, mesh=mesh, in_specs=in_specs, out_specs=out_specs, check_vma=False)
```

```python
import functools

import jax
import jax.numpy as jnp
from jax import lax
from jax.experimental import pallas as pl
from jax.experimental.pallas import tpu as pltpu
from jax.sharding import PartitionSpec as P

VMEM_BYTES = 32 * 1024 * 1024
LANES = 128
SHARES = (3, 3, 2)


def cut_pieces(layers, columns):
    tiles = columns // LANES
    pieces, start = [], 0
    for i, eighths in enumerate(SHARES):
        stop = tiles if i + 1 == len(SHARES) else min(tiles, start + -(-tiles * eighths // 8))
        if stop > start:
            pieces.append((tuple(range(layers)), start * LANES, (stop - start) * LANES))
        start = stop
    return pieces


def part_copies(piece, dec_hbm, part_ref, sems):
    layers, first, width = piece
    groups, cols = dec_hbm.shape[1], dec_hbm.shape[3]
    start = pl.multiple_of(lax.axis_index("rep") * (cols // 2) + first, LANES)
    copies = []
    for i, layer in enumerate(layers):
        for group in range(groups):
            source = dec_hbm.at[layer, group, :, pl.ds(start, width)]
            sem = sems.at[i * groups + group]
            copies.append(pltpu.make_async_copy(source, part_ref.at[i, group], sem))
            copies[-1].start()
    return copies


def encode_kernel(n, pieces, acts_hbm, w_hbm, dec_hbm, *refs):
    term_refs, part_refs, refs = refs[:n], refs[n:-5], refs[-5:]
    acts_ref, w_ref, part_sems, acts_sems, w_sems = refs
    half = n // 2
    width = w_ref.shape[1] // half
    depth = w_ref.shape[0] // 8
    copies = []
    for i in range(2):
        for j in range(half):
            copies.append(
                pltpu.make_async_copy(
                    acts_hbm.at[j, i], acts_ref.at[i, j], acts_sems.at[i * half + j]
                )
            )
    for i in range(8):
        rows = slice(i * depth, (i + 1) * depth)
        copies.append(pltpu.make_async_copy(w_hbm.at[rows], w_ref.at[rows], w_sems.at[i]))
    for copy in copies:
        copy.start()
    for copy in copies:
        copy.wait()
    copies_part = []
    for i, piece in enumerate(pieces):
        if i == 0:
            piece = ((lax.axis_index("parts"),), *piece[1:])
        copies_part += part_copies(piece, dec_hbm, part_refs[i], part_sems.at[i])
    src = lax.axis_index("src")
    for k in range(n):
        dest = lax.rem(src + k, n)
        rows = acts_ref[lax.rem(dest, 2)]
        rows = rows.reshape(rows.shape[0] * rows.shape[1], rows.shape[2])
        columns = pl.ds(pl.multiple_of((dest // 2) * width, width), width)
        term_refs[k][...] = jnp.dot(
            rows, w_ref[:, columns], preferred_element_type=jnp.float32
        ).astype(jnp.bfloat16)
    for copy in copies_part:
        copy.wait()


def codes_kernel(n, share, tile_rows, active_ref, bias_ref, *refs):
    term_refs, out_ref = refs[:n], refs[n]
    src = lax.axis_index("src")
    tgt = lax.axis_index("tgt")
    parity, half = lax.rem(src, 2), src // 2
    block = out_ref.shape[2] // 2
    pre = term_refs[0][...].astype(jnp.float32)
    for ref in term_refs[1:]:
        pre = pre + ref[...].astype(jnp.float32)
    tiles, slots = active_ref.shape
    for piece in range(2):
        columns = slice(piece * block, (piece + 1) * block)
        bias = bias_ref[pl.ds(half * 2 + piece, 1), :]
        wanted = tgt * n + half * 2 + piece
        flags = []
        for tile in range(tiles):
            flags.append(
                lax.fori_loop(
                    0,
                    slots,
                    lambda i, total: total + (active_ref[tile, i] == wanted).astype(jnp.int32),
                    jnp.int32(0),
                    unroll=slots <= 16,
                )
            )
        for group in range(n // 2):
            tile = ((group * 2 + parity) * share) // tile_rows
            flag = flags[0]
            for i in range(1, tiles):
                flag = jnp.where(tile == i, flags[i], flag)
            live = jnp.where(flag > 0, 1.0, 0.0).astype(jnp.float32)
            rows = slice(group * share, (group + 1) * share)
            value = live * jnp.maximum(pre[rows, columns] + bias, 0.0)
            out_ref[group, :, columns] = value.astype(jnp.bfloat16)


def decode_kernel(n, piece, shared, dec_ref, *refs):
    half = n // 2
    layers, groups, block, cols = dec_ref.shape
    _, first, width = piece
    got_refs, refs = refs[: 1 + shared], refs[1 + shared :]
    codes_ref, out_refs, lhs_ref = refs[0], refs[-2 * half - 1 : -1], refs[-1]
    src = lax.axis_index("src")
    parity = lax.rem(src, 2)
    share = codes_ref.shape[2]
    depth = groups * block
    for place in range(groups):
        for r in range(2):
            origin = place * 2 + lax.rem(lax.axis_index("rep") + r, 2)
            for side in range(2):
                latents = parity if side == 0 else 1 - parity
                latents = pl.ds(pl.multiple_of(latents * block, block), block)
                columns = slice((side * groups + place) * block, (side * groups + place + 1) * block)
                for j in range(half):
                    group = lax.rem(src // 2 + j, half)
                    rows = slice((2 * j + r) * share, (2 * j + r + 1) * share)
                    lhs_ref[rows, columns] = codes_ref[origin, group, :, latents]
    start = pl.multiple_of(lax.axis_index("rep") * (cols // 2) + first, LANES)
    for i in range(layers):
        layer = lax.rem(lax.axis_index("parts") + i, layers) if shared else i
        own = dec_ref[layer, :, :, pl.ds(start, width)].reshape(depth, width)
        got = (got_refs[i][0] if shared else got_refs[0][i]).reshape(depth, width)
        total = jnp.dot(lhs_ref[:, :depth], own, preferred_element_type=jnp.float32)
        total += jnp.dot(lhs_ref[:, depth:], got, preferred_element_type=jnp.float32)
        for j, ref in enumerate(out_refs):
            ref[layer] = total[j * share : (j + 1) * share].astype(ref.dtype)


def add_kernel(n, pieces, bias_ref, target_ref, *refs):
    out_hbm, out_ref, sems = refs[-3:]
    half = n // 2
    cols = target_ref.shape[2]
    rep = lax.axis_index("rep")
    copies = []
    for i, (layers, first, width) in enumerate(pieces):
        for side in range(2):
            core = rep if side == 0 else 1 - rep
            columns = pl.ds(pl.multiple_of(core * (cols // 2) + first, LANES), width)
            mine = refs[(2 * i + side) * half : (2 * i + side + 1) * half]
            for j, layer in enumerate(layers):
                total = bias_ref[layer : layer + 1, columns]
                total = total - target_ref[layer, :, columns].astype(jnp.float32)
                for ref in mine:
                    total = total + ref[j].astype(jnp.float32)
                out_ref[layer, :, columns] = total.astype(jnp.bfloat16)
                copies.append(
                    pltpu.make_async_copy(
                        out_ref.at[layer, :, columns],
                        out_hbm.at[layer, :, columns],
                        sems.at[len(copies)],
                    )
                )
                copies[-1].start()
    for copy in copies:
        copy.wait()


def body(acts, enc_w, enc_b, dec_w, dec_b, targets, active):
    n = lax.axis_size("src")
    rows, features = acts.shape
    layers, groups, block, cols = dec_w.shape
    share = rows // n
    half = n // 2
    pieces = cut_pieces(layers, cols // 2)
    tile_rows = rows // active.shape[0]
    pair = [(i, i ^ 1) for i in range(n)]
    params = pltpu.CompilerParams(vmem_limit_bytes=VMEM_BYTES)
    vmem = pl.BlockSpec(memory_space=pltpu.VMEM)
    smem = pl.BlockSpec(memory_space=pltpu.SMEM)
    anywhere = pl.BlockSpec(memory_space=pl.ANY)
    cost = pl.CostEstimate(flops=0, bytes_accessed=0, transcendentals=0)

    dec_rows = dec_w
    acts, enc_w, dec_w = (
        pltpu.with_memory_space_constraint(value, pltpu.HBM)
        for value in (acts.reshape(half, 2, share, features), enc_w, dec_w)
    )

    def shape(*extent, kind=jnp.bfloat16):
        return jax.ShapeDtypeStruct(extent, kind)

    results = pl.pallas_call(
        functools.partial(encode_kernel, n, pieces),
        out_shape=[shape(half * share, 2 * block)] * n
        + [
            shape(1 if i == 0 else layers, groups, block, width)
            for i, (_, _, width) in enumerate(pieces)
        ],
        in_specs=[anywhere] * 3,
        out_specs=[vmem] * (n + len(pieces)),
        scratch_shapes=[
            pltpu.VMEM((2, half, share, features), jnp.bfloat16),
            pltpu.VMEM(enc_w.shape, jnp.bfloat16),
            pltpu.SemaphoreType.DMA((len(pieces), layers * groups)),
            pltpu.SemaphoreType.DMA((2 * half,)),
            pltpu.SemaphoreType.DMA((8,)),
        ],
        compiler_params=params,
        cost_estimate=cost,
        name="encode",
    )(acts, enc_w, dec_w)
    terms, parts = list(results[:n]), list(results[n:])
    for k in range(1, n):
        terms[k] = lax.ppermute(terms[k], "src", [(i, (i + k) % n) for i in range(n)])
    own = pl.pallas_call(
        functools.partial(codes_kernel, n, share, tile_rows),
        out_shape=shape(half, share, 2 * block),
        in_specs=[smem] + [vmem] * (1 + n),
        out_specs=vmem,
        compiler_params=params,
        cost_estimate=cost,
        name="codes",
    )(active, enc_b.reshape(n, block), *terms)
    codes = lax.all_gather(own, ("tgt", "rep"), axis=0, tiled=False)

    def hold(value, after):
        return pl.pallas_call(
            lambda *refs: None,
            out_shape=jax.ShapeDtypeStruct(value.shape, value.dtype),
            in_specs=[anywhere] * 2,
            out_specs=anywhere,
            input_output_aliases={0: 0},
            compiler_params=params,
            cost_estimate=cost,
            name="hold",
        )(value, after)

    got = [[lax.ppermute(parts[0], "src", pair)]]
    got[0].append(lax.ppermute(got[0][0], "parts", [(0, 1), (1, 0)]))
    if len(pieces) > 1:
        got.append([lax.ppermute(hold(parts[1], own), "src", pair)])
    def add(some, begun):
        operands = [value for i in some for value in sums[i]]
        return pl.pallas_call(
            functools.partial(add_kernel, n, [pieces[i] for i in some]),
            out_shape=shape(layers, share, cols),
            in_specs=[vmem] * (2 + len(operands)) + [anywhere] * len(begun),
            out_specs=anywhere,
            scratch_shapes=[
                pltpu.VMEM((layers, share, cols), jnp.bfloat16),
                pltpu.SemaphoreType.DMA((2 * len(some) * layers,)),
            ],
            input_output_aliases={2 + len(operands): 0} if begun else {},
            compiler_params=params,
            cost_estimate=cost,
            name="add",
        )(dec_b, targets, *operands, *begun)

    sums, after, begun = [], [], []
    for i, (_, _, width) in enumerate(pieces):
        if i == 2:
            begun = [add([0], [])]
            after.append(begun[0])
        shapes = [shape(layers, share, width)] * (2 * half)
        shapes[0] = shape(layers, share, width, kind=jnp.float32)
        terms = pl.pallas_call(
            functools.partial(decode_kernel, n, pieces[i], i == 0),
            out_shape=shapes,
            in_specs=[vmem] * (1 + len(got[i]) + 1) + [anywhere] * len(after),
            out_specs=[vmem] * len(shapes),
            scratch_shapes=[pltpu.VMEM((rows, 2 * groups * block), jnp.bfloat16)],
            compiler_params=params,
            cost_estimate=cost,
            name="decode",
        )(dec_rows, *got[i], codes, *after)
        after = [terms[0]]
        if i == 0:
            for part in parts[2:]:
                got.append([lax.ppermute(hold(part, own), "src", pair)])
        sums.append([])
        for r in range(2):
            for j in range(half):
                perm = [
                    (d * 2 + c, (d + 2 * j) % n * 2 + (c ^ r)) for d in range(n) for c in range(2)
                ]
                term = terms[2 * j + r]
                sums[i].append(lax.ppermute(term, ("src", "rep"), perm) if j + r else term)

    return add(list(range(len(begun), len(pieces))), begun)


def solution(mesh):
    in_specs = (
        P(("parts", "rep"), "src"),
        P("src", "tgt"),
        P("tgt"),
        P(None, None, "src", "tgt"),
        P(None, "tgt"),
        P(None, ("parts", "rep", "src"), "tgt"),
        P(("parts", "rep"), None),
    )
    out_specs = P(None, ("parts", "rep", "src"), "tgt")
    return jax.shard_map(body, mesh=mesh, in_specs=in_specs, out_specs=out_specs, check_vma=False)
```

```python
import functools

import jax
import jax.numpy as jnp
from jax import lax
from jax.experimental import pallas as pl
from jax.experimental.pallas import tpu as pltpu
from jax.sharding import PartitionSpec as P

VMEM_BYTES = 32 * 1024 * 1024
LANES = 128
SHARES = (4, 4)


def cut_pieces(layers, columns):
    tiles = columns // LANES
    pieces, start = [], 0
    for i, eighths in enumerate(SHARES):
        stop = tiles if i + 1 == len(SHARES) else min(tiles, start + -(-tiles * eighths // 8))
        if stop > start:
            pieces.append((tuple(range(layers)), start * LANES, (stop - start) * LANES))
        start = stop
    return pieces


def peer(index, k, n):
    return index ^ k if n & (n - 1) == 0 else (index + k) % n


def part_copies(piece, dec_hbm, part_ref, sems):
    layers, first, width = piece
    groups, cols = dec_hbm.shape[1], dec_hbm.shape[3]
    start = pl.multiple_of(lax.axis_index("rep") * (cols // 2) + first, LANES)
    copies = []
    for i, layer in enumerate(layers):
        for group in range(groups):
            source = dec_hbm.at[layer, group, :, pl.ds(start, width)]
            sem = sems.at[i * groups + group]
            copies.append(pltpu.make_async_copy(source, part_ref.at[i, group], sem))
            copies[-1].start()
    return copies


def encode_kernel(n, pieces, acts_hbm, w_hbm, dec_hbm, *refs):
    term_refs, part_refs, refs = refs[:n], refs[n:-5], refs[-5:]
    acts_ref, w_ref, part_sems, acts_sems, w_sems = refs
    half = n // 2
    width = w_ref.shape[1] // half
    depth = w_ref.shape[0] // 8
    copies = []
    for i in range(2):
        for j in range(half):
            copies.append(
                pltpu.make_async_copy(
                    acts_hbm.at[j, i], acts_ref.at[i, j], acts_sems.at[i * half + j]
                )
            )
    for i in range(8):
        rows = slice(i * depth, (i + 1) * depth)
        copies.append(pltpu.make_async_copy(w_hbm.at[rows], w_ref.at[rows], w_sems.at[i]))
    for copy in copies:
        copy.start()
    for copy in copies:
        copy.wait()
    copies_part = []
    for i, piece in enumerate(pieces):
        if i == 0:
            piece = ((lax.axis_index("parts"),), *piece[1:])
        copies_part += part_copies(piece, dec_hbm, part_refs[i], part_sems.at[i])
    src = lax.axis_index("src")
    for k in range(n):
        dest = peer(src, k, n)
        rows = acts_ref[lax.rem(dest, 2)]
        rows = rows.reshape(rows.shape[0] * rows.shape[1], rows.shape[2])
        columns = pl.ds(pl.multiple_of((dest // 2) * width, width), width)
        term_refs[k][...] = jnp.dot(
            rows, w_ref[:, columns], preferred_element_type=jnp.float32
        ).astype(jnp.bfloat16)
    for copy in copies_part:
        copy.wait()


def codes_kernel(n, share, tile_rows, active_ref, bias_ref, *refs):
    term_refs, out_ref = refs[:n], refs[n]
    src = lax.axis_index("src")
    tgt = lax.axis_index("tgt")
    parity, half = lax.rem(src, 2), src // 2
    block = out_ref.shape[2] // 2
    pre = term_refs[0][...].astype(jnp.float32)
    for ref in term_refs[1:]:
        pre = pre + ref[...].astype(jnp.float32)
    tiles, slots = active_ref.shape
    for piece in range(2):
        columns = slice(piece * block, (piece + 1) * block)
        bias = bias_ref[pl.ds(half * 2 + piece, 1), :]
        wanted = tgt * n + half * 2 + piece
        flags = []
        for tile in range(tiles):
            flags.append(
                lax.fori_loop(
                    0,
                    slots,
                    lambda i, total: total + (active_ref[tile, i] == wanted).astype(jnp.int32),
                    jnp.int32(0),
                    unroll=slots <= 16,
                )
            )
        for group in range(n // 2):
            tile = ((group * 2 + parity) * share) // tile_rows
            flag = flags[0]
            for i in range(1, tiles):
                flag = jnp.where(tile == i, flags[i], flag)
            live = jnp.where(flag > 0, 1.0, 0.0).astype(jnp.float32)
            rows = slice(group * share, (group + 1) * share)
            value = live * jnp.maximum(pre[rows, columns] + bias, 0.0)
            out_ref[group, :, columns] = value.astype(jnp.bfloat16)


def decode_kernel(n, piece, shared, dec_ref, *refs):
    half = n // 2
    layers, groups, block, cols = dec_ref.shape
    _, first, width = piece
    got_refs, refs = refs[: 1 + shared], refs[1 + shared :]
    code_refs, out_refs, lhs_ref = refs[: 2 * groups], refs[-2 * half - 1 : -1], refs[-1]
    src, tgt = lax.axis_index("src"), lax.axis_index("tgt")
    parity = lax.rem(src, 2)
    share = code_refs[0].shape[1]
    depth = groups * block
    for k in range(groups):
        place = lax.rem(tgt - k + groups, groups)
        for side in range(2):
            latents = parity if side == 0 else 1 - parity
            latents = pl.ds(pl.multiple_of(latents * block, block), block)
            columns = pl.ds(pl.multiple_of((side * groups + place) * block, block), block)
            for j in range(half):
                group = lax.rem(src // 2 + j, half)
                for r in range(2):
                    rows = slice((2 * j + r) * share, (2 * j + r + 1) * share)
                    lhs_ref[rows, columns] = code_refs[2 * k + r][group, :, latents]
    start = pl.multiple_of(lax.axis_index("rep") * (cols // 2) + first, LANES)
    for i in range(layers):
        layer = lax.rem(lax.axis_index("parts") + i, layers) if shared else i
        own = dec_ref[layer, :, :, pl.ds(start, width)].reshape(depth, width)
        got = (got_refs[i][0] if shared else got_refs[0][i]).reshape(depth, width)
        total = jnp.dot(lhs_ref[:, :depth], own, preferred_element_type=jnp.float32)
        total += jnp.dot(lhs_ref[:, depth:], got, preferred_element_type=jnp.float32)
        for j, ref in enumerate(out_refs):
            ref[layer] = total[j * share : (j + 1) * share].astype(ref.dtype)


def add_kernel(n, pieces, bias_ref, target_ref, *refs):
    out_hbm, out_ref, sems = refs[-3:]
    half = n // 2
    cols = target_ref.shape[2]
    rep = lax.axis_index("rep")
    copies = []
    for i, (layers, first, width) in enumerate(pieces):
        for side in range(2):
            core = rep if side == 0 else 1 - rep
            columns = pl.ds(pl.multiple_of(core * (cols // 2) + first, LANES), width)
            mine = refs[(2 * i + side) * half : (2 * i + side + 1) * half]
            for j, layer in enumerate(layers):
                total = bias_ref[layer : layer + 1, columns]
                total = total - target_ref[layer, :, columns].astype(jnp.float32)
                for ref in mine:
                    total = total + ref[j].astype(jnp.float32)
                out_ref[layer, :, columns] = total.astype(jnp.bfloat16)
                copies.append(
                    pltpu.make_async_copy(
                        out_ref.at[layer, :, columns],
                        out_hbm.at[layer, :, columns],
                        sems.at[len(copies)],
                    )
                )
                copies[-1].start()
    for copy in copies:
        copy.wait()


def body(acts, enc_w, enc_b, dec_w, dec_b, targets, active):
    n = lax.axis_size("src")
    rows, features = acts.shape
    layers, groups, block, cols = dec_w.shape
    share = rows // n
    half = n // 2
    pieces = cut_pieces(layers, cols // 2)
    tile_rows = rows // active.shape[0]
    pair = [(i, i ^ 1) for i in range(n)]
    params = pltpu.CompilerParams(vmem_limit_bytes=VMEM_BYTES)
    vmem = pl.BlockSpec(memory_space=pltpu.VMEM)
    smem = pl.BlockSpec(memory_space=pltpu.SMEM)
    anywhere = pl.BlockSpec(memory_space=pl.ANY)
    cost = pl.CostEstimate(flops=0, bytes_accessed=0, transcendentals=0)

    dec_rows = dec_w
    acts, enc_w, dec_w = (
        pltpu.with_memory_space_constraint(value, pltpu.HBM)
        for value in (acts.reshape(half, 2, share, features), enc_w, dec_w)
    )

    def shape(*extent, kind=jnp.bfloat16):
        return jax.ShapeDtypeStruct(extent, kind)

    results = pl.pallas_call(
        functools.partial(encode_kernel, n, pieces),
        out_shape=[shape(half * share, 2 * block)] * n
        + [
            shape(1 if i == 0 else layers, groups, block, width)
            for i, (_, _, width) in enumerate(pieces)
        ],
        in_specs=[anywhere] * 3,
        out_specs=[vmem] * (n + len(pieces)),
        scratch_shapes=[
            pltpu.VMEM((2, half, share, features), jnp.bfloat16),
            pltpu.VMEM(enc_w.shape, jnp.bfloat16),
            pltpu.SemaphoreType.DMA((len(pieces), layers * groups)),
            pltpu.SemaphoreType.DMA((2 * half,)),
            pltpu.SemaphoreType.DMA((8,)),
        ],
        compiler_params=params,
        cost_estimate=cost,
        name="encode",
    )(acts, enc_w, dec_w)
    terms, parts = list(results[:n]), list(results[n:])
    for k in range(1, n):
        terms[k] = lax.ppermute(terms[k], "src", [(i, peer(i, k, n)) for i in range(n)])
    own = pl.pallas_call(
        functools.partial(codes_kernel, n, share, tile_rows),
        out_shape=shape(half, share, 2 * block),
        in_specs=[smem] + [vmem] * (1 + n),
        out_specs=vmem,
        compiler_params=params,
        cost_estimate=cost,
        name="codes",
    )(active, enc_b.reshape(n, block), *terms)
    codes = []
    for k in range(groups):
        for r in range(2):
            perm = [
                (i * 2 + c, (i + k) % groups * 2 + (c ^ r)) for i in range(groups) for c in range(2)
            ]
            codes.append(lax.ppermute(own, ("tgt", "rep"), perm) if k + r else own)

    def hold(value, after):
        return pl.pallas_call(
            lambda *refs: None,
            out_shape=jax.ShapeDtypeStruct(value.shape, value.dtype),
            in_specs=[anywhere] * 2,
            out_specs=anywhere,
            input_output_aliases={0: 0},
            compiler_params=params,
            cost_estimate=cost,
            name="hold",
        )(value, after)

    got = [[lax.ppermute(parts[0], "src", pair)]]
    got[0].append(lax.ppermute(got[0][0], "parts", [(0, 1), (1, 0)]))
    if len(pieces) > 1:
        got.append([lax.ppermute(hold(parts[1], codes[1]), "src", pair)])
    def add(some, begun):
        operands = [value for i in some for value in sums[i]]
        return pl.pallas_call(
            functools.partial(add_kernel, n, [pieces[i] for i in some]),
            out_shape=shape(layers, share, cols),
            in_specs=[vmem] * (2 + len(operands)) + [anywhere] * len(begun),
            out_specs=anywhere,
            scratch_shapes=[
                pltpu.VMEM((layers, share, cols), jnp.bfloat16),
                pltpu.SemaphoreType.DMA((2 * len(some) * layers,)),
            ],
            input_output_aliases={2 + len(operands): 0} if begun else {},
            compiler_params=params,
            cost_estimate=cost,
            name="add",
        )(dec_b, targets, *operands, *begun)

    sums, after, begun = [], [], []
    for i, (_, _, width) in enumerate(pieces):
        if i == 2:
            begun = [add([0], [])]
            after.append(begun[0])
        shapes = [shape(layers, share, width)] * (2 * half)
        shapes[0] = shape(layers, share, width, kind=jnp.float32)
        terms = pl.pallas_call(
            functools.partial(decode_kernel, n, pieces[i], i == 0),
            out_shape=shapes,
            in_specs=[vmem] * (1 + len(got[i]) + 2 * groups) + [anywhere] * len(after),
            out_specs=[vmem] * len(shapes),
            scratch_shapes=[pltpu.VMEM((rows, 2 * groups * block), jnp.bfloat16)],
            compiler_params=params,
            cost_estimate=cost,
            name="decode",
        )(dec_rows, *got[i], *codes, *after)
        after = [terms[0]]
        if i == 0:
            for part in parts[2:]:
                got.append([lax.ppermute(hold(part, own), "src", pair)])
        sums.append([])
        for r in range(2):
            for j in range(half):
                perm = [
                    (d * 2 + c, (d + 2 * j) % n * 2 + (c ^ r)) for d in range(n) for c in range(2)
                ]
                term = terms[2 * j + r]
                sums[i].append(lax.ppermute(term, ("src", "rep"), perm) if j + r else term)

    return add(list(range(len(begun), len(pieces))), begun)


def solution(mesh):
    in_specs = (
        P(("parts", "rep"), "src"),
        P("src", "tgt"),
        P("tgt"),
        P(None, None, "src", "tgt"),
        P(None, "tgt"),
        P(None, ("parts", "rep", "src"), "tgt"),
        P(("parts", "rep"), None),
    )
    out_specs = P(None, ("parts", "rep", "src"), "tgt")
    return jax.shard_map(body, mesh=mesh, in_specs=in_specs, out_specs=out_specs, check_vma=False)
```

```python
import functools

import jax
import jax.numpy as jnp
from jax import lax
from jax.experimental import pallas as pl
from jax.experimental.pallas import tpu as pltpu
from jax.sharding import PartitionSpec as P

VMEM_BYTES = 32 * 1024 * 1024
LANES = 128
SHARES = (4, 4)


def cut_pieces(layers, columns):
    tiles = columns // LANES
    pieces, start = [], 0
    for i, eighths in enumerate(SHARES):
        stop = tiles if i + 1 == len(SHARES) else min(tiles, start + -(-tiles * eighths // 8))
        if stop > start:
            pieces.append((tuple(range(layers)), start * LANES, (stop - start) * LANES))
        start = stop
    return pieces


def peer(index, k, n):
    return index ^ k if n & (n - 1) == 0 else (index + k) % n


def part_copies(piece, dec_hbm, part_ref, sems):
    layers, first, width = piece
    groups, cols = dec_hbm.shape[1], dec_hbm.shape[3]
    start = pl.multiple_of(lax.axis_index("rep") * (cols // 2) + first, LANES)
    copies = []
    for i, layer in enumerate(layers):
        for group in range(groups):
            source = dec_hbm.at[layer, group, :, pl.ds(start, width)]
            sem = sems.at[i * groups + group]
            copies.append(pltpu.make_async_copy(source, part_ref.at[i, group], sem))
            copies[-1].start()
    return copies


def encode_kernel(n, pieces, acts_hbm, w_hbm, dec_hbm, *refs):
    term_refs, part_refs, refs = refs[:n], refs[n:-5], refs[-5:]
    acts_ref, w_ref, part_sems, acts_sems, w_sems = refs
    half = n // 2
    width = w_ref.shape[1] // half
    depth = w_ref.shape[0] // 8
    copies = []
    for i in range(2):
        for j in range(half):
            copies.append(
                pltpu.make_async_copy(
                    acts_hbm.at[j, i], acts_ref.at[i, j], acts_sems.at[i * half + j]
                )
            )
    for i in range(8):
        rows = slice(i * depth, (i + 1) * depth)
        copies.append(pltpu.make_async_copy(w_hbm.at[rows], w_ref.at[rows], w_sems.at[i]))
    for copy in copies:
        copy.start()
    for copy in copies:
        copy.wait()
    copies_part = []
    for i, piece in enumerate(pieces):
        if i == 0:
            piece = ((lax.axis_index("parts"),), *piece[1:])
        copies_part += part_copies(piece, dec_hbm, part_refs[i], part_sems.at[i])
    src = lax.axis_index("src")
    for k in range(n):
        dest = peer(src, k, n)
        rows = acts_ref[lax.rem(dest, 2)]
        rows = rows.reshape(rows.shape[0] * rows.shape[1], rows.shape[2])
        columns = pl.ds(pl.multiple_of((dest // 2) * width, width), width)
        term_refs[k][...] = jnp.dot(
            rows, w_ref[:, columns], preferred_element_type=jnp.float32
        ).astype(jnp.bfloat16)
    for copy in copies_part:
        copy.wait()


def codes_kernel(n, share, tile_rows, active_ref, bias_ref, *refs):
    term_refs, out_ref = refs[:n], refs[n]
    src = lax.axis_index("src")
    tgt = lax.axis_index("tgt")
    parity, half = lax.rem(src, 2), src // 2
    block = out_ref.shape[2] // 2
    pre = term_refs[0][...].astype(jnp.float32)
    for ref in term_refs[1:]:
        pre = pre + ref[...].astype(jnp.float32)
    tiles, slots = active_ref.shape
    for piece in range(2):
        columns = slice(piece * block, (piece + 1) * block)
        bias = bias_ref[pl.ds(half * 2 + piece, 1), :]
        wanted = tgt * n + half * 2 + piece
        flags = []
        for tile in range(tiles):
            flags.append(
                lax.fori_loop(
                    0,
                    slots,
                    lambda i, total: total + (active_ref[tile, i] == wanted).astype(jnp.int32),
                    jnp.int32(0),
                    unroll=slots <= 16,
                )
            )
        for group in range(n // 2):
            tile = ((group * 2 + parity) * share) // tile_rows
            flag = flags[0]
            for i in range(1, tiles):
                flag = jnp.where(tile == i, flags[i], flag)
            live = jnp.where(flag > 0, 1.0, 0.0).astype(jnp.float32)
            rows = slice(group * share, (group + 1) * share)
            value = live * jnp.maximum(pre[rows, columns] + bias, 0.0)
            out_ref[group, :, columns] = value.astype(jnp.bfloat16)


def decode_kernel(n, piece, shared, dec_ref, *refs):
    half = n // 2
    layers, groups, block, cols = dec_ref.shape
    _, first, width = piece
    got_refs, refs = refs[: 1 + shared], refs[1 + shared :]
    code_refs, out_refs, lhs_ref = refs[: 2 * groups], refs[-2 * half - 1 : -1], refs[-1]
    src, tgt = lax.axis_index("src"), lax.axis_index("tgt")
    parity = lax.rem(src, 2)
    share = code_refs[0].shape[1]
    depth = groups * block
    for k in range(groups):
        place = lax.rem(tgt - k + groups, groups)
        for side in range(2):
            latents = parity if side == 0 else 1 - parity
            latents = pl.ds(pl.multiple_of(latents * block, block), block)
            columns = pl.ds(pl.multiple_of((side * groups + place) * block, block), block)
            for j in range(half):
                group = lax.rem(src // 2 + j, half)
                for r in range(2):
                    rows = slice((2 * j + r) * share, (2 * j + r + 1) * share)
                    lhs_ref[rows, columns] = code_refs[2 * k + r][group, :, latents]
    start = pl.multiple_of(lax.axis_index("rep") * (cols // 2) + first, LANES)
    for i in range(layers):
        layer = lax.rem(lax.axis_index("parts") + i, layers) if shared else i
        own = dec_ref[layer, :, :, pl.ds(start, width)].reshape(depth, width)
        got = (got_refs[i][0] if shared else got_refs[0][i]).reshape(depth, width)
        total = jnp.dot(lhs_ref[:, :depth], own, preferred_element_type=jnp.float32)
        total += jnp.dot(lhs_ref[:, depth:], got, preferred_element_type=jnp.float32)
        for j, ref in enumerate(out_refs):
            ref[layer] = total[j * share : (j + 1) * share].astype(ref.dtype)


def add_kernel(n, pieces, bias_ref, target_ref, *refs):
    out_hbm, out_ref, sems = refs[-3:]
    half = n // 2
    cols = target_ref.shape[2]
    rep = lax.axis_index("rep")
    copies = []
    for i, (layers, first, width) in enumerate(pieces):
        for side in range(2):
            core = rep if side == 0 else 1 - rep
            columns = pl.ds(pl.multiple_of(core * (cols // 2) + first, LANES), width)
            mine = refs[(2 * i + side) * half : (2 * i + side + 1) * half]
            for j, layer in enumerate(layers):
                total = bias_ref[layer : layer + 1, columns]
                total = total - target_ref[layer, :, columns].astype(jnp.float32)
                for ref in mine:
                    total = total + ref[j].astype(jnp.float32)
                out_ref[layer, :, columns] = total.astype(jnp.bfloat16)
                copies.append(
                    pltpu.make_async_copy(
                        out_ref.at[layer, :, columns],
                        out_hbm.at[layer, :, columns],
                        sems.at[len(copies)],
                    )
                )
                copies[-1].start()
    for copy in copies:
        copy.wait()


def body(acts, enc_w, enc_b, dec_w, dec_b, targets, active):
    n = lax.axis_size("src")
    rows, features = acts.shape
    layers, groups, block, cols = dec_w.shape
    share = rows // n
    half = n // 2
    pieces = cut_pieces(layers, cols // 2)
    tile_rows = rows // active.shape[0]
    pair = [(i, i ^ 1) for i in range(n)]
    params = pltpu.CompilerParams(vmem_limit_bytes=VMEM_BYTES)
    vmem = pl.BlockSpec(memory_space=pltpu.VMEM)
    smem = pl.BlockSpec(memory_space=pltpu.SMEM)
    anywhere = pl.BlockSpec(memory_space=pl.ANY)
    cost = pl.CostEstimate(flops=0, bytes_accessed=0, transcendentals=0)

    dec_rows = dec_w
    acts, enc_w, dec_w = (
        pltpu.with_memory_space_constraint(value, pltpu.HBM)
        for value in (acts.reshape(half, 2, share, features), enc_w, dec_w)
    )

    def shape(*extent, kind=jnp.bfloat16):
        return jax.ShapeDtypeStruct(extent, kind)

    results = pl.pallas_call(
        functools.partial(encode_kernel, n, pieces),
        out_shape=[shape(half * share, 2 * block)] * n
        + [
            shape(1 if i == 0 else layers, groups, block, width)
            for i, (_, _, width) in enumerate(pieces)
        ],
        in_specs=[anywhere] * 3,
        out_specs=[vmem] * (n + len(pieces)),
        scratch_shapes=[
            pltpu.VMEM((2, half, share, features), jnp.bfloat16),
            pltpu.VMEM(enc_w.shape, jnp.bfloat16),
            pltpu.SemaphoreType.DMA((len(pieces), layers * groups)),
            pltpu.SemaphoreType.DMA((2 * half,)),
            pltpu.SemaphoreType.DMA((8,)),
        ],
        compiler_params=params,
        cost_estimate=cost,
        name="encode",
    )(acts, enc_w, dec_w)
    terms, parts = list(results[:n]), list(results[n:])
    for k in range(1, n):
        terms[k] = lax.ppermute(terms[k], "src", [(i, peer(i, k, n)) for i in range(n)])
    own = pl.pallas_call(
        functools.partial(codes_kernel, n, share, tile_rows),
        out_shape=shape(half, share, 2 * block),
        in_specs=[smem] + [vmem] * (1 + n),
        out_specs=vmem,
        compiler_params=params,
        cost_estimate=cost,
        name="codes",
    )(active, enc_b.reshape(n, block), terms[0], *reversed(terms[1:]))
    codes = []
    for k in range(groups):
        for r in range(2):
            perm = [
                (i * 2 + c, (i + k) % groups * 2 + (c ^ r)) for i in range(groups) for c in range(2)
            ]
            codes.append(lax.ppermute(own, ("tgt", "rep"), perm) if k + r else own)

    def hold(value, after):
        return pl.pallas_call(
            lambda *refs: None,
            out_shape=jax.ShapeDtypeStruct(value.shape, value.dtype),
            in_specs=[anywhere] * 2,
            out_specs=anywhere,
            input_output_aliases={0: 0},
            compiler_params=params,
            cost_estimate=cost,
            name="hold",
        )(value, after)

    got = [[lax.ppermute(parts[0], "src", pair)]]
    got[0].append(lax.ppermute(got[0][0], "parts", [(0, 1), (1, 0)]))
    if len(pieces) > 1:
        got.append([lax.ppermute(hold(parts[1], codes[1]), "src", pair)])
    def add(some, begun):
        operands = [value for i in some for value in sums[i]]
        return pl.pallas_call(
            functools.partial(add_kernel, n, [pieces[i] for i in some]),
            out_shape=shape(layers, share, cols),
            in_specs=[vmem] * (2 + len(operands)) + [anywhere] * len(begun),
            out_specs=anywhere,
            scratch_shapes=[
                pltpu.VMEM((layers, share, cols), jnp.bfloat16),
                pltpu.SemaphoreType.DMA((2 * len(some) * layers,)),
            ],
            input_output_aliases={2 + len(operands): 0} if begun else {},
            compiler_params=params,
            cost_estimate=cost,
            name="add",
        )(dec_b, targets, *operands, *begun)

    sums, after, begun = [], [], []
    for i, (_, _, width) in enumerate(pieces):
        if i == 2:
            begun = [add([0], [])]
            after.append(begun[0])
        shapes = [shape(layers, share, width)] * (2 * half)
        shapes[0] = shape(layers, share, width, kind=jnp.float32)
        terms = pl.pallas_call(
            functools.partial(decode_kernel, n, pieces[i], i == 0),
            out_shape=shapes,
            in_specs=[vmem] * (1 + len(got[i]) + 2 * groups) + [anywhere] * len(after),
            out_specs=[vmem] * len(shapes),
            scratch_shapes=[pltpu.VMEM((rows, 2 * groups * block), jnp.bfloat16)],
            compiler_params=params,
            cost_estimate=cost,
            name="decode",
        )(dec_rows, *got[i], *codes, *after)
        after = [terms[0]]
        if i == 0:
            for part in parts[2:]:
                got.append([lax.ppermute(hold(part, own), "src", pair)])
        sums.append([])
        for r in range(2):
            for j in range(half):
                perm = [
                    (d * 2 + c, (d + 2 * j) % n * 2 + (c ^ r)) for d in range(n) for c in range(2)
                ]
                term = terms[2 * j + r]
                sums[i].append(lax.ppermute(term, ("src", "rep"), perm) if j + r else term)

    return add(list(range(len(begun), len(pieces))), begun)


def solution(mesh):
    in_specs = (
        P(("parts", "rep"), "src"),
        P("src", "tgt"),
        P("tgt"),
        P(None, None, "src", "tgt"),
        P(None, "tgt"),
        P(None, ("parts", "rep", "src"), "tgt"),
        P(("parts", "rep"), None),
    )
    out_specs = P(None, ("parts", "rep", "src"), "tgt")
    return jax.shard_map(body, mesh=mesh, in_specs=in_specs, out_specs=out_specs, check_vma=False)
```

```python
import functools

import jax
import jax.numpy as jnp
from jax import lax
from jax.experimental import pallas as pl
from jax.experimental.pallas import tpu as pltpu
from jax.sharding import PartitionSpec as P

VMEM_BYTES = 32 * 1024 * 1024
LANES = 128
PIECES = ((0, 0, False), (0, 1, False), (1, 0, True), (1, 1, False))


def cut_pieces(columns):
    tiles = columns // LANES
    middle = -(-tiles // 2) * LANES
    bounds = ((0, middle), (middle, columns))
    return [
        (offset, bounds[side][0], bounds[side][1] - bounds[side][0], across)
        for offset, side, across in PIECES
    ]


def layer_of(piece, layers):
    return lax.rem(lax.axis_index("parts") + piece[0], layers)


def peer(index, k, n):
    return index ^ k if n & (n - 1) == 0 else (index + k) % n


def part_copies(piece, dec_hbm, part_ref, sems):
    layers, groups, _, cols = dec_hbm.shape
    start = pl.multiple_of(lax.axis_index("rep") * (cols // 2) + piece[1], LANES)
    layer = layer_of(piece, layers)
    copies = []
    for group in range(groups):
        source = dec_hbm.at[layer, group, :, pl.ds(start, piece[2])]
        copies.append(pltpu.make_async_copy(source, part_ref.at[group], sems.at[group]))
        copies[-1].start()
    return copies


def encode_kernel(n, pieces, acts_hbm, w_hbm, dec_hbm, *refs):
    term_refs, part_refs, refs = refs[:n], refs[n:-5], refs[-5:]
    acts_ref, w_ref, part_sems, acts_sems, w_sems = refs
    half = n // 2
    width = w_ref.shape[1] // half
    depth = w_ref.shape[0] // 8
    copies = []
    for i in range(2):
        for j in range(half):
            copies.append(
                pltpu.make_async_copy(
                    acts_hbm.at[j, i], acts_ref.at[i, j], acts_sems.at[i * half + j]
                )
            )
    for i in range(8):
        rows = slice(i * depth, (i + 1) * depth)
        copies.append(pltpu.make_async_copy(w_hbm.at[rows], w_ref.at[rows], w_sems.at[i]))
    for copy in copies:
        copy.start()
    for copy in copies:
        copy.wait()
    copies_part = []
    for i, ref in enumerate(part_refs):
        copies_part += part_copies(pieces[i], dec_hbm, ref, part_sems.at[i])
    src = lax.axis_index("src")
    for k in range(n):
        dest = peer(src, k, n)
        rows = acts_ref[lax.rem(dest, 2)]
        rows = rows.reshape(rows.shape[0] * rows.shape[1], rows.shape[2])
        columns = pl.ds(pl.multiple_of((dest // 2) * width, width), width)
        term_refs[k][...] = jnp.dot(
            rows, w_ref[:, columns], preferred_element_type=jnp.float32
        ).astype(jnp.bfloat16)
    for copy in copies_part:
        copy.wait()


def codes_kernel(n, share, tile_rows, active_ref, bias_ref, *refs):
    term_refs, out_ref = refs[:n], refs[n]
    src = lax.axis_index("src")
    tgt = lax.axis_index("tgt")
    parity, half = lax.rem(src, 2), src // 2
    block = out_ref.shape[2] // 2
    pre = term_refs[0][...].astype(jnp.float32)
    for ref in term_refs[1:]:
        pre = pre + ref[...].astype(jnp.float32)
    tiles, slots = active_ref.shape
    for piece in range(2):
        columns = slice(piece * block, (piece + 1) * block)
        bias = bias_ref[pl.ds(half * 2 + piece, 1), :]
        wanted = tgt * n + half * 2 + piece
        flags = []
        for tile in range(tiles):
            flags.append(
                lax.fori_loop(
                    0,
                    slots,
                    lambda i, total: total + (active_ref[tile, i] == wanted).astype(jnp.int32),
                    jnp.int32(0),
                    unroll=slots <= 16,
                )
            )
        for group in range(n // 2):
            tile = ((group * 2 + parity) * share) // tile_rows
            flag = flags[0]
            for i in range(1, tiles):
                flag = jnp.where(tile == i, flags[i], flag)
            live = jnp.where(flag > 0, 1.0, 0.0).astype(jnp.float32)
            rows = slice(group * share, (group + 1) * share)
            value = live * jnp.maximum(pre[rows, columns] + bias, 0.0)
            out_ref[group, :, columns] = value.astype(jnp.bfloat16)


def decode_kernel(n, piece, dec_ref, got_ref, codes_ref, *refs):
    half = n // 2
    layers, groups, block, cols = dec_ref.shape
    _, first, width, _ = piece
    out_refs, lhs_ref = refs[-2 * half - 1 : -1], refs[-1]
    src, rep = lax.axis_index("src"), lax.axis_index("rep")
    parity = lax.rem(src, 2)
    share = codes_ref.shape[2]
    depth = groups * block
    for place in range(groups):
        for r in range(2):
            origin = place * 2 + lax.rem(rep + r, 2)
            for side in range(2):
                latents = parity if side == 0 else 1 - parity
                latents = pl.ds(pl.multiple_of(latents * block, block), block)
                columns = slice((side * groups + place) * block, (side * groups + place + 1) * block)
                for j in range(half):
                    group = lax.rem(src // 2 + j, half)
                    rows = slice((2 * j + r) * share, (2 * j + r + 1) * share)
                    lhs_ref[rows, columns] = codes_ref[origin, group, :, latents]
    start = pl.multiple_of(rep * (cols // 2) + first, LANES)
    own = dec_ref[layer_of(piece, layers), :, :, pl.ds(start, width)].reshape(depth, width)
    got = got_ref[...].reshape(depth, width)
    total = jnp.dot(lhs_ref[:, :depth], own, preferred_element_type=jnp.float32)
    total += jnp.dot(lhs_ref[:, depth:], got, preferred_element_type=jnp.float32)
    for i, ref in enumerate(out_refs):
        ref[...] = total[i * share : (i + 1) * share].astype(ref.dtype)


def add_kernel(n, pieces, bias_ref, target_ref, *refs):
    out_hbm, out_ref, sems = refs[-3:]
    half = n // 2
    layers, _, cols = target_ref.shape
    rep = lax.axis_index("rep")
    copies = []
    for i, piece in enumerate(pieces):
        _, first, width, _ = piece
        layer = layer_of(piece, layers)
        for side in range(2):
            core = rep if side == 0 else 1 - rep
            columns = pl.ds(pl.multiple_of(core * (cols // 2) + first, LANES), width)
            total = bias_ref[0:1, columns]
            for other in range(1, layers):
                total = jnp.where(layer == other, bias_ref[other : other + 1, columns], total)
            total = total - target_ref[layer, :, columns].astype(jnp.float32)
            for ref in refs[(2 * i + side) * half : (2 * i + side + 1) * half]:
                total = total + ref[...].astype(jnp.float32)
            place = 2 * i + side
            out_ref[place, :, :width] = total.astype(jnp.bfloat16)
            copies.append(
                pltpu.make_async_copy(
                    out_ref.at[place, :, :width], out_hbm.at[layer, :, columns], sems.at[place]
                )
            )
            copies[-1].start()
    for copy in copies:
        copy.wait()


def body(acts, enc_w, enc_b, dec_w, dec_b, targets, active):
    n = lax.axis_size("src")
    rows, features = acts.shape
    layers, groups, block, cols = dec_w.shape
    share = rows // n
    half = n // 2
    pieces = cut_pieces(cols // 2)
    fetched = [piece for piece in pieces if not piece[3]]
    tile_rows = rows // active.shape[0]
    pair = [(i, i ^ 1) for i in range(n)]
    params = pltpu.CompilerParams(vmem_limit_bytes=VMEM_BYTES)
    vmem = pl.BlockSpec(memory_space=pltpu.VMEM)
    smem = pl.BlockSpec(memory_space=pltpu.SMEM)
    anywhere = pl.BlockSpec(memory_space=pl.ANY)
    cost = pl.CostEstimate(flops=0, bytes_accessed=0, transcendentals=0)

    dec_rows = dec_w
    acts, enc_w, dec_w = (
        pltpu.with_memory_space_constraint(value, pltpu.HBM)
        for value in (acts.reshape(half, 2, share, features), enc_w, dec_w)
    )

    def shape(*extent, kind=jnp.bfloat16):
        return jax.ShapeDtypeStruct(extent, kind)

    results = pl.pallas_call(
        functools.partial(encode_kernel, n, fetched),
        out_shape=[shape(half * share, 2 * block)] * n
        + [shape(groups, block, piece[2]) for piece in fetched],
        in_specs=[anywhere] * 3,
        out_specs=[vmem] * (n + len(fetched)),
        scratch_shapes=[
            pltpu.VMEM((2, half, share, features), jnp.bfloat16),
            pltpu.VMEM(enc_w.shape, jnp.bfloat16),
            pltpu.SemaphoreType.DMA((len(fetched), groups)),
            pltpu.SemaphoreType.DMA((2 * half,)),
            pltpu.SemaphoreType.DMA((8,)),
        ],
        compiler_params=params,
        cost_estimate=cost,
        name="encode",
    )(acts, enc_w, dec_w)
    terms, parts = list(results[:n]), list(results[n:])
    for k in range(1, n):
        terms[k] = lax.ppermute(terms[k], "src", [(i, peer(i, k, n)) for i in range(n)])
    own = pl.pallas_call(
        functools.partial(codes_kernel, n, share, tile_rows),
        out_shape=shape(half, share, 2 * block),
        in_specs=[smem] + [vmem] * (1 + n),
        out_specs=vmem,
        compiler_params=params,
        cost_estimate=cost,
        name="codes",
    )(active, enc_b.reshape(n, block), *terms)
    codes = lax.all_gather(own, ("tgt", "rep"), axis=0, tiled=False)

    def hold(value, after):
        return pl.pallas_call(
            lambda *refs: None,
            out_shape=jax.ShapeDtypeStruct(value.shape, value.dtype),
            in_specs=[anywhere] * 2,
            out_specs=anywhere,
            input_output_aliases={0: 0},
            compiler_params=params,
            cost_estimate=cost,
            name="hold",
        )(value, after)

    got = []
    for i, piece in enumerate(pieces):
        if piece[3]:
            first = next(j for j in range(i) if pieces[j][1] == piece[1])
            value = hold(got[first], codes)
            got.append(lax.ppermute(value, "parts", [(0, 1), (1, 0)]))
        else:
            value = parts.pop(0)
            if i > 0:
                value = hold(value, own)
            got.append(lax.ppermute(value, "src", pair))

    def add(some, begun):
        operands = [value for i in some for value in sums[i]]
        widest = max(piece[2] for piece in pieces)
        return pl.pallas_call(
            functools.partial(add_kernel, n, [pieces[i] for i in some]),
            out_shape=shape(layers, share, cols),
            in_specs=[vmem] * (2 + len(operands)) + [anywhere] * len(begun),
            out_specs=anywhere,
            scratch_shapes=[
                pltpu.VMEM((2 * len(some), share, widest), jnp.bfloat16),
                pltpu.SemaphoreType.DMA((2 * len(some),)),
            ],
            input_output_aliases={2 + len(operands): 0} if begun else {},
            compiler_params=params,
            cost_estimate=cost,
            name="add",
        )(dec_b, targets, *operands, *begun)

    sums, after, begun = [], [], []
    for i, piece in enumerate(pieces):
        if i == 3:
            begun = [add(list(range(2)), [])]
            after.append(begun[0])
        shapes = [shape(share, piece[2])] * (2 * half)
        shapes[0] = shape(share, piece[2], kind=jnp.float32)
        terms = pl.pallas_call(
            functools.partial(decode_kernel, n, piece),
            out_shape=shapes,
            in_specs=[vmem] * 3 + [anywhere] * len(after),
            out_specs=[vmem] * len(shapes),
            scratch_shapes=[pltpu.VMEM((rows, 2 * groups * block), jnp.bfloat16)],
            compiler_params=params,
            cost_estimate=cost,
            name="decode",
        )(dec_rows, got[i], codes, *after)
        after = [terms[0]]
        sums.append([None] * (2 * half))
        for j in [*range(1, half), 0]:
            for r in range(2):
                perm = [
                    (d * 2 + c, (d + 2 * j) % n * 2 + (c ^ r)) for d in range(n) for c in range(2)
                ]
                term = terms[2 * j + r]
                sums[i][r * half + j] = (
                    lax.ppermute(term, ("src", "rep"), perm) if j + r else term
                )

    return add(list(range(2, len(pieces))), begun)


def solution(mesh):
    in_specs = (
        P(("parts", "rep"), "src"),
        P("src", "tgt"),
        P("tgt"),
        P(None, None, "src", "tgt"),
        P(None, "tgt"),
        P(None, ("parts", "rep", "src"), "tgt"),
        P(("parts", "rep"), None),
    )
    out_specs = P(None, ("parts", "rep", "src"), "tgt")
    return jax.shard_map(body, mesh=mesh, in_specs=in_specs, out_specs=out_specs, check_vma=False)
```

```python
import functools

import jax
import jax.numpy as jnp
from jax import lax
from jax.experimental import pallas as pl
from jax.experimental.pallas import tpu as pltpu
from jax.sharding import PartitionSpec as P

VMEM_BYTES = 32 * 1024 * 1024
LANES = 128
SHARES = (3, 5)


def cut_pieces(layers, columns):
    tiles = columns // LANES
    pieces, start = [], 0
    for i, eighths in enumerate(SHARES):
        stop = tiles if i + 1 == len(SHARES) else min(tiles, start + -(-tiles * eighths // 8))
        if stop > start:
            pieces.append((tuple(range(layers)), start * LANES, (stop - start) * LANES))
        start = stop
    return pieces


def peer(index, k, n):
    return index ^ k if n & (n - 1) == 0 else (index + k) % n


def part_copies(piece, dec_hbm, part_ref, sems):
    layers, first, width = piece
    groups, cols = dec_hbm.shape[1], dec_hbm.shape[3]
    start = pl.multiple_of(lax.axis_index("rep") * (cols // 2) + first, LANES)
    copies = []
    for i, layer in enumerate(layers):
        for group in range(groups):
            source = dec_hbm.at[layer, group, :, pl.ds(start, width)]
            sem = sems.at[i * groups + group]
            copies.append(pltpu.make_async_copy(source, part_ref.at[i, group], sem))
            copies[-1].start()
    return copies


def encode_kernel(n, pieces, acts_hbm, w_hbm, dec_hbm, *refs):
    term_refs, part_refs, refs = refs[:n], refs[n:-5], refs[-5:]
    acts_ref, w_ref, part_sems, acts_sems, w_sems = refs
    half = n // 2
    width = w_ref.shape[1] // half
    depth = w_ref.shape[0] // 8
    copies = []
    for i in range(2):
        for j in range(half):
            copies.append(
                pltpu.make_async_copy(
                    acts_hbm.at[j, i], acts_ref.at[i, j], acts_sems.at[i * half + j]
                )
            )
    for i in range(8):
        rows = slice(i * depth, (i + 1) * depth)
        copies.append(pltpu.make_async_copy(w_hbm.at[rows], w_ref.at[rows], w_sems.at[i]))
    for copy in copies:
        copy.start()
    for copy in copies:
        copy.wait()
    copies_part = []
    for i, piece in enumerate(pieces):
        if i == 0:
            piece = ((lax.axis_index("parts"),), *piece[1:])
        copies_part += part_copies(piece, dec_hbm, part_refs[i], part_sems.at[i])
    src = lax.axis_index("src")
    for k in range(n):
        dest = peer(src, k, n)
        rows = acts_ref[lax.rem(dest, 2)]
        rows = rows.reshape(rows.shape[0] * rows.shape[1], rows.shape[2])
        columns = pl.ds(pl.multiple_of((dest // 2) * width, width), width)
        term_refs[k][...] = jnp.dot(
            rows, w_ref[:, columns], preferred_element_type=jnp.float32
        ).astype(jnp.bfloat16)
    for copy in copies_part:
        copy.wait()


def codes_kernel(n, share, tile_rows, active_ref, bias_ref, *refs):
    term_refs, out_ref = refs[:n], refs[n]
    src = lax.axis_index("src")
    tgt = lax.axis_index("tgt")
    parity, half = lax.rem(src, 2), src // 2
    block = out_ref.shape[2] // 2
    pre = term_refs[0][...].astype(jnp.float32)
    for ref in term_refs[1:]:
        pre = pre + ref[...].astype(jnp.float32)
    tiles, slots = active_ref.shape
    for piece in range(2):
        columns = slice(piece * block, (piece + 1) * block)
        bias = bias_ref[pl.ds(half * 2 + piece, 1), :]
        wanted = tgt * n + half * 2 + piece
        flags = []
        for tile in range(tiles):
            flags.append(
                lax.fori_loop(
                    0,
                    slots,
                    lambda i, total: total + (active_ref[tile, i] == wanted).astype(jnp.int32),
                    jnp.int32(0),
                    unroll=slots <= 16,
                )
            )
        for group in range(n // 2):
            tile = ((group * 2 + parity) * share) // tile_rows
            flag = flags[0]
            for i in range(1, tiles):
                flag = jnp.where(tile == i, flags[i], flag)
            live = jnp.where(flag > 0, 1.0, 0.0).astype(jnp.float32)
            rows = slice(group * share, (group + 1) * share)
            value = live * jnp.maximum(pre[rows, columns] + bias, 0.0)
            out_ref[group, :, columns] = value.astype(jnp.bfloat16)


def gather_kernel(n, *refs):
    half = n // 2
    code_refs, out_ref = refs[:-1], refs[-1]
    groups = len(code_refs) // 2
    src, tgt = lax.axis_index("src"), lax.axis_index("tgt")
    parity = lax.rem(src, 2)
    share, block = code_refs[0].shape[1], code_refs[0].shape[2] // 2
    for k in range(groups):
        place = lax.rem(tgt - k + groups, groups)
        for side in range(2):
            latents = parity if side == 0 else 1 - parity
            latents = pl.ds(pl.multiple_of(latents * block, block), block)
            columns = pl.ds(pl.multiple_of((side * groups + place) * block, block), block)
            for j in range(half):
                group = lax.rem(src // 2 + j, half)
                for r in range(2):
                    rows = slice((2 * j + r) * share, (2 * j + r + 1) * share)
                    out_ref[rows, columns] = code_refs[2 * k + r][group, :, latents]


def decode_kernel(n, piece, shared, dec_ref, lhs_ref, *refs):
    layers, groups, block, cols = dec_ref.shape
    _, first, width = piece
    got_refs, out_refs = refs[: 1 + shared], refs[-2 * (n // 2) :]
    depth = groups * block
    share = lhs_ref.shape[0] // len(out_refs)
    start = pl.multiple_of(lax.axis_index("rep") * (cols // 2) + first, LANES)
    for i in range(layers):
        layer = lax.rem(lax.axis_index("parts") + i, layers) if shared else i
        own = dec_ref[layer, :, :, pl.ds(start, width)].reshape(depth, width)
        got = (got_refs[i][0] if shared else got_refs[0][i]).reshape(depth, width)
        total = jnp.dot(lhs_ref[:, :depth], own, preferred_element_type=jnp.float32)
        total += jnp.dot(lhs_ref[:, depth:], got, preferred_element_type=jnp.float32)
        for j, ref in enumerate(out_refs):
            ref[layer] = total[j * share : (j + 1) * share].astype(ref.dtype)


def add_kernel(n, pieces, bias_ref, target_ref, *refs):
    out_hbm, out_ref, sems = refs[-3:]
    half = n // 2
    cols = target_ref.shape[2]
    rep = lax.axis_index("rep")
    copies = []
    for i, (layers, first, width) in enumerate(pieces):
        for side in range(2):
            core = rep if side == 0 else 1 - rep
            columns = pl.ds(pl.multiple_of(core * (cols // 2) + first, LANES), width)
            mine = refs[(2 * i + side) * half : (2 * i + side + 1) * half]
            for j, layer in enumerate(layers):
                total = bias_ref[layer : layer + 1, columns]
                total = total - target_ref[layer, :, columns].astype(jnp.float32)
                for ref in mine:
                    total = total + ref[j].astype(jnp.float32)
                out_ref[layer, :, columns] = total.astype(jnp.bfloat16)
                copies.append(
                    pltpu.make_async_copy(
                        out_ref.at[layer, :, columns],
                        out_hbm.at[layer, :, columns],
                        sems.at[len(copies)],
                    )
                )
                copies[-1].start()
    for copy in copies:
        copy.wait()


def body(acts, enc_w, enc_b, dec_w, dec_b, targets, active):
    n = lax.axis_size("src")
    rows, features = acts.shape
    layers, groups, block, cols = dec_w.shape
    share = rows // n
    half = n // 2
    pieces = cut_pieces(layers, cols // 2)
    tile_rows = rows // active.shape[0]
    pair = [(i, i ^ 1) for i in range(n)]
    params = pltpu.CompilerParams(vmem_limit_bytes=VMEM_BYTES)
    vmem = pl.BlockSpec(memory_space=pltpu.VMEM)
    smem = pl.BlockSpec(memory_space=pltpu.SMEM)
    anywhere = pl.BlockSpec(memory_space=pl.ANY)
    def weight(billions):
        return pl.CostEstimate(
            flops=int(billions * 1e9), bytes_accessed=0, transcendentals=0
        )

    cost = weight(0)

    dec_rows = dec_w
    acts, enc_w, dec_w = (
        pltpu.with_memory_space_constraint(value, pltpu.HBM)
        for value in (acts.reshape(half, 2, share, features), enc_w, dec_w)
    )

    def shape(*extent, kind=jnp.bfloat16):
        return jax.ShapeDtypeStruct(extent, kind)

    results = pl.pallas_call(
        functools.partial(encode_kernel, n, pieces),
        out_shape=[shape(half * share, 2 * block)] * n
        + [
            shape(1 if i == 0 else layers, groups, block, width)
            for i, (_, _, width) in enumerate(pieces)
        ],
        in_specs=[anywhere] * 3,
        out_specs=[vmem] * (n + len(pieces)),
        scratch_shapes=[
            pltpu.VMEM((2, half, share, features), jnp.bfloat16),
            pltpu.VMEM(enc_w.shape, jnp.bfloat16),
            pltpu.SemaphoreType.DMA((len(pieces), layers * groups)),
            pltpu.SemaphoreType.DMA((2 * half,)),
            pltpu.SemaphoreType.DMA((8,)),
        ],
        compiler_params=params,
        cost_estimate=cost,
        name="encode",
    )(acts, enc_w, dec_w)
    terms, parts = list(results[:n]), list(results[n:])
    for k in range(1, n):
        terms[k] = lax.ppermute(terms[k], "src", [(i, peer(i, k, n)) for i in range(n)])
    own = pl.pallas_call(
        functools.partial(codes_kernel, n, share, tile_rows),
        out_shape=shape(half, share, 2 * block),
        in_specs=[smem] + [vmem] * (1 + n),
        out_specs=vmem,
        compiler_params=params,
        cost_estimate=weight(20),
        name="codes",
    )(active, enc_b.reshape(n, block), *terms)
    codes = []
    for k in range(groups):
        for r in range(2):
            perm = [
                (i * 2 + c, (i + k) % groups * 2 + (c ^ r)) for i in range(groups) for c in range(2)
            ]
            codes.append(lax.ppermute(own, ("tgt", "rep"), perm) if k + r else own)

    lhs = pl.pallas_call(
        functools.partial(gather_kernel, n),
        out_shape=shape(rows, 2 * groups * block),
        in_specs=[vmem] * len(codes),
        out_specs=vmem,
        compiler_params=params,
        cost_estimate=weight(20),
        name="gather",
    )(*codes)

    def hold(value, after):
        return pl.pallas_call(
            lambda *refs: None,
            out_shape=jax.ShapeDtypeStruct(value.shape, value.dtype),
            in_specs=[anywhere] * 2,
            out_specs=anywhere,
            input_output_aliases={0: 0},
            compiler_params=params,
            cost_estimate=cost,
            name="hold",
        )(value, after)

    got = [[lax.ppermute(parts[0], "src", pair)]]
    got[0].append(lax.ppermute(got[0][0], "parts", [(0, 1), (1, 0)]))
    if len(pieces) > 1:
        got.append([lax.ppermute(hold(parts[1], own), "src", pair)])
    def add(some, begun, billions):
        operands = [value for i in some for value in sums[i]]
        return pl.pallas_call(
            functools.partial(add_kernel, n, [pieces[i] for i in some]),
            out_shape=shape(layers, share, cols),
            in_specs=[vmem] * (2 + len(operands)) + [anywhere] * len(begun),
            out_specs=anywhere,
            scratch_shapes=[
                pltpu.VMEM((layers, share, cols), jnp.bfloat16),
                pltpu.SemaphoreType.DMA((2 * len(some) * layers,)),
            ],
            input_output_aliases={2 + len(operands): 0} if begun else {},
            compiler_params=params,
            cost_estimate=weight(billions),
            name="add",
        )(dec_b, targets, *operands, *begun)

    sums, after, begun = [], [], []
    for i, (_, _, width) in enumerate(pieces):
        shapes = [shape(layers, share, width)] * (2 * half)
        shapes[0] = shape(layers, share, width, kind=jnp.float32)
        terms = pl.pallas_call(
            functools.partial(decode_kernel, n, pieces[i], i == 0),
            out_shape=shapes,
            in_specs=[vmem] * (2 + len(got[i])) + [anywhere] * len(after),
            out_specs=[vmem] * len(shapes),
            compiler_params=params,
            cost_estimate=weight(0),
            name="decode",
        )(dec_rows, lhs, *got[i], *after)
        after = [terms[0]]
        if i == 0:
            for part in parts[2:]:
                got.append([lax.ppermute(hold(part, own), "src", pair)])
        sums.append([])
        for r in range(2):
            for j in range(half):
                perm = [
                    (d * 2 + c, (d + 2 * j) % n * 2 + (c ^ r)) for d in range(n) for c in range(2)
                ]
                term = terms[2 * j + r]
                sums[i].append(lax.ppermute(term, ("src", "rep"), perm) if j + r else term)

    for i in range(len(pieces) - 1):
        begun = [add([i], begun, 20)]
    return add([len(pieces) - 1], begun, 0)


def solution(mesh):
    in_specs = (
        P(("parts", "rep"), "src"),
        P("src", "tgt"),
        P("tgt"),
        P(None, None, "src", "tgt"),
        P(None, "tgt"),
        P(None, ("parts", "rep", "src"), "tgt"),
        P(("parts", "rep"), None),
    )
    out_specs = P(None, ("parts", "rep", "src"), "tgt")
    return jax.shard_map(body, mesh=mesh, in_specs=in_specs, out_specs=out_specs, check_vma=False)
```

```python
import functools

import jax
import jax.numpy as jnp
from jax import lax
from jax.experimental import pallas as pl
from jax.experimental.pallas import tpu as pltpu
from jax.sharding import PartitionSpec as P

VMEM_BYTES = 32 * 1024 * 1024
LANES = 128
PIECES = (((0,), 0, False), ((1,), 0, True), ((0, 1), 1, False))


def cut_pieces(columns):
    middle = -(-(columns // LANES) // 2) * LANES
    bounds = ((0, middle), (middle, columns))
    return [
        (layers, bounds[side][0], bounds[side][1] - bounds[side][0], across)
        for layers, side, across in PIECES
    ]


def layer_of(offset, layers):
    return lax.rem(lax.axis_index("parts") + offset, layers)


def peer(index, k, n):
    return index ^ k if n & (n - 1) == 0 else (index + k) % n


def part_copies(piece, dec_hbm, part_ref, sems):
    offsets, first, width, _ = piece
    layers, groups, _, cols = dec_hbm.shape
    start = pl.multiple_of(lax.axis_index("rep") * (cols // 2) + first, LANES)
    copies = []
    for i, offset in enumerate(offsets):
        for group in range(groups):
            source = dec_hbm.at[layer_of(offset, layers), group, :, pl.ds(start, width)]
            sem = sems.at[i * groups + group]
            copies.append(pltpu.make_async_copy(source, part_ref.at[i, group], sem))
            copies[-1].start()
    return copies


def encode_kernel(n, pieces, acts_hbm, w_hbm, dec_hbm, *refs):
    term_refs, part_refs, refs = refs[:n], refs[n:-5], refs[-5:]
    acts_ref, w_ref, part_sems, acts_sems, w_sems = refs
    half = n // 2
    width = w_ref.shape[1] // half
    depth = w_ref.shape[0] // 8
    copies = []
    for i in range(2):
        for j in range(half):
            copies.append(
                pltpu.make_async_copy(
                    acts_hbm.at[j, i], acts_ref.at[i, j], acts_sems.at[i * half + j]
                )
            )
    for i in range(8):
        rows = slice(i * depth, (i + 1) * depth)
        copies.append(pltpu.make_async_copy(w_hbm.at[rows], w_ref.at[rows], w_sems.at[i]))
    for copy in copies:
        copy.start()
    for copy in copies:
        copy.wait()
    copies_part = []
    for i, piece in enumerate(pieces):
        copies_part += part_copies(piece, dec_hbm, part_refs[i], part_sems.at[i])
    src = lax.axis_index("src")
    for k in range(n):
        dest = peer(src, k, n)
        rows = acts_ref[lax.rem(dest, 2)]
        rows = rows.reshape(rows.shape[0] * rows.shape[1], rows.shape[2])
        columns = pl.ds(pl.multiple_of((dest // 2) * width, width), width)
        term_refs[k][...] = jnp.dot(
            rows, w_ref[:, columns], preferred_element_type=jnp.float32
        ).astype(jnp.bfloat16)
    for copy in copies_part:
        copy.wait()


def codes_kernel(n, share, tile_rows, active_ref, bias_ref, *refs):
    term_refs, out_ref = refs[:n], refs[n]
    src = lax.axis_index("src")
    tgt = lax.axis_index("tgt")
    parity, half = lax.rem(src, 2), src // 2
    block = out_ref.shape[2] // 2
    pre = term_refs[0][...].astype(jnp.float32)
    for ref in term_refs[1:]:
        pre = pre + ref[...].astype(jnp.float32)
    tiles, slots = active_ref.shape
    for piece in range(2):
        columns = slice(piece * block, (piece + 1) * block)
        bias = bias_ref[pl.ds(half * 2 + piece, 1), :]
        wanted = tgt * n + half * 2 + piece
        flags = []
        for tile in range(tiles):
            flags.append(
                lax.fori_loop(
                    0,
                    slots,
                    lambda i, total: total + (active_ref[tile, i] == wanted).astype(jnp.int32),
                    jnp.int32(0),
                    unroll=slots <= 16,
                )
            )
        for group in range(n // 2):
            tile = ((group * 2 + parity) * share) // tile_rows
            flag = flags[0]
            for i in range(1, tiles):
                flag = jnp.where(tile == i, flags[i], flag)
            live = jnp.where(flag > 0, 1.0, 0.0).astype(jnp.float32)
            rows = slice(group * share, (group + 1) * share)
            value = live * jnp.maximum(pre[rows, columns] + bias, 0.0)
            out_ref[group, :, columns] = value.astype(jnp.bfloat16)


def gather_kernel(n, *refs):
    half = n // 2
    code_refs, out_ref = refs[:-1], refs[-1]
    groups = len(code_refs) // 2
    src, tgt = lax.axis_index("src"), lax.axis_index("tgt")
    parity = lax.rem(src, 2)
    share, block = code_refs[0].shape[1], code_refs[0].shape[2] // 2
    for k in range(groups):
        place = lax.rem(tgt - k + groups, groups)
        for side in range(2):
            latents = parity if side == 0 else 1 - parity
            latents = pl.ds(pl.multiple_of(latents * block, block), block)
            columns = pl.ds(pl.multiple_of((side * groups + place) * block, block), block)
            for j in range(half):
                group = lax.rem(src // 2 + j, half)
                for r in range(2):
                    rows = slice((2 * j + r) * share, (2 * j + r + 1) * share)
                    out_ref[rows, columns] = code_refs[2 * k + r][group, :, latents]


def decode_kernel(n, piece, dec_ref, lhs_ref, got_ref, *refs):
    offsets, first, width, _ = piece
    layers, groups, block, cols = dec_ref.shape
    out_refs = refs[-2 * (n // 2) :]
    depth = groups * block
    share = lhs_ref.shape[0] // len(out_refs)
    start = pl.multiple_of(lax.axis_index("rep") * (cols // 2) + first, LANES)
    for i, offset in enumerate(offsets):
        own = dec_ref[layer_of(offset, layers), :, :, pl.ds(start, width)].reshape(depth, width)
        got = got_ref[i].reshape(depth, width)
        total = jnp.dot(lhs_ref[:, :depth], own, preferred_element_type=jnp.float32)
        total += jnp.dot(lhs_ref[:, depth:], got, preferred_element_type=jnp.float32)
        for j, ref in enumerate(out_refs):
            ref[i] = total[j * share : (j + 1) * share].astype(ref.dtype)


def add_kernel(n, pieces, bias_ref, target_ref, *refs):
    out_hbm, out_ref, sems = refs[-3:]
    half = n // 2
    layers, _, cols = target_ref.shape
    rep = lax.axis_index("rep")
    copies = []
    for i, (offsets, first, width, _) in enumerate(pieces):
        for side in range(2):
            core = rep if side == 0 else 1 - rep
            columns = pl.ds(pl.multiple_of(core * (cols // 2) + first, LANES), width)
            for j, offset in enumerate(offsets):
                layer = layer_of(offset, layers)
                total = bias_ref[0:1, columns]
                for other in range(1, layers):
                    total = jnp.where(layer == other, bias_ref[other : other + 1, columns], total)
                total = total - target_ref[layer, :, columns].astype(jnp.float32)
                for ref in refs[(2 * i + side) * half : (2 * i + side + 1) * half]:
                    total = total + ref[j].astype(jnp.float32)
                place = len(copies)
                out_ref[place, :, :width] = total.astype(jnp.bfloat16)
                copies.append(
                    pltpu.make_async_copy(
                        out_ref.at[place, :, :width], out_hbm.at[layer, :, columns], sems.at[place]
                    )
                )
                copies[-1].start()
    for copy in copies:
        copy.wait()


def body(acts, enc_w, enc_b, dec_w, dec_b, targets, active):
    n = lax.axis_size("src")
    rows, features = acts.shape
    layers, groups, block, cols = dec_w.shape
    share = rows // n
    half = n // 2
    pieces = cut_pieces(cols // 2)
    fetched = [piece for piece in pieces if not piece[3]]
    tile_rows = rows // active.shape[0]
    pair = [(i, i ^ 1) for i in range(n)]
    params = pltpu.CompilerParams(vmem_limit_bytes=VMEM_BYTES)
    vmem = pl.BlockSpec(memory_space=pltpu.VMEM)
    smem = pl.BlockSpec(memory_space=pltpu.SMEM)
    anywhere = pl.BlockSpec(memory_space=pl.ANY)
    def weight(billions):
        return pl.CostEstimate(
            flops=int(billions * 1e9), bytes_accessed=0, transcendentals=0
        )

    cost = weight(0)

    dec_rows = dec_w
    acts, enc_w, dec_w = (
        pltpu.with_memory_space_constraint(value, pltpu.HBM)
        for value in (acts.reshape(half, 2, share, features), enc_w, dec_w)
    )

    def shape(*extent, kind=jnp.bfloat16):
        return jax.ShapeDtypeStruct(extent, kind)

    results = pl.pallas_call(
        functools.partial(encode_kernel, n, fetched),
        out_shape=[shape(half * share, 2 * block)] * n
        + [shape(len(offsets), groups, block, width) for offsets, _, width, _ in fetched],
        in_specs=[anywhere] * 3,
        out_specs=[vmem] * (n + len(fetched)),
        scratch_shapes=[
            pltpu.VMEM((2, half, share, features), jnp.bfloat16),
            pltpu.VMEM(enc_w.shape, jnp.bfloat16),
            pltpu.SemaphoreType.DMA((len(fetched), layers * groups)),
            pltpu.SemaphoreType.DMA((2 * half,)),
            pltpu.SemaphoreType.DMA((8,)),
        ],
        compiler_params=params,
        cost_estimate=cost,
        name="encode",
    )(acts, enc_w, dec_w)
    terms, parts = list(results[:n]), list(results[n:])
    for k in range(1, n):
        terms[k] = lax.ppermute(terms[k], "src", [(i, peer(i, k, n)) for i in range(n)])
    own = pl.pallas_call(
        functools.partial(codes_kernel, n, share, tile_rows),
        out_shape=shape(half, share, 2 * block),
        in_specs=[smem] + [vmem] * (1 + n),
        out_specs=vmem,
        compiler_params=params,
        cost_estimate=weight(20),
        name="codes",
    )(active, enc_b.reshape(n, block), *terms)
    codes = []
    for k in range(groups):
        for r in range(2):
            perm = [
                (i * 2 + c, (i + k) % groups * 2 + (c ^ r)) for i in range(groups) for c in range(2)
            ]
            codes.append(lax.ppermute(own, ("tgt", "rep"), perm) if k + r else own)

    lhs = pl.pallas_call(
        functools.partial(gather_kernel, n),
        out_shape=shape(rows, 2 * groups * block),
        in_specs=[vmem] * len(codes),
        out_specs=vmem,
        compiler_params=params,
        cost_estimate=weight(20),
        name="gather",
    )(*codes)

    def hold(value, after):
        return pl.pallas_call(
            lambda *refs: None,
            out_shape=jax.ShapeDtypeStruct(value.shape, value.dtype),
            in_specs=[anywhere] * 2,
            out_specs=anywhere,
            input_output_aliases={0: 0},
            compiler_params=params,
            cost_estimate=cost,
            name="hold",
        )(value, after)

    got = [lax.ppermute(parts[0], "src", pair)]
    got.append(lax.ppermute(got[0], "parts", [(0, 1), (1, 0)]))
    got.append(lax.ppermute(hold(parts[1], own), "src", pair))

    def add(some, begun, billions):
        operands = [value for i in some for value in sums[i]]
        count = 2 * sum(len(pieces[i][0]) for i in some)
        widest = max(piece[2] for piece in pieces)
        return pl.pallas_call(
            functools.partial(add_kernel, n, [pieces[i] for i in some]),
            out_shape=shape(layers, share, cols),
            in_specs=[vmem] * (2 + len(operands)) + [anywhere] * len(begun),
            out_specs=anywhere,
            scratch_shapes=[
                pltpu.VMEM((count, share, widest), jnp.bfloat16),
                pltpu.SemaphoreType.DMA((count,)),
            ],
            input_output_aliases={2 + len(operands): 0} if begun else {},
            compiler_params=params,
            cost_estimate=weight(billions),
            name="add",
        )(dec_b, targets, *operands, *begun)

    sums, after = [], []
    for i, piece in enumerate(pieces):
        offsets, _, width, _ = piece
        shapes = [shape(len(offsets), share, width)] * (2 * half)
        shapes[0] = shape(len(offsets), share, width, kind=jnp.float32)
        terms = pl.pallas_call(
            functools.partial(decode_kernel, n, piece),
            out_shape=shapes,
            in_specs=[vmem] * 3 + [anywhere] * len(after),
            out_specs=[vmem] * len(shapes),
            compiler_params=params,
            cost_estimate=weight(0),
            name="decode",
        )(dec_rows, lhs, got[i], *after)
        after = [terms[0]]
        sums.append([None] * (2 * half))
        for j in [*range(1, half), 0]:
            for r in range(2):
                perm = [
                    (d * 2 + c, (d + 2 * j) % n * 2 + (c ^ r)) for d in range(n) for c in range(2)
                ]
                term = terms[2 * j + r]
                sums[i][r * half + j] = (
                    lax.ppermute(term, ("src", "rep"), perm) if j + r else term
                )

    begun = []
    begun = [add([0, 1], begun, 20)]
    return add([2], begun, 0)


def solution(mesh):
    in_specs = (
        P(("parts", "rep"), "src"),
        P("src", "tgt"),
        P("tgt"),
        P(None, None, "src", "tgt"),
        P(None, "tgt"),
        P(None, ("parts", "rep", "src"), "tgt"),
        P(("parts", "rep"), None),
    )
    out_specs = P(None, ("parts", "rep", "src"), "tgt")
    return jax.shard_map(body, mesh=mesh, in_specs=in_specs, out_specs=out_specs, check_vma=False)
```

```python
import functools

import jax
import jax.numpy as jnp
from jax import lax
from jax.experimental import pallas as pl
from jax.experimental.pallas import tpu as pltpu
from jax.sharding import PartitionSpec as P

VMEM_BYTES = 32 * 1024 * 1024
LANES = 128
FIRST = 5
PIECES = (((0,), 0, False), ((1,), 0, True), ((0, 1), 1, False))


def cut_pieces(columns):
    middle = columns // LANES * FIRST // 8 * LANES
    bounds = ((0, middle), (middle, columns))
    return [
        (layers, bounds[side][0], bounds[side][1] - bounds[side][0], across)
        for layers, side, across in PIECES
    ]


def layer_of(offset, layers):
    return lax.rem(lax.axis_index("parts") + offset, layers)


def peer(index, k, n):
    return index ^ k if n & (n - 1) == 0 else (index + k) % n


def part_copies(piece, dec_hbm, part_ref, sems):
    offsets, first, width, _ = piece
    layers, groups, _, cols = dec_hbm.shape
    start = pl.multiple_of(lax.axis_index("rep") * (cols // 2) + first, LANES)
    copies = []
    for i, offset in enumerate(offsets):
        for group in range(groups):
            source = dec_hbm.at[layer_of(offset, layers), group, :, pl.ds(start, width)]
            sem = sems.at[i * groups + group]
            copies.append(pltpu.make_async_copy(source, part_ref.at[i, group], sem))
            copies[-1].start()
    return copies


def encode_kernel(n, pieces, acts_hbm, w_hbm, dec_hbm, *refs):
    term_refs, part_refs, refs = refs[:n], refs[n:-5], refs[-5:]
    acts_ref, w_ref, part_sems, acts_sems, w_sems = refs
    half = n // 2
    width = w_ref.shape[1] // half
    depth = w_ref.shape[0] // 8
    copies = []
    for i in range(2):
        for j in range(half):
            copies.append(
                pltpu.make_async_copy(
                    acts_hbm.at[j, i], acts_ref.at[i, j], acts_sems.at[i * half + j]
                )
            )
    for i in range(8):
        rows = slice(i * depth, (i + 1) * depth)
        copies.append(pltpu.make_async_copy(w_hbm.at[rows], w_ref.at[rows], w_sems.at[i]))
    for copy in copies:
        copy.start()
    for copy in copies:
        copy.wait()
    copies_part = []
    for i, piece in enumerate(pieces):
        copies_part += part_copies(piece, dec_hbm, part_refs[i], part_sems.at[i])
    src = lax.axis_index("src")
    for k in range(n):
        dest = peer(src, k, n)
        rows = acts_ref[lax.rem(dest, 2)]
        rows = rows.reshape(rows.shape[0] * rows.shape[1], rows.shape[2])
        columns = pl.ds(pl.multiple_of((dest // 2) * width, width), width)
        term_refs[k][...] = jnp.dot(
            rows, w_ref[:, columns], preferred_element_type=jnp.float32
        ).astype(jnp.bfloat16)
    for copy in copies_part:
        copy.wait()


def codes_kernel(n, share, tile_rows, active_ref, bias_ref, *refs):
    term_refs, out_ref = refs[:n], refs[n]
    src = lax.axis_index("src")
    tgt = lax.axis_index("tgt")
    parity, half = lax.rem(src, 2), src // 2
    block = out_ref.shape[2] // 2
    pre = term_refs[0][...].astype(jnp.float32)
    for ref in term_refs[1:]:
        pre = pre + ref[...].astype(jnp.float32)
    tiles, slots = active_ref.shape
    for piece in range(2):
        columns = slice(piece * block, (piece + 1) * block)
        bias = bias_ref[pl.ds(half * 2 + piece, 1), :]
        wanted = tgt * n + half * 2 + piece
        flags = []
        for tile in range(tiles):
            flags.append(
                lax.fori_loop(
                    0,
                    slots,
                    lambda i, total: total + (active_ref[tile, i] == wanted).astype(jnp.int32),
                    jnp.int32(0),
                    unroll=slots <= 16,
                )
            )
        for group in range(n // 2):
            tile = ((group * 2 + parity) * share) // tile_rows
            flag = flags[0]
            for i in range(1, tiles):
                flag = jnp.where(tile == i, flags[i], flag)
            live = jnp.where(flag > 0, 1.0, 0.0).astype(jnp.float32)
            rows = slice(group * share, (group + 1) * share)
            value = live * jnp.maximum(pre[rows, columns] + bias, 0.0)
            out_ref[group, :, columns] = value.astype(jnp.bfloat16)


def gather_kernel(n, *refs):
    half = n // 2
    code_refs, out_ref = refs[:-1], refs[-1]
    groups = len(code_refs) // 2
    src, tgt = lax.axis_index("src"), lax.axis_index("tgt")
    parity = lax.rem(src, 2)
    share, block = code_refs[0].shape[1], code_refs[0].shape[2] // 2
    for k in range(groups):
        place = lax.rem(tgt - k + groups, groups)
        for side in range(2):
            latents = parity if side == 0 else 1 - parity
            latents = pl.ds(pl.multiple_of(latents * block, block), block)
            columns = pl.ds(pl.multiple_of((side * groups + place) * block, block), block)
            for j in range(half):
                group = lax.rem(src // 2 + j, half)
                for r in range(2):
                    rows = slice((2 * j + r) * share, (2 * j + r + 1) * share)
                    out_ref[rows, columns] = code_refs[2 * k + r][group, :, latents]


def decode_kernel(n, piece, dec_ref, lhs_ref, got_ref, *refs):
    offsets, first, width, _ = piece
    layers, groups, block, cols = dec_ref.shape
    out_refs = refs[-2 * (n // 2) :]
    depth = groups * block
    share = lhs_ref.shape[0] // len(out_refs)
    start = pl.multiple_of(lax.axis_index("rep") * (cols // 2) + first, LANES)
    for i, offset in enumerate(offsets):
        own = dec_ref[layer_of(offset, layers), :, :, pl.ds(start, width)].reshape(depth, width)
        got = got_ref[i].reshape(depth, width)
        total = jnp.dot(lhs_ref[:, :depth], own, preferred_element_type=jnp.float32)
        total += jnp.dot(lhs_ref[:, depth:], got, preferred_element_type=jnp.float32)
        for j, ref in enumerate(out_refs):
            ref[i] = total[j * share : (j + 1) * share].astype(ref.dtype)


def add_kernel(n, pieces, bias_ref, target_ref, *refs):
    out_hbm, out_ref, sems = refs[-3:]
    half = n // 2
    layers, _, cols = target_ref.shape
    rep = lax.axis_index("rep")
    copies = []
    for i, (offsets, first, width, _) in enumerate(pieces):
        for side in range(2):
            core = rep if side == 0 else 1 - rep
            columns = pl.ds(pl.multiple_of(core * (cols // 2) + first, LANES), width)
            for j, offset in enumerate(offsets):
                layer = layer_of(offset, layers)
                total = bias_ref[0:1, columns]
                for other in range(1, layers):
                    total = jnp.where(layer == other, bias_ref[other : other + 1, columns], total)
                total = total - target_ref[layer, :, columns].astype(jnp.float32)
                mine = refs[2 * half * i : 2 * half * (i + 1)]
                first_sum = side * (half - 1)
                for ref in (*mine[first_sum : first_sum + half - 1], mine[-1 - side]):
                    total = total + ref[j].astype(jnp.float32)
                place = len(copies)
                out_ref[place, :, :width] = total.astype(jnp.bfloat16)
                copies.append(
                    pltpu.make_async_copy(
                        out_ref.at[place, :, :width], out_hbm.at[layer, :, columns], sems.at[place]
                    )
                )
                copies[-1].start()
    for copy in copies:
        copy.wait()


def body(acts, enc_w, enc_b, dec_w, dec_b, targets, active):
    n = lax.axis_size("src")
    rows, features = acts.shape
    layers, groups, block, cols = dec_w.shape
    share = rows // n
    half = n // 2
    pieces = cut_pieces(cols // 2)
    fetched = [piece for piece in pieces if not piece[3]]
    tile_rows = rows // active.shape[0]
    pair = [(i, i ^ 1) for i in range(n)]
    params = pltpu.CompilerParams(vmem_limit_bytes=VMEM_BYTES)
    vmem = pl.BlockSpec(memory_space=pltpu.VMEM)
    smem = pl.BlockSpec(memory_space=pltpu.SMEM)
    anywhere = pl.BlockSpec(memory_space=pl.ANY)
    def weight(billions):
        return pl.CostEstimate(
            flops=int(billions * 1e9), bytes_accessed=0, transcendentals=0
        )

    cost = weight(0)

    dec_rows = dec_w
    acts, enc_w, dec_w = (
        pltpu.with_memory_space_constraint(value, pltpu.HBM)
        for value in (acts.reshape(half, 2, share, features), enc_w, dec_w)
    )

    def shape(*extent, kind=jnp.bfloat16):
        return jax.ShapeDtypeStruct(extent, kind)

    results = pl.pallas_call(
        functools.partial(encode_kernel, n, fetched),
        out_shape=[shape(half * share, 2 * block)] * n
        + [shape(len(offsets), groups, block, width) for offsets, _, width, _ in fetched],
        in_specs=[anywhere] * 3,
        out_specs=[vmem] * (n + len(fetched)),
        scratch_shapes=[
            pltpu.VMEM((2, half, share, features), jnp.bfloat16),
            pltpu.VMEM(enc_w.shape, jnp.bfloat16),
            pltpu.SemaphoreType.DMA((len(fetched), layers * groups)),
            pltpu.SemaphoreType.DMA((2 * half,)),
            pltpu.SemaphoreType.DMA((8,)),
        ],
        compiler_params=params,
        cost_estimate=cost,
        name="encode",
    )(acts, enc_w, dec_w)
    terms, parts = list(results[:n]), list(results[n:])
    for k in range(1, n):
        terms[k] = lax.ppermute(terms[k], "src", [(i, peer(i, k, n)) for i in range(n)])
    own = pl.pallas_call(
        functools.partial(codes_kernel, n, share, tile_rows),
        out_shape=shape(half, share, 2 * block),
        in_specs=[smem] + [vmem] * (1 + n),
        out_specs=vmem,
        compiler_params=params,
        cost_estimate=weight(20),
        name="codes",
    )(active, enc_b.reshape(n, block), *terms)
    codes = []
    for k in range(groups):
        for r in range(2):
            perm = [
                (i * 2 + c, (i + k) % groups * 2 + (c ^ r)) for i in range(groups) for c in range(2)
            ]
            codes.append(lax.ppermute(own, ("tgt", "rep"), perm) if k + r else own)

    lhs = pl.pallas_call(
        functools.partial(gather_kernel, n),
        out_shape=shape(rows, 2 * groups * block),
        in_specs=[vmem] * len(codes),
        out_specs=vmem,
        compiler_params=params,
        cost_estimate=weight(20),
        name="gather",
    )(*codes)

    def hold(value, after):
        return pl.pallas_call(
            lambda *refs: None,
            out_shape=jax.ShapeDtypeStruct(value.shape, value.dtype),
            in_specs=[anywhere] * 2,
            out_specs=anywhere,
            input_output_aliases={0: 0},
            compiler_params=params,
            cost_estimate=cost,
            name="hold",
        )(value, after)

    got = [lax.ppermute(parts[0], "src", pair)]
    got.append(lax.ppermute(got[0], "parts", [(0, 1), (1, 0)]))
    got.append(lax.ppermute(hold(parts[1], own), "src", pair))

    def add(some, begun, billions):
        operands = [value for i in some for value in sums[i]]
        count = 2 * sum(len(pieces[i][0]) for i in some)
        widest = max(piece[2] for piece in pieces)
        return pl.pallas_call(
            functools.partial(add_kernel, n, [pieces[i] for i in some]),
            out_shape=shape(layers, share, cols),
            in_specs=[vmem] * (2 + len(operands)) + [anywhere] * len(begun),
            out_specs=anywhere,
            scratch_shapes=[
                pltpu.VMEM((count, share, widest), jnp.bfloat16),
                pltpu.SemaphoreType.DMA((count,)),
            ],
            input_output_aliases={2 + len(operands): 0} if begun else {},
            compiler_params=params,
            cost_estimate=weight(billions),
            name="add",
        )(dec_b, targets, *operands, *begun)

    sums, after = [], []
    for i, piece in enumerate(pieces):
        offsets, _, width, _ = piece
        shapes = [shape(len(offsets), share, width)] * (2 * half)
        shapes[0] = shape(len(offsets), share, width, kind=jnp.float32)
        terms = pl.pallas_call(
            functools.partial(decode_kernel, n, piece),
            out_shape=shapes,
            in_specs=[vmem] * 3 + [anywhere] * len(after),
            out_specs=[vmem] * len(shapes),
            compiler_params=params,
            cost_estimate=weight(0),
            name="decode",
        )(dec_rows, lhs, got[i], *after)
        after = [terms[0]]
        sums.append([])
        for r, j in [(r, j) for r in range(2) for j in range(1, half)] + [(1, 0)]:
            perm = [(d * 2 + c, (d + 2 * j) % n * 2 + (c ^ r)) for d in range(n) for c in range(2)]
            sums[i].append(lax.ppermute(terms[2 * j + r], ("src", "rep"), perm))
        sums[i].append(terms[0])

    begun = []
    begun = [add([0, 1], begun, 20)]
    return add([2], begun, 0)


def solution(mesh):
    in_specs = (
        P(("parts", "rep"), "src"),
        P("src", "tgt"),
        P("tgt"),
        P(None, None, "src", "tgt"),
        P(None, "tgt"),
        P(None, ("parts", "rep", "src"), "tgt"),
        P(("parts", "rep"), None),
    )
    out_specs = P(None, ("parts", "rep", "src"), "tgt")
    return jax.shard_map(body, mesh=mesh, in_specs=in_specs, out_specs=out_specs, check_vma=False)
```

```python
import functools

import jax
import jax.numpy as jnp
from jax import lax
from jax.experimental import pallas as pl
from jax.experimental.pallas import tpu as pltpu
from jax.sharding import PartitionSpec as P

VMEM_BYTES = 32 * 1024 * 1024
LANES = 128
FIRST = 5
PIECES = (((0,), 0, False), ((1,), 0, True), ((0, 1), 1, False))


def cut_pieces(columns):
    middle = columns // LANES * FIRST // 8 * LANES
    bounds = ((0, middle), (middle, columns))
    return [
        (layers, bounds[side][0], bounds[side][1] - bounds[side][0], across)
        for layers, side, across in PIECES
    ]


def layer_of(offset, layers):
    return lax.rem(lax.axis_index("parts") + offset, layers)


def peer(index, k, n):
    return index ^ k if n & (n - 1) == 0 else (index + k) % n


def part_copies(piece, dec_hbm, part_ref, sems):
    offsets, first, width, _ = piece
    layers, groups, _, cols = dec_hbm.shape
    start = pl.multiple_of(lax.axis_index("rep") * (cols // 2) + first, LANES)
    copies = []
    for i, offset in enumerate(offsets):
        for group in range(groups):
            source = dec_hbm.at[layer_of(offset, layers), group, :, pl.ds(start, width)]
            sem = sems.at[i * groups + group]
            copies.append(pltpu.make_async_copy(source, part_ref.at[i, group], sem))
            copies[-1].start()
    return copies


def encode_kernel(n, pieces, acts_hbm, w_hbm, dec_hbm, *refs):
    term_refs, part_refs, refs = refs[:n], refs[n:-5], refs[-5:]
    acts_ref, w_ref, part_sems, acts_sems, w_sems = refs
    half = n // 2
    width = w_ref.shape[1] // half
    depth = w_ref.shape[0] // 8
    copies = []
    for i in range(2):
        for j in range(half):
            copies.append(
                pltpu.make_async_copy(
                    acts_hbm.at[j, i], acts_ref.at[i, j], acts_sems.at[i * half + j]
                )
            )
    for i in range(8):
        rows = slice(i * depth, (i + 1) * depth)
        copies.append(pltpu.make_async_copy(w_hbm.at[rows], w_ref.at[rows], w_sems.at[i]))
    for copy in copies:
        copy.start()
    for copy in copies:
        copy.wait()
    copies_part = []
    for i, piece in enumerate(pieces):
        copies_part += part_copies(piece, dec_hbm, part_refs[i], part_sems.at[i])
    src = lax.axis_index("src")
    for k in range(n):
        dest = peer(src, k, n)
        rows = acts_ref[lax.rem(dest, 2)]
        rows = rows.reshape(rows.shape[0] * rows.shape[1], rows.shape[2])
        columns = pl.ds(pl.multiple_of((dest // 2) * width, width), width)
        term_refs[k][...] = jnp.dot(
            rows, w_ref[:, columns], preferred_element_type=jnp.float32
        ).astype(jnp.bfloat16)
    for copy in copies_part:
        copy.wait()


def part_kernel(piece, before_ref, dec_hbm, after_ref, part_ref, sems):
    for copy in part_copies(piece, dec_hbm, part_ref, sems):
        copy.wait()


def codes_kernel(n, share, tile_rows, active_ref, bias_ref, *refs):
    term_refs, out_ref = refs[:n], refs[n]
    src = lax.axis_index("src")
    tgt = lax.axis_index("tgt")
    parity, half = lax.rem(src, 2), src // 2
    block = out_ref.shape[2] // 2
    pre = term_refs[0][...].astype(jnp.float32)
    for ref in term_refs[1:]:
        pre = pre + ref[...].astype(jnp.float32)
    tiles, slots = active_ref.shape
    for piece in range(2):
        columns = slice(piece * block, (piece + 1) * block)
        bias = bias_ref[pl.ds(half * 2 + piece, 1), :]
        wanted = tgt * n + half * 2 + piece
        flags = []
        for tile in range(tiles):
            flags.append(
                lax.fori_loop(
                    0,
                    slots,
                    lambda i, total: total + (active_ref[tile, i] == wanted).astype(jnp.int32),
                    jnp.int32(0),
                    unroll=slots <= 16,
                )
            )
        for group in range(n // 2):
            tile = ((group * 2 + parity) * share) // tile_rows
            flag = flags[0]
            for i in range(1, tiles):
                flag = jnp.where(tile == i, flags[i], flag)
            live = jnp.where(flag > 0, 1.0, 0.0).astype(jnp.float32)
            rows = slice(group * share, (group + 1) * share)
            value = live * jnp.maximum(pre[rows, columns] + bias, 0.0)
            out_ref[group, :, columns] = value.astype(jnp.bfloat16)


def gather_kernel(n, *refs):
    half = n // 2
    code_refs, out_ref = refs[:-1], refs[-1]
    groups = len(code_refs) // 2
    src, tgt = lax.axis_index("src"), lax.axis_index("tgt")
    parity = lax.rem(src, 2)
    share, block = code_refs[0].shape[1], code_refs[0].shape[2] // 2
    for k in range(groups):
        place = lax.rem(tgt - k + groups, groups)
        for side in range(2):
            latents = parity if side == 0 else 1 - parity
            latents = pl.ds(pl.multiple_of(latents * block, block), block)
            columns = pl.ds(pl.multiple_of((side * groups + place) * block, block), block)
            for j in range(half):
                group = lax.rem(src // 2 + j, half)
                for r in range(2):
                    rows = slice((2 * j + r) * share, (2 * j + r + 1) * share)
                    out_ref[rows, columns] = code_refs[2 * k + r][group, :, latents]


def decode_kernel(n, piece, dec_ref, lhs_ref, got_ref, *refs):
    offsets, first, width, _ = piece
    layers, groups, block, cols = dec_ref.shape
    out_refs = refs[-2 * (n // 2) :]
    depth = groups * block
    share = lhs_ref.shape[0] // len(out_refs)
    start = pl.multiple_of(lax.axis_index("rep") * (cols // 2) + first, LANES)
    for i, offset in enumerate(offsets):
        own = dec_ref[layer_of(offset, layers), :, :, pl.ds(start, width)].reshape(depth, width)
        got = got_ref[i].reshape(depth, width)
        total = jnp.dot(lhs_ref[:, :depth], own, preferred_element_type=jnp.float32)
        total += jnp.dot(lhs_ref[:, depth:], got, preferred_element_type=jnp.float32)
        for j, ref in enumerate(out_refs):
            ref[i] = total[j * share : (j + 1) * share].astype(ref.dtype)


def add_kernel(n, pieces, bias_ref, target_ref, *refs):
    out_hbm, out_ref, sems = refs[-3:]
    half = n // 2
    layers, _, cols = target_ref.shape
    rep = lax.axis_index("rep")
    copies = []
    for i, (offsets, first, width, _) in enumerate(pieces):
        for side in range(2):
            core = rep if side == 0 else 1 - rep
            columns = pl.ds(pl.multiple_of(core * (cols // 2) + first, LANES), width)
            for j, offset in enumerate(offsets):
                layer = layer_of(offset, layers)
                total = bias_ref[0:1, columns]
                for other in range(1, layers):
                    total = jnp.where(layer == other, bias_ref[other : other + 1, columns], total)
                total = total - target_ref[layer, :, columns].astype(jnp.float32)
                mine = refs[2 * half * i : 2 * half * (i + 1)]
                first_sum = side * (half - 1)
                for ref in (*mine[first_sum : first_sum + half - 1], mine[-1 - side]):
                    total = total + ref[j].astype(jnp.float32)
                place = len(copies)
                out_ref[place, :, :width] = total.astype(jnp.bfloat16)
                copies.append(
                    pltpu.make_async_copy(
                        out_ref.at[place, :, :width], out_hbm.at[layer, :, columns], sems.at[place]
                    )
                )
                copies[-1].start()
    for copy in copies:
        copy.wait()


def body(acts, enc_w, enc_b, dec_w, dec_b, targets, active):
    n = lax.axis_size("src")
    rows, features = acts.shape
    layers, groups, block, cols = dec_w.shape
    share = rows // n
    half = n // 2
    pieces = cut_pieces(cols // 2)
    fetched = [piece for piece in pieces if not piece[3]]
    tile_rows = rows // active.shape[0]
    pair = [(i, i ^ 1) for i in range(n)]
    params = pltpu.CompilerParams(vmem_limit_bytes=VMEM_BYTES)
    vmem = pl.BlockSpec(memory_space=pltpu.VMEM)
    smem = pl.BlockSpec(memory_space=pltpu.SMEM)
    anywhere = pl.BlockSpec(memory_space=pl.ANY)
    def weight(billions):
        return pl.CostEstimate(
            flops=int(billions * 1e9), bytes_accessed=0, transcendentals=0
        )

    cost = weight(0)

    dec_rows = dec_w
    acts, enc_w, dec_w = (
        pltpu.with_memory_space_constraint(value, pltpu.HBM)
        for value in (acts.reshape(half, 2, share, features), enc_w, dec_w)
    )

    def shape(*extent, kind=jnp.bfloat16):
        return jax.ShapeDtypeStruct(extent, kind)

    results = pl.pallas_call(
        functools.partial(encode_kernel, n, fetched[:1]),
        out_shape=[shape(half * share, 2 * block)] * n
        + [shape(len(offsets), groups, block, width) for offsets, _, width, _ in fetched[:1]],
        in_specs=[anywhere] * 3,
        out_specs=[vmem] * (n + 1),
        scratch_shapes=[
            pltpu.VMEM((2, half, share, features), jnp.bfloat16),
            pltpu.VMEM(enc_w.shape, jnp.bfloat16),
            pltpu.SemaphoreType.DMA((1, layers * groups)),
            pltpu.SemaphoreType.DMA((2 * half,)),
            pltpu.SemaphoreType.DMA((8,)),
        ],
        compiler_params=params,
        cost_estimate=cost,
        name="encode",
    )(acts, enc_w, dec_w)
    terms, parts = list(results[:n]), list(results[n:])
    for k in range(1, n):
        terms[k] = lax.ppermute(terms[k], "src", [(i, peer(i, k, n)) for i in range(n)])
    order = [0, half, *(k for k in range(1, n) if k != half)]
    own = pl.pallas_call(
        functools.partial(codes_kernel, n, share, tile_rows),
        out_shape=shape(half, share, 2 * block),
        in_specs=[smem] + [vmem] * (1 + n),
        out_specs=vmem,
        compiler_params=params,
        cost_estimate=weight(20),
        name="codes",
    )(active, enc_b.reshape(n, block), *[terms[k] for k in order])
    codes = []
    for k in range(groups):
        for r in range(2):
            perm = [
                (i * 2 + c, (i + k) % groups * 2 + (c ^ r)) for i in range(groups) for c in range(2)
            ]
            codes.append(lax.ppermute(own, ("tgt", "rep"), perm) if k + r else own)

    lhs = pl.pallas_call(
        functools.partial(gather_kernel, n),
        out_shape=shape(rows, 2 * groups * block),
        in_specs=[vmem] * len(codes),
        out_specs=vmem,
        compiler_params=params,
        cost_estimate=weight(20),
        name="gather",
    )(*codes)

    part = pl.pallas_call(
        functools.partial(part_kernel, fetched[1]),
        out_shape=shape(len(fetched[1][0]), groups, block, fetched[1][2]),
        in_specs=[anywhere] * 3,
        out_specs=vmem,
        scratch_shapes=[pltpu.SemaphoreType.DMA((layers * groups,))],
        compiler_params=params,
        cost_estimate=weight(0),
        name="part",
    )(parts[0], dec_w, own)

    got = [lax.ppermute(parts[0], "src", pair)]
    got.append(lax.ppermute(got[0], "parts", [(0, 1), (1, 0)]))
    got.append(lax.ppermute(part, "src", pair))

    def add(some, begun, billions):
        operands = [value for i in some for value in sums[i]]
        count = 2 * sum(len(pieces[i][0]) for i in some)
        widest = max(piece[2] for piece in pieces)
        return pl.pallas_call(
            functools.partial(add_kernel, n, [pieces[i] for i in some]),
            out_shape=shape(layers, share, cols),
            in_specs=[vmem] * (2 + len(operands)) + [anywhere] * len(begun),
            out_specs=anywhere,
            scratch_shapes=[
                pltpu.VMEM((count, share, widest), jnp.bfloat16),
                pltpu.SemaphoreType.DMA((count,)),
            ],
            input_output_aliases={2 + len(operands): 0} if begun else {},
            compiler_params=params,
            cost_estimate=weight(billions),
            name="add",
        )(dec_b, targets, *operands, *begun)

    sums, after = [], []
    for i, piece in enumerate(pieces):
        offsets, _, width, _ = piece
        shapes = [shape(len(offsets), share, width)] * (2 * half)
        shapes[0] = shape(len(offsets), share, width, kind=jnp.float32)
        terms = pl.pallas_call(
            functools.partial(decode_kernel, n, piece),
            out_shape=shapes,
            in_specs=[vmem] * 3 + [anywhere] * len(after),
            out_specs=[vmem] * len(shapes),
            compiler_params=params,
            cost_estimate=weight(0),
            name="decode",
        )(dec_rows, lhs, got[i], *after)
        after = [terms[0]]
        sums.append([])
        for r, j in [(r, j) for r in range(2) for j in range(1, half)] + [(1, 0)]:
            perm = [(d * 2 + c, (d + 2 * j) % n * 2 + (c ^ r)) for d in range(n) for c in range(2)]
            sums[i].append(lax.ppermute(terms[2 * j + r], ("src", "rep"), perm))
        sums[i].append(terms[0])

    begun = []
    begun = [add([0, 1], begun, 20)]
    return add([2], begun, 0)


def solution(mesh):
    in_specs = (
        P(("parts", "rep"), "src"),
        P("src", "tgt"),
        P("tgt"),
        P(None, None, "src", "tgt"),
        P(None, "tgt"),
        P(None, ("parts", "rep", "src"), "tgt"),
        P(("parts", "rep"), None),
    )
    out_specs = P(None, ("parts", "rep", "src"), "tgt")
    return jax.shard_map(body, mesh=mesh, in_specs=in_specs, out_specs=out_specs, check_vma=False)
```

```python
import functools

import jax
import jax.numpy as jnp
from jax import lax
from jax.experimental import pallas as pl
from jax.experimental.pallas import tpu as pltpu
from jax.sharding import PartitionSpec as P

VMEM_BYTES = 32 * 1024 * 1024
LANES = 128
FIRST = 4
PIECES = (((0,), 0), ((1,), 0), ((0, 1), 1))


def cut_pieces(columns):
    middle = columns // LANES * FIRST // 8 * LANES
    bounds = ((0, middle), (middle, columns))
    return [
        (layers, bounds[side][0], bounds[side][1] - bounds[side][0])
        for layers, side in PIECES
    ]


def layer_of(offset, layers):
    return lax.rem(lax.axis_index("parts") + offset, layers)


def peer(index, k, n):
    return index ^ k if n & (n - 1) == 0 else (index + k) % n


def part_copies(piece, dec_hbm, part_ref, sems):
    offsets, first, width = piece
    layers, groups, _, cols = dec_hbm.shape
    start = pl.multiple_of(lax.axis_index("rep") * (cols // 2) + first, LANES)
    copies = []
    for i, offset in enumerate(offsets):
        for group in range(groups):
            source = dec_hbm.at[layer_of(offset, layers), group, :, pl.ds(start, width)]
            sem = sems.at[i * groups + group]
            copies.append(pltpu.make_async_copy(source, part_ref.at[i, group], sem))
            copies[-1].start()
    return copies


def encode_kernel(n, pieces, acts_hbm, w_hbm, dec_hbm, *refs):
    term_refs, part_refs, refs = refs[:n], refs[n:-5], refs[-5:]
    acts_ref, w_ref, part_sems, acts_sems, w_sems = refs
    half = n // 2
    width = w_ref.shape[1] // half
    depth = w_ref.shape[0] // 8
    copies = []
    for i in range(2):
        for j in range(half):
            copies.append(
                pltpu.make_async_copy(
                    acts_hbm.at[j, i], acts_ref.at[i, j], acts_sems.at[i * half + j]
                )
            )
    for i in range(8):
        rows = slice(i * depth, (i + 1) * depth)
        copies.append(pltpu.make_async_copy(w_hbm.at[rows], w_ref.at[rows], w_sems.at[i]))
    for copy in copies:
        copy.start()
    for copy in copies:
        copy.wait()
    copies_part = []
    for i, piece in enumerate(pieces):
        copies_part += part_copies(piece, dec_hbm, part_refs[i], part_sems.at[i])
    src = lax.axis_index("src")
    for k in range(n):
        dest = peer(src, k, n)
        rows = acts_ref[lax.rem(dest, 2)]
        rows = rows.reshape(rows.shape[0] * rows.shape[1], rows.shape[2])
        columns = pl.ds(pl.multiple_of((dest // 2) * width, width), width)
        term_refs[k][...] = jnp.dot(
            rows, w_ref[:, columns], preferred_element_type=jnp.float32
        ).astype(jnp.bfloat16)
    for copy in copies_part:
        copy.wait()


def part_kernel(piece, before_ref, dec_hbm, after_ref, part_ref, sems):
    for copy in part_copies(piece, dec_hbm, part_ref, sems):
        copy.wait()


def codes_kernel(n, share, tile_rows, active_ref, bias_ref, *refs):
    term_refs, out_ref = refs[:n], refs[n]
    src = lax.axis_index("src")
    tgt = lax.axis_index("tgt")
    parity, half = lax.rem(src, 2), src // 2
    block = out_ref.shape[2] // 2
    pre = term_refs[0][...].astype(jnp.float32)
    for ref in term_refs[1:]:
        pre = pre + ref[...].astype(jnp.float32)
    tiles, slots = active_ref.shape
    for piece in range(2):
        columns = slice(piece * block, (piece + 1) * block)
        bias = bias_ref[pl.ds(half * 2 + piece, 1), :]
        wanted = tgt * n + half * 2 + piece
        flags = []
        for tile in range(tiles):
            flags.append(
                lax.fori_loop(
                    0,
                    slots,
                    lambda i, total: total + (active_ref[tile, i] == wanted).astype(jnp.int32),
                    jnp.int32(0),
                    unroll=slots <= 16,
                )
            )
        for group in range(n // 2):
            tile = ((group * 2 + parity) * share) // tile_rows
            flag = flags[0]
            for i in range(1, tiles):
                flag = jnp.where(tile == i, flags[i], flag)
            live = jnp.where(flag > 0, 1.0, 0.0).astype(jnp.float32)
            rows = slice(group * share, (group + 1) * share)
            value = live * jnp.maximum(pre[rows, columns] + bias, 0.0)
            out_ref[group, :, columns] = value.astype(jnp.bfloat16)


def gather_kernel(n, *refs):
    half = n // 2
    code_refs, out_ref = refs[:-1], refs[-1]
    groups = len(code_refs) // 2
    src, tgt = lax.axis_index("src"), lax.axis_index("tgt")
    parity = lax.rem(src, 2)
    share, block = code_refs[0].shape[1], code_refs[0].shape[2] // 2
    for k in range(groups):
        place = lax.rem(tgt - k + groups, groups)
        for side in range(2):
            latents = parity if side == 0 else 1 - parity
            latents = pl.ds(pl.multiple_of(latents * block, block), block)
            columns = pl.ds(pl.multiple_of((side * groups + place) * block, block), block)
            for j in range(half):
                group = lax.rem(src // 2 + j, half)
                for r in range(2):
                    rows = slice((2 * j + r) * share, (2 * j + r + 1) * share)
                    out_ref[rows, columns] = code_refs[2 * k + r][group, :, latents]


def decode_kernel(n, piece, dec_ref, lhs_ref, *refs):
    offsets, first, width = piece
    layers, groups, block, cols = dec_ref.shape
    out_refs = refs[-2 * (n // 2) :]
    depth = groups * block
    share = lhs_ref.shape[0] // len(out_refs)
    start = pl.multiple_of(lax.axis_index("rep") * (cols // 2) + first, LANES)
    for i, offset in enumerate(offsets):
        own = dec_ref[layer_of(offset, layers), :, :, pl.ds(start, width)].reshape(depth, width)
        got = refs[i][0].reshape(depth, width)
        total = jnp.dot(lhs_ref[:, :depth], own, preferred_element_type=jnp.float32)
        total += jnp.dot(lhs_ref[:, depth:], got, preferred_element_type=jnp.float32)
        for j, ref in enumerate(out_refs):
            ref[i] = total[j * share : (j + 1) * share].astype(ref.dtype)


def add_kernel(n, pieces, bias_ref, target_ref, *refs):
    out_hbm, out_ref, sems = refs[-3:]
    half = n // 2
    layers, _, cols = target_ref.shape
    rep = lax.axis_index("rep")
    copies = []
    for i, (offsets, first, width) in enumerate(pieces):
        for side in range(2):
            core = rep if side == 0 else 1 - rep
            columns = pl.ds(pl.multiple_of(core * (cols // 2) + first, LANES), width)
            for j, offset in enumerate(offsets):
                layer = layer_of(offset, layers)
                total = bias_ref[0:1, columns]
                for other in range(1, layers):
                    total = jnp.where(layer == other, bias_ref[other : other + 1, columns], total)
                total = total - target_ref[layer, :, columns].astype(jnp.float32)
                mine = refs[2 * half * i : 2 * half * (i + 1)]
                first_sum = side * (half - 1)
                for ref in (*mine[first_sum : first_sum + half - 1], mine[-1 - side]):
                    total = total + ref[j].astype(jnp.float32)
                place = len(copies)
                out_ref[place, :, :width] = total.astype(jnp.bfloat16)
                copies.append(
                    pltpu.make_async_copy(
                        out_ref.at[place, :, :width], out_hbm.at[layer, :, columns], sems.at[place]
                    )
                )
                copies[-1].start()
    for copy in copies:
        copy.wait()


def body(acts, enc_w, enc_b, dec_w, dec_b, targets, active):
    n = lax.axis_size("src")
    rows, features = acts.shape
    layers, groups, block, cols = dec_w.shape
    share = rows // n
    half = n // 2
    pieces = cut_pieces(cols // 2)
    fetched = [((0,), *pieces[i][1:]) for i in (0, 2)]
    tile_rows = rows // active.shape[0]
    pair = [(i, i ^ 1) for i in range(n)]
    params = pltpu.CompilerParams(vmem_limit_bytes=VMEM_BYTES)
    vmem = pl.BlockSpec(memory_space=pltpu.VMEM)
    smem = pl.BlockSpec(memory_space=pltpu.SMEM)
    anywhere = pl.BlockSpec(memory_space=pl.ANY)
    def weight(billions):
        return pl.CostEstimate(
            flops=int(billions * 1e9), bytes_accessed=0, transcendentals=0
        )

    cost = weight(0)

    dec_rows = dec_w
    acts, enc_w, dec_w = (
        pltpu.with_memory_space_constraint(value, pltpu.HBM)
        for value in (acts.reshape(half, 2, share, features), enc_w, dec_w)
    )

    def shape(*extent, kind=jnp.bfloat16):
        return jax.ShapeDtypeStruct(extent, kind)

    results = pl.pallas_call(
        functools.partial(encode_kernel, n, fetched[:1]),
        out_shape=[shape(half * share, 2 * block)] * n
        + [shape(len(offsets), groups, block, width) for offsets, _, width in fetched[:1]],
        in_specs=[anywhere] * 3,
        out_specs=[vmem] * (n + 1),
        scratch_shapes=[
            pltpu.VMEM((2, half, share, features), jnp.bfloat16),
            pltpu.VMEM(enc_w.shape, jnp.bfloat16),
            pltpu.SemaphoreType.DMA((1, layers * groups)),
            pltpu.SemaphoreType.DMA((2 * half,)),
            pltpu.SemaphoreType.DMA((8,)),
        ],
        compiler_params=params,
        cost_estimate=cost,
        name="encode",
    )(acts, enc_w, dec_w)
    terms, parts = list(results[:n]), list(results[n:])
    for k in range(1, n):
        terms[k] = lax.ppermute(terms[k], "src", [(i, peer(i, k, n)) for i in range(n)])
    order = [0, half, *(k for k in range(1, n) if k != half)]
    own = pl.pallas_call(
        functools.partial(codes_kernel, n, share, tile_rows),
        out_shape=shape(half, share, 2 * block),
        in_specs=[smem] + [vmem] * (1 + n),
        out_specs=vmem,
        compiler_params=params,
        cost_estimate=weight(20),
        name="codes",
    )(active, enc_b.reshape(n, block), *[terms[k] for k in order])
    codes = []
    for k in range(groups):
        for r in range(2):
            perm = [
                (i * 2 + c, (i + k) % groups * 2 + (c ^ r)) for i in range(groups) for c in range(2)
            ]
            codes.append(lax.ppermute(own, ("tgt", "rep"), perm) if k + r else own)

    lhs = pl.pallas_call(
        functools.partial(gather_kernel, n),
        out_shape=shape(rows, 2 * groups * block),
        in_specs=[vmem] * len(codes),
        out_specs=vmem,
        compiler_params=params,
        cost_estimate=weight(20),
        name="gather",
    )(*codes)

    part = pl.pallas_call(
        functools.partial(part_kernel, fetched[1]),
        out_shape=shape(len(fetched[1][0]), groups, block, fetched[1][2]),
        in_specs=[anywhere] * 3,
        out_specs=vmem,
        scratch_shapes=[pltpu.SemaphoreType.DMA((layers * groups,))],
        compiler_params=params,
        cost_estimate=weight(0),
        name="part",
    )(parts[0], dec_w, own)

    def hold(value, after):
        return pl.pallas_call(
            lambda *refs: None,
            out_shape=jax.ShapeDtypeStruct(value.shape, value.dtype),
            in_specs=[anywhere] * 2,
            out_specs=anywhere,
            input_output_aliases={0: 0},
            compiler_params=params,
            cost_estimate=cost,
            name="hold",
        )(value, after)

    swap = [(0, 1), (1, 0)]
    got = [[lax.ppermute(parts[0], "src", pair)]]
    got.append([lax.ppermute(got[0][0], "parts", swap)])
    got.append([lax.ppermute(part, "src", pair)])

    def add(some, begun, billions):
        operands = [value for i in some for value in sums[i]]
        count = 2 * sum(len(pieces[i][0]) for i in some)
        widest = max(width for _, _, width in pieces)
        return pl.pallas_call(
            functools.partial(add_kernel, n, [pieces[i] for i in some]),
            out_shape=shape(layers, share, cols),
            in_specs=[vmem] * (2 + len(operands)) + [anywhere] * len(begun),
            out_specs=anywhere,
            scratch_shapes=[
                pltpu.VMEM((count, share, widest), jnp.bfloat16),
                pltpu.SemaphoreType.DMA((count,)),
            ],
            input_output_aliases={2 + len(operands): 0} if begun else {},
            compiler_params=params,
            cost_estimate=weight(billions),
            name="add",
        )(dec_b, targets, *operands, *begun)

    sums, after = [], []
    for i, piece in enumerate(pieces):
        offsets, _, width = piece
        shapes = [shape(len(offsets), share, width)] * (2 * half)
        shapes[0] = shape(len(offsets), share, width, kind=jnp.float32)
        terms = pl.pallas_call(
            functools.partial(decode_kernel, n, piece),
            out_shape=shapes,
            in_specs=[vmem] * (2 + len(got[i])) + [anywhere] * len(after),
            out_specs=[vmem] * len(shapes),
            compiler_params=params,
            cost_estimate=weight((0, 20, 0)[i]),
            name="decode",
        )(dec_rows, lhs, *got[i], *after)
        after = [terms[0]]
        if i == 0:
            got[2].append(lax.ppermute(hold(got[2][0], terms[0]), "parts", swap))
        sums.append([])
        for r, j in [(r, j) for r in range(2) for j in range(1, half)] + [(1, 0)]:
            perm = [(d * 2 + c, (d + 2 * j) % n * 2 + (c ^ r)) for d in range(n) for c in range(2)]
            sums[i].append(lax.ppermute(terms[2 * j + r], ("src", "rep"), perm))
        sums[i].append(terms[0])

    begun = []
    begun = [add([0, 1], begun, 20)]
    return add([2], begun, 0)


def solution(mesh):
    in_specs = (
        P(("parts", "rep"), "src"),
        P("src", "tgt"),
        P("tgt"),
        P(None, None, "src", "tgt"),
        P(None, "tgt"),
        P(None, ("parts", "rep", "src"), "tgt"),
        P(("parts", "rep"), None),
    )
    out_specs = P(None, ("parts", "rep", "src"), "tgt")
    return jax.shard_map(body, mesh=mesh, in_specs=in_specs, out_specs=out_specs, check_vma=False)
```

```python
import functools

import jax
import jax.numpy as jnp
from jax import lax
from jax.experimental import pallas as pl
from jax.experimental.pallas import tpu as pltpu
from jax.sharding import PartitionSpec as P

VMEM_BYTES = 32 * 1024 * 1024
LANES = 128
FIRST = 5
PIECES = (((0,), 0, False), ((1,), 0, True), ((0, 1), 1, False))


def cut_pieces(columns):
    middle = columns // LANES * FIRST // 8 * LANES
    bounds = ((0, middle), (middle, columns))
    return [
        (layers, bounds[side][0], bounds[side][1] - bounds[side][0], across)
        for layers, side, across in PIECES
    ]


def layer_of(offset, layers):
    return lax.rem(lax.axis_index("parts") + offset, layers)


def peer(index, k, n):
    return index ^ k if n & (n - 1) == 0 else (index + k) % n


def part_copies(piece, dec_hbm, part_ref, sems):
    offsets, first, width, _ = piece
    layers, groups, _, cols = dec_hbm.shape
    start = pl.multiple_of(lax.axis_index("rep") * (cols // 2) + first, LANES)
    copies = []
    for i, offset in enumerate(offsets):
        for group in range(groups):
            source = dec_hbm.at[layer_of(offset, layers), group, :, pl.ds(start, width)]
            sem = sems.at[i * groups + group]
            copies.append(pltpu.make_async_copy(source, part_ref.at[i, group], sem))
            copies[-1].start()
    return copies


def encode_kernel(n, pieces, acts_hbm, w_hbm, dec_hbm, *refs):
    term_refs, part_refs, refs = refs[:n], refs[n:-5], refs[-5:]
    acts_ref, w_ref, part_sems, acts_sems, w_sems = refs
    half = n // 2
    width = w_ref.shape[1] // half
    depth = w_ref.shape[0] // 8
    copies = []
    for i in range(2):
        for j in range(half):
            copies.append(
                pltpu.make_async_copy(
                    acts_hbm.at[j, i], acts_ref.at[i, j], acts_sems.at[i * half + j]
                )
            )
    for i in range(8):
        rows = slice(i * depth, (i + 1) * depth)
        copies.append(pltpu.make_async_copy(w_hbm.at[rows], w_ref.at[rows], w_sems.at[i]))
    for copy in copies:
        copy.start()
    for copy in copies:
        copy.wait()
    copies_part = []
    for i, piece in enumerate(pieces):
        copies_part += part_copies(piece, dec_hbm, part_refs[i], part_sems.at[i])
    src = lax.axis_index("src")
    for k in range(n):
        dest = peer(src, k, n)
        rows = acts_ref[lax.rem(dest, 2)]
        rows = rows.reshape(rows.shape[0] * rows.shape[1], rows.shape[2])
        columns = pl.ds(pl.multiple_of((dest // 2) * width, width), width)
        term_refs[k][...] = jnp.dot(
            rows, w_ref[:, columns], preferred_element_type=jnp.float32
        ).astype(jnp.bfloat16)
    for copy in copies_part:
        copy.wait()


def codes_kernel(n, share, tile_rows, active_ref, bias_ref, *refs):
    term_refs, out_ref = refs[:n], refs[n]
    src = lax.axis_index("src")
    tgt = lax.axis_index("tgt")
    parity, half = lax.rem(src, 2), src // 2
    block = out_ref.shape[2] // 2
    pre = term_refs[0][...].astype(jnp.float32)
    for ref in term_refs[1:]:
        pre = pre + ref[...].astype(jnp.float32)
    tiles, slots = active_ref.shape
    for piece in range(2):
        columns = slice(piece * block, (piece + 1) * block)
        bias = bias_ref[pl.ds(half * 2 + piece, 1), :]
        wanted = tgt * n + half * 2 + piece
        flags = []
        for tile in range(tiles):
            flags.append(
                lax.fori_loop(
                    0,
                    slots,
                    lambda i, total: total + (active_ref[tile, i] == wanted).astype(jnp.int32),
                    jnp.int32(0),
                    unroll=slots <= 16,
                )
            )
        for group in range(n // 2):
            tile = ((group * 2 + parity) * share) // tile_rows
            flag = flags[0]
            for i in range(1, tiles):
                flag = jnp.where(tile == i, flags[i], flag)
            live = jnp.where(flag > 0, 1.0, 0.0).astype(jnp.float32)
            rows = slice(group * share, (group + 1) * share)
            value = live * jnp.maximum(pre[rows, columns] + bias, 0.0)
            out_ref[group, :, columns] = value.astype(jnp.bfloat16)


def gather_kernel(n, *refs):
    half = n // 2
    code_refs, out_ref = refs[:-1], refs[-1]
    groups = len(code_refs) // 2
    src, tgt = lax.axis_index("src"), lax.axis_index("tgt")
    parity = lax.rem(src, 2)
    share, block = code_refs[0].shape[1], code_refs[0].shape[2] // 2
    for k in range(groups):
        place = lax.rem(tgt - k + groups, groups)
        for side in range(2):
            latents = parity if side == 0 else 1 - parity
            latents = pl.ds(pl.multiple_of(latents * block, block), block)
            columns = pl.ds(pl.multiple_of((side * groups + place) * block, block), block)
            for j in range(half):
                group = lax.rem(src // 2 + j, half)
                for r in range(2):
                    rows = slice((2 * j + r) * share, (2 * j + r + 1) * share)
                    out_ref[rows, columns] = code_refs[2 * k + r][group, :, latents]


def decode_kernel(n, piece, dec_ref, lhs_ref, got_ref, *refs):
    offsets, first, width, _ = piece
    layers, groups, block, cols = dec_ref.shape
    out_refs = refs[-2 * (n // 2) :]
    depth = groups * block
    share = lhs_ref.shape[0] // len(out_refs)
    start = pl.multiple_of(lax.axis_index("rep") * (cols // 2) + first, LANES)
    for i, offset in enumerate(offsets):
        own = dec_ref[layer_of(offset, layers), :, :, pl.ds(start, width)].reshape(depth, width)
        got = got_ref[i].reshape(depth, width)
        total = jnp.dot(lhs_ref[:, :depth], own, preferred_element_type=jnp.float32)
        total += jnp.dot(lhs_ref[:, depth:], got, preferred_element_type=jnp.float32)
        for j, ref in enumerate(out_refs):
            ref[i] = total[j * share : (j + 1) * share].astype(ref.dtype)


def add_kernel(n, pieces, bias_ref, target_ref, *refs):
    out_hbm, out_ref, sems = refs[-3:]
    half = n // 2
    layers, _, cols = target_ref.shape
    rep = lax.axis_index("rep")
    copies = []
    for i, (offsets, first, width, _) in enumerate(pieces):
        for side in range(2):
            core = rep if side == 0 else 1 - rep
            columns = pl.ds(pl.multiple_of(core * (cols // 2) + first, LANES), width)
            for j, offset in enumerate(offsets):
                layer = layer_of(offset, layers)
                total = bias_ref[0:1, columns]
                for other in range(1, layers):
                    total = jnp.where(layer == other, bias_ref[other : other + 1, columns], total)
                total = total - target_ref[layer, :, columns].astype(jnp.float32)
                mine = refs[2 * half * i : 2 * half * (i + 1)]
                first_sum = side * (half - 1)
                for ref in (*mine[first_sum : first_sum + half - 1], mine[-1 - side]):
                    total = total + ref[j].astype(jnp.float32)
                place = len(copies)
                out_ref[place, :, :width] = total.astype(jnp.bfloat16)
                copies.append(
                    pltpu.make_async_copy(
                        out_ref.at[place, :, :width], out_hbm.at[layer, :, columns], sems.at[place]
                    )
                )
                copies[-1].start()
    for copy in copies:
        copy.wait()


def body(acts, enc_w, enc_b, dec_w, dec_b, targets, active):
    n = lax.axis_size("src")
    rows, features = acts.shape
    layers, groups, block, cols = dec_w.shape
    share = rows // n
    half = n // 2
    pieces = cut_pieces(cols // 2)
    fetched = [piece for piece in pieces if not piece[3]]
    tile_rows = rows // active.shape[0]
    pair = [(i, i ^ 1) for i in range(n)]
    params = pltpu.CompilerParams(vmem_limit_bytes=VMEM_BYTES)
    vmem = pl.BlockSpec(memory_space=pltpu.VMEM)
    smem = pl.BlockSpec(memory_space=pltpu.SMEM)
    anywhere = pl.BlockSpec(memory_space=pl.ANY)
    def weight(billions):
        return pl.CostEstimate(
            flops=int(billions * 1e9), bytes_accessed=0, transcendentals=0
        )

    cost = weight(0)

    dec_rows = dec_w
    acts, enc_w, dec_w = (
        pltpu.with_memory_space_constraint(value, pltpu.HBM)
        for value in (acts.reshape(half, 2, share, features), enc_w, dec_w)
    )

    def shape(*extent, kind=jnp.bfloat16):
        return jax.ShapeDtypeStruct(extent, kind)

    results = pl.pallas_call(
        functools.partial(encode_kernel, n, fetched),
        out_shape=[shape(half * share, 2 * block)] * n
        + [shape(len(offsets), groups, block, width) for offsets, _, width, _ in fetched],
        in_specs=[anywhere] * 3,
        out_specs=[vmem] * (n + len(fetched)),
        scratch_shapes=[
            pltpu.VMEM((2, half, share, features), jnp.bfloat16),
            pltpu.VMEM(enc_w.shape, jnp.bfloat16),
            pltpu.SemaphoreType.DMA((len(fetched), layers * groups)),
            pltpu.SemaphoreType.DMA((2 * half,)),
            pltpu.SemaphoreType.DMA((8,)),
        ],
        compiler_params=params,
        cost_estimate=cost,
        name="encode",
    )(acts, enc_w, dec_w)
    terms, parts = list(results[:n]), list(results[n:])
    for k in range(1, n):
        terms[k] = lax.ppermute(terms[k], "src", [(i, peer(i, k, n)) for i in range(n)])
    order = [0, half, *(k for k in range(1, n) if k != half)]
    own = pl.pallas_call(
        functools.partial(codes_kernel, n, share, tile_rows),
        out_shape=shape(half, share, 2 * block),
        in_specs=[smem] + [vmem] * (1 + n),
        out_specs=vmem,
        compiler_params=params,
        cost_estimate=weight(20),
        name="codes",
    )(active, enc_b.reshape(n, block), *[terms[k] for k in order])
    codes = []
    for k in range(groups):
        perm = [(i, (i + k) % groups) for i in range(groups)]
        codes.append(lax.ppermute(own, "tgt", perm) if k else own)
        codes.append(lax.ppermute(codes[-1], "rep", [(0, 1), (1, 0)]))
    lhs = pl.pallas_call(
        functools.partial(gather_kernel, n),
        out_shape=shape(rows, 2 * groups * block),
        in_specs=[vmem] * len(codes),
        out_specs=vmem,
        compiler_params=params,
        cost_estimate=weight(20),
        name="gather",
    )(*codes)

    def hold(value, after):
        return pl.pallas_call(
            lambda *refs: None,
            out_shape=jax.ShapeDtypeStruct(value.shape, value.dtype),
            in_specs=[anywhere] * 2,
            out_specs=anywhere,
            input_output_aliases={0: 0},
            compiler_params=params,
            cost_estimate=cost,
            name="hold",
        )(value, after)

    got = [lax.ppermute(parts[0], "src", pair)]
    got.append(lax.ppermute(got[0], "parts", [(0, 1), (1, 0)]))
    got.append(lax.ppermute(hold(parts[1], own), "src", pair))

    def add(some, begun, billions):
        operands = [value for i in some for value in sums[i]]
        count = 2 * sum(len(pieces[i][0]) for i in some)
        widest = max(piece[2] for piece in pieces)
        return pl.pallas_call(
            functools.partial(add_kernel, n, [pieces[i] for i in some]),
            out_shape=shape(layers, share, cols),
            in_specs=[vmem] * (2 + len(operands)) + [anywhere] * len(begun),
            out_specs=anywhere,
            scratch_shapes=[
                pltpu.VMEM((count, share, widest), jnp.bfloat16),
                pltpu.SemaphoreType.DMA((count,)),
            ],
            input_output_aliases={2 + len(operands): 0} if begun else {},
            compiler_params=params,
            cost_estimate=weight(billions),
            name="add",
        )(dec_b, targets, *operands, *begun)

    sums, after = [], []
    for i, piece in enumerate(pieces):
        offsets, _, width, _ = piece
        shapes = [shape(len(offsets), share, width)] * (2 * half)
        shapes[0] = shape(len(offsets), share, width, kind=jnp.float32)
        terms = pl.pallas_call(
            functools.partial(decode_kernel, n, piece),
            out_shape=shapes,
            in_specs=[vmem] * 3 + [anywhere] * len(after),
            out_specs=[vmem] * len(shapes),
            compiler_params=params,
            cost_estimate=weight(0),
            name="decode",
        )(dec_rows, lhs, got[i], *after)
        after = [terms[0]]
        sums.append([])
        for r, j in [(r, j) for r in range(2) for j in range(1, half)] + [(1, 0)]:
            perm = [(d * 2 + c, (d + 2 * j) % n * 2 + (c ^ r)) for d in range(n) for c in range(2)]
            sums[i].append(lax.ppermute(terms[2 * j + r], ("src", "rep"), perm))
        sums[i].append(terms[0])

    begun = []
    begun = [add([0, 1], begun, 20)]
    return add([2], begun, 0)


def solution(mesh):
    in_specs = (
        P(("parts", "rep"), "src"),
        P("src", "tgt"),
        P("tgt"),
        P(None, None, "src", "tgt"),
        P(None, "tgt"),
        P(None, ("parts", "rep", "src"), "tgt"),
        P(("parts", "rep"), None),
    )
    out_specs = P(None, ("parts", "rep", "src"), "tgt")
    return jax.shard_map(body, mesh=mesh, in_specs=in_specs, out_specs=out_specs, check_vma=False)
```

```python
import functools

import jax
import jax.numpy as jnp
from jax import lax
from jax.experimental import pallas as pl
from jax.experimental.pallas import tpu as pltpu
from jax.sharding import PartitionSpec as P

VMEM_BYTES = 32 * 1024 * 1024
LANES = 128
FIRST = 6
PIECES = (((0,), 0, False), ((1,), 0, True), ((0, 1), 1, False))


def cut_pieces(columns):
    middle = columns // LANES * FIRST // 8 * LANES
    bounds = ((0, middle), (middle, columns))
    return [
        (layers, bounds[side][0], bounds[side][1] - bounds[side][0], across)
        for layers, side, across in PIECES
    ]


def layer_of(offset, layers):
    return lax.rem(lax.axis_index("parts") + offset, layers)


def peer(index, k, n):
    return index ^ k if n & (n - 1) == 0 else (index + k) % n


def part_copies(piece, dec_hbm, part_ref, sems):
    offsets, first, width, _ = piece
    layers, groups, _, cols = dec_hbm.shape
    start = pl.multiple_of(lax.axis_index("rep") * (cols // 2) + first, LANES)
    copies = []
    for i, offset in enumerate(offsets):
        for group in range(groups):
            source = dec_hbm.at[layer_of(offset, layers), group, :, pl.ds(start, width)]
            sem = sems.at[i * groups + group]
            copies.append(pltpu.make_async_copy(source, part_ref.at[i, group], sem))
            copies[-1].start()
    return copies


def encode_kernel(n, pieces, acts_hbm, w_hbm, dec_hbm, *refs):
    term_refs, part_refs, refs = refs[:n], refs[n:-5], refs[-5:]
    acts_ref, w_ref, part_sems, acts_sems, w_sems = refs
    half = n // 2
    width = w_ref.shape[1] // half
    depth = w_ref.shape[0] // 8
    copies = []
    for i in range(2):
        for j in range(half):
            copies.append(
                pltpu.make_async_copy(
                    acts_hbm.at[j, i], acts_ref.at[i, j], acts_sems.at[i * half + j]
                )
            )
    for i in range(8):
        rows = slice(i * depth, (i + 1) * depth)
        copies.append(pltpu.make_async_copy(w_hbm.at[rows], w_ref.at[rows], w_sems.at[i]))
    for copy in copies:
        copy.start()
    for copy in copies:
        copy.wait()
    copies_part = []
    for i, piece in enumerate(pieces):
        copies_part += part_copies(piece, dec_hbm, part_refs[i], part_sems.at[i])
    src = lax.axis_index("src")
    for k in range(n):
        dest = peer(src, k, n)
        rows = acts_ref[lax.rem(dest, 2)]
        rows = rows.reshape(rows.shape[0] * rows.shape[1], rows.shape[2])
        columns = pl.ds(pl.multiple_of((dest // 2) * width, width), width)
        term_refs[k][...] = jnp.dot(
            rows, w_ref[:, columns], preferred_element_type=jnp.float32
        ).astype(jnp.bfloat16)
    for copy in copies_part:
        copy.wait()


def codes_kernel(n, share, tile_rows, active_ref, bias_ref, *refs):
    term_refs, out_ref = refs[:n], refs[n]
    src = lax.axis_index("src")
    tgt = lax.axis_index("tgt")
    parity, half = lax.rem(src, 2), src // 2
    block = out_ref.shape[2] // 2
    pre = term_refs[0][...].astype(jnp.float32)
    for ref in term_refs[1:]:
        pre = pre + ref[...].astype(jnp.float32)
    tiles, slots = active_ref.shape
    for piece in range(2):
        columns = slice(piece * block, (piece + 1) * block)
        bias = bias_ref[pl.ds(half * 2 + piece, 1), :]
        wanted = tgt * n + half * 2 + piece
        flags = []
        for tile in range(tiles):
            flags.append(
                lax.fori_loop(
                    0,
                    slots,
                    lambda i, total: total + (active_ref[tile, i] == wanted).astype(jnp.int32),
                    jnp.int32(0),
                    unroll=slots <= 16,
                )
            )
        for group in range(n // 2):
            tile = ((group * 2 + parity) * share) // tile_rows
            flag = flags[0]
            for i in range(1, tiles):
                flag = jnp.where(tile == i, flags[i], flag)
            live = jnp.where(flag > 0, 1.0, 0.0).astype(jnp.float32)
            rows = slice(group * share, (group + 1) * share)
            value = live * jnp.maximum(pre[rows, columns] + bias, 0.0)
            out_ref[group, :, columns] = value.astype(jnp.bfloat16)


def gather_kernel(n, *refs):
    half = n // 2
    code_refs, out_ref = refs[:-1], refs[-1]
    groups = len(code_refs) // 2
    src, tgt = lax.axis_index("src"), lax.axis_index("tgt")
    parity = lax.rem(src, 2)
    share, block = code_refs[0].shape[1], code_refs[0].shape[2] // 2
    for k in range(groups):
        place = lax.rem(tgt - k + groups, groups)
        for side in range(2):
            latents = parity if side == 0 else 1 - parity
            latents = pl.ds(pl.multiple_of(latents * block, block), block)
            columns = pl.ds(pl.multiple_of((side * groups + place) * block, block), block)
            for j in range(half):
                group = lax.rem(src // 2 + j, half)
                for r in range(2):
                    rows = slice((2 * j + r) * share, (2 * j + r + 1) * share)
                    out_ref[rows, columns] = code_refs[2 * k + r][group, :, latents]


def decode_kernel(n, piece, dec_ref, lhs_ref, got_ref, *refs):
    offsets, first, width, _ = piece
    layers, groups, block, cols = dec_ref.shape
    out_refs = refs[-2 * (n // 2) :]
    depth = groups * block
    share = lhs_ref.shape[0] // len(out_refs)
    start = pl.multiple_of(lax.axis_index("rep") * (cols // 2) + first, LANES)
    for i, offset in enumerate(offsets):
        own = dec_ref[layer_of(offset, layers), :, :, pl.ds(start, width)].reshape(depth, width)
        got = got_ref[i].reshape(depth, width)
        total = jnp.dot(lhs_ref[:, :depth], own, preferred_element_type=jnp.float32)
        total += jnp.dot(lhs_ref[:, depth:], got, preferred_element_type=jnp.float32)
        for j, ref in enumerate(out_refs):
            ref[i] = total[j * share : (j + 1) * share].astype(ref.dtype)


def add_kernel(n, pieces, bias_ref, target_ref, *refs):
    out_hbm, out_ref, sems = refs[-3:]
    half = n // 2
    layers, _, cols = target_ref.shape
    rep = lax.axis_index("rep")
    copies = []
    for i, (offsets, first, width, _) in enumerate(pieces):
        for side in range(2):
            core = rep if side == 0 else 1 - rep
            columns = pl.ds(pl.multiple_of(core * (cols // 2) + first, LANES), width)
            for j, offset in enumerate(offsets):
                layer = layer_of(offset, layers)
                total = bias_ref[0:1, columns]
                for other in range(1, layers):
                    total = jnp.where(layer == other, bias_ref[other : other + 1, columns], total)
                total = total - target_ref[layer, :, columns].astype(jnp.float32)
                mine = refs[2 * half * i : 2 * half * (i + 1)]
                first_sum = side * (half - 1)
                for ref in (*mine[first_sum : first_sum + half - 1], mine[-1 - side]):
                    total = total + ref[j].astype(jnp.float32)
                place = len(copies)
                out_ref[place, :, :width] = total.astype(jnp.bfloat16)
                copies.append(
                    pltpu.make_async_copy(
                        out_ref.at[place, :, :width], out_hbm.at[layer, :, columns], sems.at[place]
                    )
                )
                copies[-1].start()
    for copy in copies:
        copy.wait()


def body(acts, enc_w, enc_b, dec_w, dec_b, targets, active):
    n = lax.axis_size("src")
    rows, features = acts.shape
    layers, groups, block, cols = dec_w.shape
    share = rows // n
    half = n // 2
    pieces = cut_pieces(cols // 2)
    fetched = [piece for piece in pieces if not piece[3]]
    tile_rows = rows // active.shape[0]
    pair = [(i, i ^ 1) for i in range(n)]
    params = pltpu.CompilerParams(vmem_limit_bytes=VMEM_BYTES)
    vmem = pl.BlockSpec(memory_space=pltpu.VMEM)
    smem = pl.BlockSpec(memory_space=pltpu.SMEM)
    anywhere = pl.BlockSpec(memory_space=pl.ANY)
    def weight(billions):
        return pl.CostEstimate(
            flops=int(billions * 1e9), bytes_accessed=0, transcendentals=0
        )

    cost = weight(0)

    dec_rows = dec_w
    acts, enc_w, dec_w = (
        pltpu.with_memory_space_constraint(value, pltpu.HBM)
        for value in (acts.reshape(half, 2, share, features), enc_w, dec_w)
    )

    def shape(*extent, kind=jnp.bfloat16):
        return jax.ShapeDtypeStruct(extent, kind)

    results = pl.pallas_call(
        functools.partial(encode_kernel, n, fetched),
        out_shape=[shape(half * share, 2 * block)] * n
        + [shape(len(offsets), groups, block, width) for offsets, _, width, _ in fetched],
        in_specs=[anywhere] * 3,
        out_specs=[vmem] * (n + len(fetched)),
        scratch_shapes=[
            pltpu.VMEM((2, half, share, features), jnp.bfloat16),
            pltpu.VMEM(enc_w.shape, jnp.bfloat16),
            pltpu.SemaphoreType.DMA((len(fetched), layers * groups)),
            pltpu.SemaphoreType.DMA((2 * half,)),
            pltpu.SemaphoreType.DMA((8,)),
        ],
        compiler_params=params,
        cost_estimate=cost,
        name="encode",
    )(acts, enc_w, dec_w)
    terms, parts = list(results[:n]), list(results[n:])
    for k in range(1, n):
        terms[k] = lax.ppermute(terms[k], "src", [(i, peer(i, k, n)) for i in range(n)])
    own = pl.pallas_call(
        functools.partial(codes_kernel, n, share, tile_rows),
        out_shape=shape(half, share, 2 * block),
        in_specs=[smem] + [vmem] * (1 + n),
        out_specs=vmem,
        compiler_params=params,
        cost_estimate=weight(20),
        name="codes",
    )(active, enc_b.reshape(n, block), *terms)
    codes = []
    for k in range(groups):
        for r in range(2):
            perm = [
                (i * 2 + c, (i + k) % groups * 2 + (c ^ r)) for i in range(groups) for c in range(2)
            ]
            codes.append(lax.ppermute(own, ("tgt", "rep"), perm) if k + r else own)

    lhs = pl.pallas_call(
        functools.partial(gather_kernel, n),
        out_shape=shape(rows, 2 * groups * block),
        in_specs=[vmem] * len(codes),
        out_specs=vmem,
        compiler_params=params,
        cost_estimate=weight(20),
        name="gather",
    )(*codes)

    def hold(value, after):
        return pl.pallas_call(
            lambda *refs: None,
            out_shape=jax.ShapeDtypeStruct(value.shape, value.dtype),
            in_specs=[anywhere] * 2,
            out_specs=anywhere,
            input_output_aliases={0: 0},
            compiler_params=params,
            cost_estimate=cost,
            name="hold",
        )(value, after)

    got = [lax.ppermute(parts[0], "src", pair)]
    got.append(lax.ppermute(got[0], "parts", [(0, 1), (1, 0)]))
    got.append(lax.ppermute(hold(parts[1], own), "src", pair))

    def add(some, begun, billions):
        operands = [value for i in some for value in sums[i]]
        count = 2 * sum(len(pieces[i][0]) for i in some)
        widest = max(piece[2] for piece in pieces)
        return pl.pallas_call(
            functools.partial(add_kernel, n, [pieces[i] for i in some]),
            out_shape=shape(layers, share, cols),
            in_specs=[vmem] * (2 + len(operands)) + [anywhere] * len(begun),
            out_specs=anywhere,
            scratch_shapes=[
                pltpu.VMEM((count, share, widest), jnp.bfloat16),
                pltpu.SemaphoreType.DMA((count,)),
            ],
            input_output_aliases={2 + len(operands): 0} if begun else {},
            compiler_params=params,
            cost_estimate=weight(billions),
            name="add",
        )(dec_b, targets, *operands, *begun)

    sums, after = [], []
    for i, piece in enumerate(pieces):
        offsets, _, width, _ = piece
        shapes = [shape(len(offsets), share, width)] * (2 * half)
        shapes[0] = shape(len(offsets), share, width, kind=jnp.float32)
        terms = pl.pallas_call(
            functools.partial(decode_kernel, n, piece),
            out_shape=shapes,
            in_specs=[vmem] * 3 + [anywhere] * len(after),
            out_specs=[vmem] * len(shapes),
            compiler_params=params,
            cost_estimate=weight(0),
            name="decode",
        )(dec_rows, lhs, got[i], *after)
        after = [terms[0]]
        sums.append([])
        for r, j in [(r, j) for r in range(2) for j in range(1, half)] + [(1, 0)]:
            perm = [(d * 2 + c, (d + 2 * j) % n * 2 + (c ^ r)) for d in range(n) for c in range(2)]
            sums[i].append(lax.ppermute(terms[2 * j + r], ("src", "rep"), perm))
        sums[i].append(terms[0])

    begun = []
    begun = [add([0, 1], begun, 20)]
    return add([2], begun, 0)


def solution(mesh):
    in_specs = (
        P(("parts", "rep"), "src"),
        P("src", "tgt"),
        P("tgt"),
        P(None, None, "src", "tgt"),
        P(None, "tgt"),
        P(None, ("parts", "rep", "src"), "tgt"),
        P(("parts", "rep"), None),
    )
    out_specs = P(None, ("parts", "rep", "src"), "tgt")
    return jax.shard_map(body, mesh=mesh, in_specs=in_specs, out_specs=out_specs, check_vma=False)
```

```python
import functools

import jax
import jax.numpy as jnp
from jax import lax
from jax.experimental import pallas as pl
from jax.experimental.pallas import tpu as pltpu
from jax.sharding import PartitionSpec as P

VMEM_BYTES = 32 * 1024 * 1024
LANES = 128
FIRST = 7
PIECES = (((0,), 0, False), ((1,), 0, True), ((0, 1), 1, False))


def cut_pieces(columns):
    middle = columns // LANES * FIRST // 8 * LANES
    bounds = ((0, middle), (middle, columns))
    return [
        (layers, bounds[side][0], bounds[side][1] - bounds[side][0], across)
        for layers, side, across in PIECES
    ]


def layer_of(offset, layers):
    return lax.rem(lax.axis_index("parts") + offset, layers)


def peer(index, k, n):
    return index ^ k if n & (n - 1) == 0 else (index + k) % n


def part_copies(piece, dec_hbm, part_ref, sems):
    offsets, first, width, _ = piece
    layers, groups, _, cols = dec_hbm.shape
    start = pl.multiple_of(lax.axis_index("rep") * (cols // 2) + first, LANES)
    copies = []
    for i, offset in enumerate(offsets):
        for group in range(groups):
            source = dec_hbm.at[layer_of(offset, layers), group, :, pl.ds(start, width)]
            sem = sems.at[i * groups + group]
            copies.append(pltpu.make_async_copy(source, part_ref.at[i, group], sem))
            copies[-1].start()
    return copies


def encode_kernel(n, pieces, acts_hbm, w_hbm, dec_hbm, *refs):
    term_refs, part_refs, refs = refs[:n], refs[n:-5], refs[-5:]
    acts_ref, w_ref, part_sems, acts_sems, w_sems = refs
    half = n // 2
    width = w_ref.shape[1] // half
    depth = w_ref.shape[0] // 8
    copies = []
    for i in range(2):
        for j in range(half):
            copies.append(
                pltpu.make_async_copy(
                    acts_hbm.at[j, i], acts_ref.at[i, j], acts_sems.at[i * half + j]
                )
            )
    for i in range(8):
        rows = slice(i * depth, (i + 1) * depth)
        copies.append(pltpu.make_async_copy(w_hbm.at[rows], w_ref.at[rows], w_sems.at[i]))
    for copy in copies:
        copy.start()
    for copy in copies:
        copy.wait()
    copies_part = []
    for i, piece in enumerate(pieces):
        copies_part += part_copies(piece, dec_hbm, part_refs[i], part_sems.at[i])
    src = lax.axis_index("src")
    for k in range(n):
        dest = peer(src, k, n)
        rows = acts_ref[lax.rem(dest, 2)]
        rows = rows.reshape(rows.shape[0] * rows.shape[1], rows.shape[2])
        columns = pl.ds(pl.multiple_of((dest // 2) * width, width), width)
        term_refs[k][...] = jnp.dot(
            rows, w_ref[:, columns], preferred_element_type=jnp.float32
        ).astype(jnp.bfloat16)
    for copy in copies_part:
        copy.wait()


def codes_kernel(n, share, tile_rows, active_ref, bias_ref, *refs):
    term_refs, out_ref = refs[:n], refs[n]
    src = lax.axis_index("src")
    tgt = lax.axis_index("tgt")
    parity, half = lax.rem(src, 2), src // 2
    block = out_ref.shape[2] // 2
    pre = term_refs[0][...].astype(jnp.float32)
    for ref in term_refs[1:]:
        pre = pre + ref[...].astype(jnp.float32)
    tiles, slots = active_ref.shape
    for piece in range(2):
        columns = slice(piece * block, (piece + 1) * block)
        bias = bias_ref[pl.ds(half * 2 + piece, 1), :]
        wanted = tgt * n + half * 2 + piece
        flags = []
        for tile in range(tiles):
            flags.append(
                lax.fori_loop(
                    0,
                    slots,
                    lambda i, total: total + (active_ref[tile, i] == wanted).astype(jnp.int32),
                    jnp.int32(0),
                    unroll=slots <= 16,
                )
            )
        for group in range(n // 2):
            tile = ((group * 2 + parity) * share) // tile_rows
            flag = flags[0]
            for i in range(1, tiles):
                flag = jnp.where(tile == i, flags[i], flag)
            live = jnp.where(flag > 0, 1.0, 0.0).astype(jnp.float32)
            rows = slice(group * share, (group + 1) * share)
            value = live * jnp.maximum(pre[rows, columns] + bias, 0.0)
            out_ref[group, :, columns] = value.astype(jnp.bfloat16)


def gather_kernel(n, *refs):
    half = n // 2
    code_refs, out_ref = refs[:-1], refs[-1]
    groups = len(code_refs) // 2
    src, tgt = lax.axis_index("src"), lax.axis_index("tgt")
    parity = lax.rem(src, 2)
    share, block = code_refs[0].shape[1], code_refs[0].shape[2] // 2
    for k in range(groups):
        place = lax.rem(tgt - k + groups, groups)
        for side in range(2):
            latents = parity if side == 0 else 1 - parity
            latents = pl.ds(pl.multiple_of(latents * block, block), block)
            columns = pl.ds(pl.multiple_of((side * groups + place) * block, block), block)
            for j in range(half):
                group = lax.rem(src // 2 + j, half)
                for r in range(2):
                    rows = slice((2 * j + r) * share, (2 * j + r + 1) * share)
                    out_ref[rows, columns] = code_refs[2 * k + r][group, :, latents]


def decode_kernel(n, piece, dec_ref, lhs_ref, got_ref, *refs):
    offsets, first, width, _ = piece
    layers, groups, block, cols = dec_ref.shape
    out_refs = refs[-2 * (n // 2) :]
    depth = groups * block
    share = lhs_ref.shape[0] // len(out_refs)
    start = pl.multiple_of(lax.axis_index("rep") * (cols // 2) + first, LANES)
    for i, offset in enumerate(offsets):
        own = dec_ref[layer_of(offset, layers), :, :, pl.ds(start, width)].reshape(depth, width)
        got = got_ref[i].reshape(depth, width)
        total = jnp.dot(lhs_ref[:, :depth], own, preferred_element_type=jnp.float32)
        total += jnp.dot(lhs_ref[:, depth:], got, preferred_element_type=jnp.float32)
        for j, ref in enumerate(out_refs):
            ref[i] = total[j * share : (j + 1) * share].astype(ref.dtype)


def add_kernel(n, pieces, bias_ref, target_ref, *refs):
    out_hbm, out_ref, sems = refs[-3:]
    half = n // 2
    layers, _, cols = target_ref.shape
    rep = lax.axis_index("rep")
    copies = []
    for i, (offsets, first, width, _) in enumerate(pieces):
        for side in range(2):
            core = rep if side == 0 else 1 - rep
            columns = pl.ds(pl.multiple_of(core * (cols // 2) + first, LANES), width)
            for j, offset in enumerate(offsets):
                layer = layer_of(offset, layers)
                total = bias_ref[0:1, columns]
                for other in range(1, layers):
                    total = jnp.where(layer == other, bias_ref[other : other + 1, columns], total)
                total = total - target_ref[layer, :, columns].astype(jnp.float32)
                mine = refs[2 * half * i : 2 * half * (i + 1)]
                first_sum = side * (half - 1)
                for ref in (*mine[first_sum : first_sum + half - 1], mine[-1 - side]):
                    total = total + ref[j].astype(jnp.float32)
                place = len(copies)
                out_ref[place, :, :width] = total.astype(jnp.bfloat16)
                copies.append(
                    pltpu.make_async_copy(
                        out_ref.at[place, :, :width], out_hbm.at[layer, :, columns], sems.at[place]
                    )
                )
                copies[-1].start()
    for copy in copies:
        copy.wait()


def body(acts, enc_w, enc_b, dec_w, dec_b, targets, active):
    n = lax.axis_size("src")
    rows, features = acts.shape
    layers, groups, block, cols = dec_w.shape
    share = rows // n
    half = n // 2
    pieces = cut_pieces(cols // 2)
    fetched = [piece for piece in pieces if not piece[3]]
    tile_rows = rows // active.shape[0]
    pair = [(i, i ^ 1) for i in range(n)]
    params = pltpu.CompilerParams(vmem_limit_bytes=VMEM_BYTES)
    vmem = pl.BlockSpec(memory_space=pltpu.VMEM)
    smem = pl.BlockSpec(memory_space=pltpu.SMEM)
    anywhere = pl.BlockSpec(memory_space=pl.ANY)
    def weight(billions):
        return pl.CostEstimate(
            flops=int(billions * 1e9), bytes_accessed=0, transcendentals=0
        )

    cost = weight(0)

    dec_rows = dec_w
    acts, enc_w, dec_w = (
        pltpu.with_memory_space_constraint(value, pltpu.HBM)
        for value in (acts.reshape(half, 2, share, features), enc_w, dec_w)
    )

    def shape(*extent, kind=jnp.bfloat16):
        return jax.ShapeDtypeStruct(extent, kind)

    results = pl.pallas_call(
        functools.partial(encode_kernel, n, fetched),
        out_shape=[shape(half * share, 2 * block)] * n
        + [shape(len(offsets), groups, block, width) for offsets, _, width, _ in fetched],
        in_specs=[anywhere] * 3,
        out_specs=[vmem] * (n + len(fetched)),
        scratch_shapes=[
            pltpu.VMEM((2, half, share, features), jnp.bfloat16),
            pltpu.VMEM(enc_w.shape, jnp.bfloat16),
            pltpu.SemaphoreType.DMA((len(fetched), layers * groups)),
            pltpu.SemaphoreType.DMA((2 * half,)),
            pltpu.SemaphoreType.DMA((8,)),
        ],
        compiler_params=params,
        cost_estimate=cost,
        name="encode",
    )(acts, enc_w, dec_w)
    terms, parts = list(results[:n]), list(results[n:])
    for k in range(1, n):
        terms[k] = lax.ppermute(terms[k], "src", [(i, peer(i, k, n)) for i in range(n)])
    own = pl.pallas_call(
        functools.partial(codes_kernel, n, share, tile_rows),
        out_shape=shape(half, share, 2 * block),
        in_specs=[smem] + [vmem] * (1 + n),
        out_specs=vmem,
        compiler_params=params,
        cost_estimate=weight(20),
        name="codes",
    )(active, enc_b.reshape(n, block), *terms)
    codes = []
    for k in range(groups):
        for r in range(2):
            perm = [
                (i * 2 + c, (i + k) % groups * 2 + (c ^ r)) for i in range(groups) for c in range(2)
            ]
            codes.append(lax.ppermute(own, ("tgt", "rep"), perm) if k + r else own)

    lhs = pl.pallas_call(
        functools.partial(gather_kernel, n),
        out_shape=shape(rows, 2 * groups * block),
        in_specs=[vmem] * len(codes),
        out_specs=vmem,
        compiler_params=params,
        cost_estimate=weight(20),
        name="gather",
    )(*codes)

    def hold(value, after):
        return pl.pallas_call(
            lambda *refs: None,
            out_shape=jax.ShapeDtypeStruct(value.shape, value.dtype),
            in_specs=[anywhere] * 2,
            out_specs=anywhere,
            input_output_aliases={0: 0},
            compiler_params=params,
            cost_estimate=cost,
            name="hold",
        )(value, after)

    got = [lax.ppermute(parts[0], "src", pair)]
    got.append(lax.ppermute(got[0], "parts", [(0, 1), (1, 0)]))
    got.append(lax.ppermute(hold(parts[1], own), "src", pair))

    def add(some, begun, billions):
        operands = [value for i in some for value in sums[i]]
        count = 2 * sum(len(pieces[i][0]) for i in some)
        widest = max(piece[2] for piece in pieces)
        return pl.pallas_call(
            functools.partial(add_kernel, n, [pieces[i] for i in some]),
            out_shape=shape(layers, share, cols),
            in_specs=[vmem] * (2 + len(operands)) + [anywhere] * len(begun),
            out_specs=anywhere,
            scratch_shapes=[
                pltpu.VMEM((count, share, widest), jnp.bfloat16),
                pltpu.SemaphoreType.DMA((count,)),
            ],
            input_output_aliases={2 + len(operands): 0} if begun else {},
            compiler_params=params,
            cost_estimate=weight(billions),
            name="add",
        )(dec_b, targets, *operands, *begun)

    sums, after = [], []
    for i, piece in enumerate(pieces):
        offsets, _, width, _ = piece
        shapes = [shape(len(offsets), share, width)] * (2 * half)
        shapes[0] = shape(len(offsets), share, width, kind=jnp.float32)
        terms = pl.pallas_call(
            functools.partial(decode_kernel, n, piece),
            out_shape=shapes,
            in_specs=[vmem] * 3 + [anywhere] * len(after),
            out_specs=[vmem] * len(shapes),
            compiler_params=params,
            cost_estimate=weight(0),
            name="decode",
        )(dec_rows, lhs, got[i], *after)
        after = [terms[0]]
        sums.append([])
        for r, j in [(r, j) for r in range(2) for j in range(1, half)] + [(1, 0)]:
            perm = [(d * 2 + c, (d + 2 * j) % n * 2 + (c ^ r)) for d in range(n) for c in range(2)]
            sums[i].append(lax.ppermute(terms[2 * j + r], ("src", "rep"), perm))
        sums[i].append(terms[0])

    begun = []
    begun = [add([0, 1], begun, 20)]
    return add([2], begun, 0)


def solution(mesh):
    in_specs = (
        P(("parts", "rep"), "src"),
        P("src", "tgt"),
        P("tgt"),
        P(None, None, "src", "tgt"),
        P(None, "tgt"),
        P(None, ("parts", "rep", "src"), "tgt"),
        P(("parts", "rep"), None),
    )
    out_specs = P(None, ("parts", "rep", "src"), "tgt")
    return jax.shard_map(body, mesh=mesh, in_specs=in_specs, out_specs=out_specs, check_vma=False)
```

```python
import functools

import jax
import jax.numpy as jnp
from jax import lax
from jax.experimental import pallas as pl
from jax.experimental.pallas import tpu as pltpu
from jax.sharding import PartitionSpec as P

VMEM_BYTES = 32 * 1024 * 1024
LANES = 128
FIRST = 6
PIECES = (((0,), 0, False), ((1,), 0, True), ((0, 1), 1, False))


def cut_pieces(columns):
    middle = columns // LANES * FIRST // 8 * LANES
    bounds = ((0, middle), (middle, columns))
    return [
        (layers, bounds[side][0], bounds[side][1] - bounds[side][0], across)
        for layers, side, across in PIECES
    ]


def layer_of(offset, layers):
    return lax.rem(lax.axis_index("parts") + offset, layers)


def peer(index, k, n):
    return index ^ k if n & (n - 1) == 0 else (index + k) % n


def part_copies(piece, dec_hbm, part_ref, sems):
    offsets, first, width, _ = piece
    layers, groups, _, cols = dec_hbm.shape
    start = pl.multiple_of(lax.axis_index("rep") * (cols // 2) + first, LANES)
    copies = []
    for i, offset in enumerate(offsets):
        for group in range(groups):
            source = dec_hbm.at[layer_of(offset, layers), group, :, pl.ds(start, width)]
            sem = sems.at[i * groups + group]
            copies.append(pltpu.make_async_copy(source, part_ref.at[i, group], sem))
            copies[-1].start()
    return copies


def encode_kernel(n, pieces, acts_hbm, w_hbm, dec_hbm, *refs):
    term_refs, part_refs, refs = refs[:n], refs[n:-5], refs[-5:]
    acts_ref, w_ref, part_sems, acts_sems, w_sems = refs
    half = n // 2
    width = w_ref.shape[1] // half
    depth = w_ref.shape[0] // 8
    copies = []
    for i in range(2):
        for j in range(half):
            copies.append(
                pltpu.make_async_copy(
                    acts_hbm.at[j, i], acts_ref.at[i, j], acts_sems.at[i * half + j]
                )
            )
    for i in range(8):
        rows = slice(i * depth, (i + 1) * depth)
        copies.append(pltpu.make_async_copy(w_hbm.at[rows], w_ref.at[rows], w_sems.at[i]))
    for copy in copies:
        copy.start()
    for copy in copies:
        copy.wait()
    copies_part = []
    for i, piece in enumerate(pieces):
        copies_part += part_copies(piece, dec_hbm, part_refs[i], part_sems.at[i])
    src = lax.axis_index("src")
    for k in range(n):
        dest = peer(src, k, n)
        rows = acts_ref[lax.rem(dest, 2)]
        rows = rows.reshape(rows.shape[0] * rows.shape[1], rows.shape[2])
        columns = pl.ds(pl.multiple_of((dest // 2) * width, width), width)
        term_refs[k][...] = jnp.dot(
            rows, w_ref[:, columns], preferred_element_type=jnp.float32
        ).astype(jnp.bfloat16)
    for copy in copies_part:
        copy.wait()


def part_kernel(piece, before_ref, dec_hbm, after_ref, part_ref, sems):
    for copy in part_copies(piece, dec_hbm, part_ref, sems):
        copy.wait()


def codes_kernel(n, share, tile_rows, active_ref, bias_ref, *refs):
    term_refs, out_ref = refs[:n], refs[n]
    src = lax.axis_index("src")
    tgt = lax.axis_index("tgt")
    parity, half = lax.rem(src, 2), src // 2
    block = out_ref.shape[2] // 2
    pre = term_refs[0][...].astype(jnp.float32)
    for ref in term_refs[1:]:
        pre = pre + ref[...].astype(jnp.float32)
    tiles, slots = active_ref.shape
    for piece in range(2):
        columns = slice(piece * block, (piece + 1) * block)
        bias = bias_ref[pl.ds(half * 2 + piece, 1), :]
        wanted = tgt * n + half * 2 + piece
        flags = []
        for tile in range(tiles):
            flags.append(
                lax.fori_loop(
                    0,
                    slots,
                    lambda i, total: total + (active_ref[tile, i] == wanted).astype(jnp.int32),
                    jnp.int32(0),
                    unroll=slots <= 16,
                )
            )
        for group in range(n // 2):
            tile = ((group * 2 + parity) * share) // tile_rows
            flag = flags[0]
            for i in range(1, tiles):
                flag = jnp.where(tile == i, flags[i], flag)
            live = jnp.where(flag > 0, 1.0, 0.0).astype(jnp.float32)
            rows = slice(group * share, (group + 1) * share)
            value = live * jnp.maximum(pre[rows, columns] + bias, 0.0)
            out_ref[group, :, columns] = value.astype(jnp.bfloat16)


def gather_kernel(n, *refs):
    half = n // 2
    code_refs, out_ref = refs[:-1], refs[-1]
    groups = len(code_refs) // 2
    src, tgt = lax.axis_index("src"), lax.axis_index("tgt")
    parity = lax.rem(src, 2)
    share, block = code_refs[0].shape[1], code_refs[0].shape[2] // 2
    for k in range(groups):
        place = lax.rem(tgt - k + groups, groups)
        for side in range(2):
            latents = parity if side == 0 else 1 - parity
            latents = pl.ds(pl.multiple_of(latents * block, block), block)
            columns = pl.ds(pl.multiple_of((side * groups + place) * block, block), block)
            for j in range(half):
                group = lax.rem(src // 2 + j, half)
                for r in range(2):
                    rows = slice((2 * j + r) * share, (2 * j + r + 1) * share)
                    out_ref[rows, columns] = code_refs[2 * k + r][group, :, latents]


def decode_kernel(n, piece, dec_ref, lhs_ref, got_ref, *refs):
    offsets, first, width, _ = piece
    layers, groups, block, cols = dec_ref.shape
    out_refs = refs[-2 * (n // 2) :]
    depth = groups * block
    share = lhs_ref.shape[0] // len(out_refs)
    start = pl.multiple_of(lax.axis_index("rep") * (cols // 2) + first, LANES)
    for i, offset in enumerate(offsets):
        own = dec_ref[layer_of(offset, layers), :, :, pl.ds(start, width)].reshape(depth, width)
        got = got_ref[i].reshape(depth, width)
        total = jnp.dot(lhs_ref[:, :depth], own, preferred_element_type=jnp.float32)
        total += jnp.dot(lhs_ref[:, depth:], got, preferred_element_type=jnp.float32)
        for j, ref in enumerate(out_refs):
            ref[i] = total[j * share : (j + 1) * share].astype(ref.dtype)


def add_kernel(n, pieces, bias_ref, target_ref, *refs):
    out_hbm, out_ref, sems = refs[-3:]
    half = n // 2
    layers, _, cols = target_ref.shape
    rep = lax.axis_index("rep")
    copies = []
    for i, (offsets, first, width, _) in enumerate(pieces):
        for side in range(2):
            core = rep if side == 0 else 1 - rep
            columns = pl.ds(pl.multiple_of(core * (cols // 2) + first, LANES), width)
            for j, offset in enumerate(offsets):
                layer = layer_of(offset, layers)
                total = bias_ref[0:1, columns]
                for other in range(1, layers):
                    total = jnp.where(layer == other, bias_ref[other : other + 1, columns], total)
                total = total - target_ref[layer, :, columns].astype(jnp.float32)
                mine = refs[2 * half * i : 2 * half * (i + 1)]
                first_sum = side * (half - 1)
                for ref in (*mine[first_sum : first_sum + half - 1], mine[-1 - side]):
                    total = total + ref[j].astype(jnp.float32)
                place = len(copies)
                out_ref[place, :, :width] = total.astype(jnp.bfloat16)
                copies.append(
                    pltpu.make_async_copy(
                        out_ref.at[place, :, :width], out_hbm.at[layer, :, columns], sems.at[place]
                    )
                )
                copies[-1].start()
    for copy in copies:
        copy.wait()


def body(acts, enc_w, enc_b, dec_w, dec_b, targets, active):
    n = lax.axis_size("src")
    rows, features = acts.shape
    layers, groups, block, cols = dec_w.shape
    share = rows // n
    half = n // 2
    pieces = cut_pieces(cols // 2)
    fetched = [piece for piece in pieces if not piece[3]]
    tile_rows = rows // active.shape[0]
    pair = [(i, i ^ 1) for i in range(n)]
    params = pltpu.CompilerParams(vmem_limit_bytes=VMEM_BYTES)
    vmem = pl.BlockSpec(memory_space=pltpu.VMEM)
    smem = pl.BlockSpec(memory_space=pltpu.SMEM)
    anywhere = pl.BlockSpec(memory_space=pl.ANY)
    def weight(billions):
        return pl.CostEstimate(
            flops=int(billions * 1e9), bytes_accessed=0, transcendentals=0
        )

    cost = weight(0)

    dec_rows = dec_w
    acts, enc_w, dec_w = (
        pltpu.with_memory_space_constraint(value, pltpu.HBM)
        for value in (acts.reshape(half, 2, share, features), enc_w, dec_w)
    )

    def shape(*extent, kind=jnp.bfloat16):
        return jax.ShapeDtypeStruct(extent, kind)

    results = pl.pallas_call(
        functools.partial(encode_kernel, n, fetched[:1]),
        out_shape=[shape(half * share, 2 * block)] * n
        + [shape(len(offsets), groups, block, width) for offsets, _, width, _ in fetched[:1]],
        in_specs=[anywhere] * 3,
        out_specs=[vmem] * (n + 1),
        scratch_shapes=[
            pltpu.VMEM((2, half, share, features), jnp.bfloat16),
            pltpu.VMEM(enc_w.shape, jnp.bfloat16),
            pltpu.SemaphoreType.DMA((1, layers * groups)),
            pltpu.SemaphoreType.DMA((2 * half,)),
            pltpu.SemaphoreType.DMA((8,)),
        ],
        compiler_params=params,
        cost_estimate=cost,
        name="encode",
    )(acts, enc_w, dec_w)
    terms, parts = list(results[:n]), list(results[n:])
    for k in range(1, n):
        terms[k] = lax.ppermute(terms[k], "src", [(i, peer(i, k, n)) for i in range(n)])
    order = range(n)
    own = pl.pallas_call(
        functools.partial(codes_kernel, n, share, tile_rows),
        out_shape=shape(half, share, 2 * block),
        in_specs=[smem] + [vmem] * (1 + n),
        out_specs=vmem,
        compiler_params=params,
        cost_estimate=weight(20),
        name="codes",
    )(active, enc_b.reshape(n, block), *[terms[k] for k in order])
    codes = []
    for k in range(groups):
        for r in range(2):
            perm = [
                (i * 2 + c, (i + k) % groups * 2 + (c ^ r)) for i in range(groups) for c in range(2)
            ]
            codes.append(lax.ppermute(own, ("tgt", "rep"), perm) if k + r else own)

    lhs = pl.pallas_call(
        functools.partial(gather_kernel, n),
        out_shape=shape(rows, 2 * groups * block),
        in_specs=[vmem] * len(codes),
        out_specs=vmem,
        compiler_params=params,
        cost_estimate=weight(20),
        name="gather",
    )(*codes)

    part = pl.pallas_call(
        functools.partial(part_kernel, fetched[1]),
        out_shape=shape(len(fetched[1][0]), groups, block, fetched[1][2]),
        in_specs=[anywhere] * 3,
        out_specs=vmem,
        scratch_shapes=[pltpu.SemaphoreType.DMA((layers * groups,))],
        compiler_params=params,
        cost_estimate=weight(0),
        name="part",
    )(parts[0], dec_w, own)

    got = [lax.ppermute(parts[0], "src", pair)]
    got.append(lax.ppermute(got[0], "parts", [(0, 1), (1, 0)]))
    got.append(lax.ppermute(part, "src", pair))

    def add(some, begun, billions):
        operands = [value for i in some for value in sums[i]]
        count = 2 * sum(len(pieces[i][0]) for i in some)
        widest = max(piece[2] for piece in pieces)
        return pl.pallas_call(
            functools.partial(add_kernel, n, [pieces[i] for i in some]),
            out_shape=shape(layers, share, cols),
            in_specs=[vmem] * (2 + len(operands)) + [anywhere] * len(begun),
            out_specs=anywhere,
            scratch_shapes=[
                pltpu.VMEM((count, share, widest), jnp.bfloat16),
                pltpu.SemaphoreType.DMA((count,)),
            ],
            input_output_aliases={2 + len(operands): 0} if begun else {},
            compiler_params=params,
            cost_estimate=weight(billions),
            name="add",
        )(dec_b, targets, *operands, *begun)

    sums, after = [], []
    for i, piece in enumerate(pieces):
        offsets, _, width, _ = piece
        shapes = [shape(len(offsets), share, width)] * (2 * half)
        shapes[0] = shape(len(offsets), share, width, kind=jnp.float32)
        terms = pl.pallas_call(
            functools.partial(decode_kernel, n, piece),
            out_shape=shapes,
            in_specs=[vmem] * 3 + [anywhere] * len(after),
            out_specs=[vmem] * len(shapes),
            compiler_params=params,
            cost_estimate=weight(0),
            name="decode",
        )(dec_rows, lhs, got[i], *after)
        after = [terms[0]]
        sums.append([])
        for r, j in [(r, j) for r in range(2) for j in range(1, half)] + [(1, 0)]:
            perm = [(d * 2 + c, (d + 2 * j) % n * 2 + (c ^ r)) for d in range(n) for c in range(2)]
            sums[i].append(lax.ppermute(terms[2 * j + r], ("src", "rep"), perm))
        sums[i].append(terms[0])

    begun = []
    begun = [add([0, 1], begun, 20)]
    return add([2], begun, 0)


def solution(mesh):
    in_specs = (
        P(("parts", "rep"), "src"),
        P("src", "tgt"),
        P("tgt"),
        P(None, None, "src", "tgt"),
        P(None, "tgt"),
        P(None, ("parts", "rep", "src"), "tgt"),
        P(("parts", "rep"), None),
    )
    out_specs = P(None, ("parts", "rep", "src"), "tgt")
    return jax.shard_map(body, mesh=mesh, in_specs=in_specs, out_specs=out_specs, check_vma=False)
```

```python
import functools

import jax
import jax.numpy as jnp
from jax import lax
from jax.experimental import pallas as pl
from jax.experimental.pallas import tpu as pltpu
from jax.sharding import PartitionSpec as P

VMEM_BYTES = 32 * 1024 * 1024
LANES = 128
FIRST = 6
PIECES = (((0,), 0, False), ((1,), 0, True), ((0, 1), 1, False))


def cut_pieces(columns):
    middle = columns // LANES * FIRST // 8 * LANES
    bounds = ((0, middle), (middle, columns))
    return [
        (layers, bounds[side][0], bounds[side][1] - bounds[side][0], across)
        for layers, side, across in PIECES
    ]


def layer_of(offset, layers):
    return lax.rem(lax.axis_index("parts") + offset, layers)


def peer(index, k, n):
    return index ^ k if n & (n - 1) == 0 else (index + k) % n


def part_copies(piece, dec_hbm, part_ref, sems):
    offsets, first, width, _ = piece
    layers, groups, _, cols = dec_hbm.shape
    start = pl.multiple_of(lax.axis_index("rep") * (cols // 2) + first, LANES)
    copies = []
    for i, offset in enumerate(offsets):
        for group in range(groups):
            source = dec_hbm.at[layer_of(offset, layers), group, :, pl.ds(start, width)]
            sem = sems.at[i * groups + group]
            copies.append(pltpu.make_async_copy(source, part_ref.at[i, group], sem))
            copies[-1].start()
    return copies


def encode_kernel(n, pieces, acts_hbm, w_hbm, dec_hbm, *refs):
    term_refs, part_refs, refs = refs[:n], refs[n:-5], refs[-5:]
    acts_ref, w_ref, part_sems, acts_sems, w_sems = refs
    half = n // 2
    width = w_ref.shape[1] // half
    depth = w_ref.shape[0] // 8
    copies = []
    for i in range(2):
        for j in range(half):
            copies.append(
                pltpu.make_async_copy(
                    acts_hbm.at[j, i], acts_ref.at[i, j], acts_sems.at[i * half + j]
                )
            )
    for i in range(8):
        rows = slice(i * depth, (i + 1) * depth)
        copies.append(pltpu.make_async_copy(w_hbm.at[rows], w_ref.at[rows], w_sems.at[i]))
    for copy in copies:
        copy.start()
    copies_part = []
    for i, piece in enumerate(pieces):
        copies_part += part_copies(piece, dec_hbm, part_refs[i], part_sems.at[i])
    for copy in copies:
        copy.wait()
    src = lax.axis_index("src")
    for k in range(n):
        dest = peer(src, k, n)
        rows = acts_ref[lax.rem(dest, 2)]
        rows = rows.reshape(rows.shape[0] * rows.shape[1], rows.shape[2])
        columns = pl.ds(pl.multiple_of((dest // 2) * width, width), width)
        term_refs[k][...] = jnp.dot(
            rows, w_ref[:, columns], preferred_element_type=jnp.float32
        ).astype(jnp.bfloat16)
    for copy in copies_part:
        copy.wait()


def part_kernel(piece, before_ref, dec_hbm, after_ref, part_ref, sems):
    for copy in part_copies(piece, dec_hbm, part_ref, sems):
        copy.wait()


def codes_kernel(n, share, tile_rows, active_ref, bias_ref, *refs):
    term_refs, out_ref = refs[:n], refs[n]
    src = lax.axis_index("src")
    tgt = lax.axis_index("tgt")
    parity, half = lax.rem(src, 2), src // 2
    block = out_ref.shape[2] // 2
    pre = term_refs[0][...].astype(jnp.float32)
    for ref in term_refs[1:]:
        pre = pre + ref[...].astype(jnp.float32)
    tiles, slots = active_ref.shape
    for piece in range(2):
        columns = slice(piece * block, (piece + 1) * block)
        bias = bias_ref[pl.ds(half * 2 + piece, 1), :]
        wanted = tgt * n + half * 2 + piece
        flags = []
        for tile in range(tiles):
            flags.append(
                lax.fori_loop(
                    0,
                    slots,
                    lambda i, total: total + (active_ref[tile, i] == wanted).astype(jnp.int32),
                    jnp.int32(0),
                    unroll=slots <= 16,
                )
            )
        for group in range(n // 2):
            tile = ((group * 2 + parity) * share) // tile_rows
            flag = flags[0]
            for i in range(1, tiles):
                flag = jnp.where(tile == i, flags[i], flag)
            live = jnp.where(flag > 0, 1.0, 0.0).astype(jnp.float32)
            rows = slice(group * share, (group + 1) * share)
            value = live * jnp.maximum(pre[rows, columns] + bias, 0.0)
            out_ref[group, :, columns] = value.astype(jnp.bfloat16)


def gather_kernel(n, *refs):
    half = n // 2
    code_refs, out_ref = refs[:-1], refs[-1]
    groups = len(code_refs) // 2
    src, tgt = lax.axis_index("src"), lax.axis_index("tgt")
    parity = lax.rem(src, 2)
    share, block = code_refs[0].shape[1], code_refs[0].shape[2] // 2
    for k in range(groups):
        place = lax.rem(tgt - k + groups, groups)
        for side in range(2):
            latents = parity if side == 0 else 1 - parity
            latents = pl.ds(pl.multiple_of(latents * block, block), block)
            columns = pl.ds(pl.multiple_of((side * groups + place) * block, block), block)
            for j in range(half):
                group = lax.rem(src // 2 + j, half)
                for r in range(2):
                    rows = slice((2 * j + r) * share, (2 * j + r + 1) * share)
                    out_ref[rows, columns] = code_refs[2 * k + r][group, :, latents]


def decode_kernel(n, piece, dec_ref, lhs_ref, got_ref, *refs):
    offsets, first, width, _ = piece
    layers, groups, block, cols = dec_ref.shape
    out_refs = refs[-2 * (n // 2) :]
    depth = groups * block
    share = lhs_ref.shape[0] // len(out_refs)
    start = pl.multiple_of(lax.axis_index("rep") * (cols // 2) + first, LANES)
    for i, offset in enumerate(offsets):
        own = dec_ref[layer_of(offset, layers), :, :, pl.ds(start, width)].reshape(depth, width)
        got = got_ref[i].reshape(depth, width)
        total = jnp.dot(lhs_ref[:, :depth], own, preferred_element_type=jnp.float32)
        total += jnp.dot(lhs_ref[:, depth:], got, preferred_element_type=jnp.float32)
        for j, ref in enumerate(out_refs):
            ref[i] = total[j * share : (j + 1) * share].astype(ref.dtype)


def add_kernel(n, pieces, bias_ref, target_ref, *refs):
    out_hbm, out_ref, sems = refs[-3:]
    half = n // 2
    layers, _, cols = target_ref.shape
    rep = lax.axis_index("rep")
    copies = []
    for i, (offsets, first, width, _) in enumerate(pieces):
        for side in range(2):
            core = rep if side == 0 else 1 - rep
            columns = pl.ds(pl.multiple_of(core * (cols // 2) + first, LANES), width)
            for j, offset in enumerate(offsets):
                layer = layer_of(offset, layers)
                total = bias_ref[0:1, columns]
                for other in range(1, layers):
                    total = jnp.where(layer == other, bias_ref[other : other + 1, columns], total)
                total = total - target_ref[layer, :, columns].astype(jnp.float32)
                mine = refs[2 * half * i : 2 * half * (i + 1)]
                first_sum = side * (half - 1)
                for ref in (*mine[first_sum : first_sum + half - 1], mine[-1 - side]):
                    total = total + ref[j].astype(jnp.float32)
                place = len(copies)
                out_ref[place, :, :width] = total.astype(jnp.bfloat16)
                copies.append(
                    pltpu.make_async_copy(
                        out_ref.at[place, :, :width], out_hbm.at[layer, :, columns], sems.at[place]
                    )
                )
                copies[-1].start()
    for copy in copies:
        copy.wait()


def body(acts, enc_w, enc_b, dec_w, dec_b, targets, active):
    n = lax.axis_size("src")
    rows, features = acts.shape
    layers, groups, block, cols = dec_w.shape
    share = rows // n
    half = n // 2
    pieces = cut_pieces(cols // 2)
    fetched = [piece for piece in pieces if not piece[3]]
    tile_rows = rows // active.shape[0]
    pair = [(i, i ^ 1) for i in range(n)]
    params = pltpu.CompilerParams(vmem_limit_bytes=VMEM_BYTES)
    vmem = pl.BlockSpec(memory_space=pltpu.VMEM)
    smem = pl.BlockSpec(memory_space=pltpu.SMEM)
    anywhere = pl.BlockSpec(memory_space=pl.ANY)
    def weight(billions):
        return pl.CostEstimate(
            flops=int(billions * 1e9), bytes_accessed=0, transcendentals=0
        )

    cost = weight(0)

    dec_rows = dec_w
    acts, enc_w, dec_w = (
        pltpu.with_memory_space_constraint(value, pltpu.HBM)
        for value in (acts.reshape(half, 2, share, features), enc_w, dec_w)
    )

    def shape(*extent, kind=jnp.bfloat16):
        return jax.ShapeDtypeStruct(extent, kind)

    results = pl.pallas_call(
        functools.partial(encode_kernel, n, fetched[:1]),
        out_shape=[shape(half * share, 2 * block)] * n
        + [shape(len(offsets), groups, block, width) for offsets, _, width, _ in fetched[:1]],
        in_specs=[anywhere] * 3,
        out_specs=[vmem] * (n + 1),
        scratch_shapes=[
            pltpu.VMEM((2, half, share, features), jnp.bfloat16),
            pltpu.VMEM(enc_w.shape, jnp.bfloat16),
            pltpu.SemaphoreType.DMA((1, layers * groups)),
            pltpu.SemaphoreType.DMA((2 * half,)),
            pltpu.SemaphoreType.DMA((8,)),
        ],
        compiler_params=params,
        cost_estimate=cost,
        name="encode",
    )(acts, enc_w, dec_w)
    terms, parts = list(results[:n]), list(results[n:])
    for k in range(1, n):
        terms[k] = lax.ppermute(terms[k], "src", [(i, peer(i, k, n)) for i in range(n)])
    order = range(n)
    own = pl.pallas_call(
        functools.partial(codes_kernel, n, share, tile_rows),
        out_shape=shape(half, share, 2 * block),
        in_specs=[smem] + [vmem] * (1 + n),
        out_specs=vmem,
        compiler_params=params,
        cost_estimate=weight(20),
        name="codes",
    )(active, enc_b.reshape(n, block), *[terms[k] for k in order])
    codes = []
    for k in range(groups):
        for r in range(2):
            perm = [
                (i * 2 + c, (i + k) % groups * 2 + (c ^ r)) for i in range(groups) for c in range(2)
            ]
            codes.append(lax.ppermute(own, ("tgt", "rep"), perm) if k + r else own)

    lhs = pl.pallas_call(
        functools.partial(gather_kernel, n),
        out_shape=shape(rows, 2 * groups * block),
        in_specs=[vmem] * len(codes),
        out_specs=vmem,
        compiler_params=params,
        cost_estimate=weight(20),
        name="gather",
    )(*codes)

    part = pl.pallas_call(
        functools.partial(part_kernel, fetched[1]),
        out_shape=shape(len(fetched[1][0]), groups, block, fetched[1][2]),
        in_specs=[anywhere] * 3,
        out_specs=vmem,
        scratch_shapes=[pltpu.SemaphoreType.DMA((layers * groups,))],
        compiler_params=params,
        cost_estimate=weight(0),
        name="part",
    )(parts[0], dec_w, own)

    got = [lax.ppermute(parts[0], "src", pair)]
    got.append(lax.ppermute(got[0], "parts", [(0, 1), (1, 0)]))
    got.append(lax.ppermute(part, "src", pair))

    def add(some, begun, billions):
        operands = [value for i in some for value in sums[i]]
        count = 2 * sum(len(pieces[i][0]) for i in some)
        widest = max(piece[2] for piece in pieces)
        return pl.pallas_call(
            functools.partial(add_kernel, n, [pieces[i] for i in some]),
            out_shape=shape(layers, share, cols),
            in_specs=[vmem] * (2 + len(operands)) + [anywhere] * len(begun),
            out_specs=anywhere,
            scratch_shapes=[
                pltpu.VMEM((count, share, widest), jnp.bfloat16),
                pltpu.SemaphoreType.DMA((count,)),
            ],
            input_output_aliases={2 + len(operands): 0} if begun else {},
            compiler_params=params,
            cost_estimate=weight(billions),
            name="add",
        )(dec_b, targets, *operands, *begun)

    sums, after = [], []
    for i, piece in enumerate(pieces):
        offsets, _, width, _ = piece
        shapes = [shape(len(offsets), share, width)] * (2 * half)
        shapes[0] = shape(len(offsets), share, width, kind=jnp.float32)
        terms = pl.pallas_call(
            functools.partial(decode_kernel, n, piece),
            out_shape=shapes,
            in_specs=[vmem] * 3 + [anywhere] * len(after),
            out_specs=[vmem] * len(shapes),
            compiler_params=params,
            cost_estimate=weight(0),
            name="decode",
        )(dec_rows, lhs, got[i], *after)
        after = [terms[0]]
        sums.append([])
        for r, j in [(r, j) for r in range(2) for j in range(1, half)] + [(1, 0)]:
            perm = [(d * 2 + c, (d + 2 * j) % n * 2 + (c ^ r)) for d in range(n) for c in range(2)]
            sums[i].append(lax.ppermute(terms[2 * j + r], ("src", "rep"), perm))
        sums[i].append(terms[0])

    begun = []
    begun = [add([0, 1], begun, 20)]
    return add([2], begun, 0)


def solution(mesh):
    in_specs = (
        P(("parts", "rep"), "src"),
        P("src", "tgt"),
        P("tgt"),
        P(None, None, "src", "tgt"),
        P(None, "tgt"),
        P(None, ("parts", "rep", "src"), "tgt"),
        P(("parts", "rep"), None),
    )
    out_specs = P(None, ("parts", "rep", "src"), "tgt")
    return jax.shard_map(body, mesh=mesh, in_specs=in_specs, out_specs=out_specs, check_vma=False)
```

```python
import functools

import jax
import jax.numpy as jnp
from jax import lax
from jax.experimental import pallas as pl
from jax.experimental.pallas import tpu as pltpu
from jax.sharding import PartitionSpec as P

VMEM_BYTES = 32 * 1024 * 1024
LANES = 128
FIRST = 6
PIECES = (((0,), 0, False), ((1,), 0, True), ((0, 1), 1, False))


def cut_pieces(columns):
    middle = columns // LANES * FIRST // 8 * LANES
    bounds = ((0, middle), (middle, columns))
    return [
        (layers, bounds[side][0], bounds[side][1] - bounds[side][0], across)
        for layers, side, across in PIECES
    ]


def layer_of(offset, layers):
    return lax.rem(lax.axis_index("parts") + offset, layers)


def peer(index, k, n):
    return index ^ k if n & (n - 1) == 0 else (index + k) % n


def part_copies(piece, dec_hbm, part_ref, sems):
    offsets, first, width, _ = piece
    layers, groups, _, cols = dec_hbm.shape
    start = pl.multiple_of(lax.axis_index("rep") * (cols // 2) + first, LANES)
    copies = []
    for i, offset in enumerate(offsets):
        for group in range(groups):
            source = dec_hbm.at[layer_of(offset, layers), group, :, pl.ds(start, width)]
            sem = sems.at[i * groups + group]
            copies.append(pltpu.make_async_copy(source, part_ref.at[i, group], sem))
            copies[-1].start()
    return copies


def encode_kernel(n, pieces, acts_hbm, w_hbm, dec_hbm, *refs):
    term_refs, part_refs, refs = refs[:n], refs[n:-5], refs[-5:]
    acts_ref, w_ref, part_sems, acts_sems, w_sems = refs
    half = n // 2
    width = w_ref.shape[1] // half
    depth = w_ref.shape[0] // 8
    copies = []
    for i in range(2):
        for j in range(half):
            copies.append(
                pltpu.make_async_copy(
                    acts_hbm.at[j, i], acts_ref.at[i, j], acts_sems.at[i * half + j]
                )
            )
    for i in range(8):
        rows = slice(i * depth, (i + 1) * depth)
        copies.append(pltpu.make_async_copy(w_hbm.at[rows], w_ref.at[rows], w_sems.at[i]))
    for copy in copies:
        copy.start()
    copies_part = []
    for i, piece in enumerate(pieces):
        copies_part += part_copies(piece, dec_hbm, part_refs[i], part_sems.at[i])
    for copy in copies[: 2 * half]:
        copy.wait()
    src = lax.axis_index("src")
    features = w_ref.shape[0]
    steps = max(1, min(4, features // 256))
    totals = [0.0] * n
    for step in range(steps):
        for copy in copies[2 * half + step * 8 // steps : 2 * half + (step + 1) * 8 // steps]:
            copy.wait()
        depths = slice(step * features // steps, (step + 1) * features // steps)
        for k in range(n):
            dest = peer(src, k, n)
            rows = acts_ref[lax.rem(dest, 2), :, :, depths]
            rows = rows.reshape(rows.shape[0] * rows.shape[1], rows.shape[2])
            columns = pl.ds(pl.multiple_of((dest // 2) * width, width), width)
            totals[k] += jnp.dot(
                rows, w_ref[depths, columns], preferred_element_type=jnp.float32
            )
            if step == steps - 1:
                term_refs[k][...] = totals[k].astype(jnp.bfloat16)
    for copy in copies_part:
        copy.wait()


def part_kernel(piece, before_ref, dec_hbm, after_ref, part_ref, sems):
    for copy in part_copies(piece, dec_hbm, part_ref, sems):
        copy.wait()


def codes_kernel(n, share, tile_rows, active_ref, bias_ref, *refs):
    term_refs, out_ref = refs[:n], refs[n]
    src = lax.axis_index("src")
    tgt = lax.axis_index("tgt")
    parity, half = lax.rem(src, 2), src // 2
    block = out_ref.shape[2] // 2
    pre = term_refs[0][...].astype(jnp.float32)
    for ref in term_refs[1:]:
        pre = pre + ref[...].astype(jnp.float32)
    tiles, slots = active_ref.shape
    for piece in range(2):
        columns = slice(piece * block, (piece + 1) * block)
        bias = bias_ref[pl.ds(half * 2 + piece, 1), :]
        wanted = tgt * n + half * 2 + piece
        flags = []
        for tile in range(tiles):
            flags.append(
                lax.fori_loop(
                    0,
                    slots,
                    lambda i, total: total + (active_ref[tile, i] == wanted).astype(jnp.int32),
                    jnp.int32(0),
                    unroll=slots <= 16,
                )
            )
        for group in range(n // 2):
            tile = ((group * 2 + parity) * share) // tile_rows
            flag = flags[0]
            for i in range(1, tiles):
                flag = jnp.where(tile == i, flags[i], flag)
            live = jnp.where(flag > 0, 1.0, 0.0).astype(jnp.float32)
            rows = slice(group * share, (group + 1) * share)
            value = live * jnp.maximum(pre[rows, columns] + bias, 0.0)
            out_ref[group, :, columns] = value.astype(jnp.bfloat16)


def gather_kernel(n, *refs):
    half = n // 2
    code_refs, out_ref = refs[:-1], refs[-1]
    groups = len(code_refs) // 2
    src, tgt = lax.axis_index("src"), lax.axis_index("tgt")
    parity = lax.rem(src, 2)
    share, block = code_refs[0].shape[1], code_refs[0].shape[2] // 2
    for k in range(groups):
        place = lax.rem(tgt - k + groups, groups)
        for side in range(2):
            latents = parity if side == 0 else 1 - parity
            latents = pl.ds(pl.multiple_of(latents * block, block), block)
            columns = pl.ds(pl.multiple_of((side * groups + place) * block, block), block)
            for j in range(half):
                group = lax.rem(src // 2 + j, half)
                for r in range(2):
                    rows = slice((2 * j + r) * share, (2 * j + r + 1) * share)
                    out_ref[rows, columns] = code_refs[2 * k + r][group, :, latents]


def decode_kernel(n, piece, dec_ref, lhs_ref, got_ref, *refs):
    offsets, first, width, _ = piece
    layers, groups, block, cols = dec_ref.shape
    out_refs = refs[-2 * (n // 2) :]
    depth = groups * block
    share = lhs_ref.shape[0] // len(out_refs)
    start = pl.multiple_of(lax.axis_index("rep") * (cols // 2) + first, LANES)
    for i, offset in enumerate(offsets):
        own = dec_ref[layer_of(offset, layers), :, :, pl.ds(start, width)].reshape(depth, width)
        got = got_ref[i].reshape(depth, width)
        total = jnp.dot(lhs_ref[:, :depth], own, preferred_element_type=jnp.float32)
        total += jnp.dot(lhs_ref[:, depth:], got, preferred_element_type=jnp.float32)
        for j, ref in enumerate(out_refs):
            ref[i] = total[j * share : (j + 1) * share].astype(ref.dtype)


def add_kernel(n, pieces, bias_ref, target_ref, *refs):
    out_hbm, out_ref, sems = refs[-3:]
    half = n // 2
    layers, _, cols = target_ref.shape
    rep = lax.axis_index("rep")
    copies = []
    for i, (offsets, first, width, _) in enumerate(pieces):
        for side in range(2):
            core = rep if side == 0 else 1 - rep
            columns = pl.ds(pl.multiple_of(core * (cols // 2) + first, LANES), width)
            for j, offset in enumerate(offsets):
                layer = layer_of(offset, layers)
                total = bias_ref[0:1, columns]
                for other in range(1, layers):
                    total = jnp.where(layer == other, bias_ref[other : other + 1, columns], total)
                total = total - target_ref[layer, :, columns].astype(jnp.float32)
                mine = refs[2 * half * i : 2 * half * (i + 1)]
                first_sum = side * (half - 1)
                for ref in (*mine[first_sum : first_sum + half - 1], mine[-1 - side]):
                    total = total + ref[j].astype(jnp.float32)
                place = len(copies)
                out_ref[place, :, :width] = total.astype(jnp.bfloat16)
                copies.append(
                    pltpu.make_async_copy(
                        out_ref.at[place, :, :width], out_hbm.at[layer, :, columns], sems.at[place]
                    )
                )
                copies[-1].start()
    for copy in copies:
        copy.wait()


def body(acts, enc_w, enc_b, dec_w, dec_b, targets, active):
    n = lax.axis_size("src")
    rows, features = acts.shape
    layers, groups, block, cols = dec_w.shape
    share = rows // n
    half = n // 2
    pieces = cut_pieces(cols // 2)
    fetched = [piece for piece in pieces if not piece[3]]
    tile_rows = rows // active.shape[0]
    pair = [(i, i ^ 1) for i in range(n)]
    params = pltpu.CompilerParams(vmem_limit_bytes=VMEM_BYTES)
    vmem = pl.BlockSpec(memory_space=pltpu.VMEM)
    smem = pl.BlockSpec(memory_space=pltpu.SMEM)
    anywhere = pl.BlockSpec(memory_space=pl.ANY)
    def weight(billions):
        return pl.CostEstimate(
            flops=int(billions * 1e9), bytes_accessed=0, transcendentals=0
        )

    cost = weight(0)

    dec_rows = dec_w
    acts, enc_w, dec_w = (
        pltpu.with_memory_space_constraint(value, pltpu.HBM)
        for value in (acts.reshape(half, 2, share, features), enc_w, dec_w)
    )

    def shape(*extent, kind=jnp.bfloat16):
        return jax.ShapeDtypeStruct(extent, kind)

    results = pl.pallas_call(
        functools.partial(encode_kernel, n, fetched[:1]),
        out_shape=[shape(half * share, 2 * block)] * n
        + [shape(len(offsets), groups, block, width) for offsets, _, width, _ in fetched[:1]],
        in_specs=[anywhere] * 3,
        out_specs=[vmem] * (n + 1),
        scratch_shapes=[
            pltpu.VMEM((2, half, share, features), jnp.bfloat16),
            pltpu.VMEM(enc_w.shape, jnp.bfloat16),
            pltpu.SemaphoreType.DMA((1, layers * groups)),
            pltpu.SemaphoreType.DMA((2 * half,)),
            pltpu.SemaphoreType.DMA((8,)),
        ],
        compiler_params=params,
        cost_estimate=cost,
        name="encode",
    )(acts, enc_w, dec_w)
    terms, parts = list(results[:n]), list(results[n:])
    for k in range(1, n):
        terms[k] = lax.ppermute(terms[k], "src", [(i, peer(i, k, n)) for i in range(n)])
    order = range(n)
    own = pl.pallas_call(
        functools.partial(codes_kernel, n, share, tile_rows),
        out_shape=shape(half, share, 2 * block),
        in_specs=[smem] + [vmem] * (1 + n),
        out_specs=vmem,
        compiler_params=params,
        cost_estimate=weight(20),
        name="codes",
    )(active, enc_b.reshape(n, block), *[terms[k] for k in order])
    codes = []
    for k in range(groups):
        for r in range(2):
            perm = [
                (i * 2 + c, (i + k) % groups * 2 + (c ^ r)) for i in range(groups) for c in range(2)
            ]
            codes.append(lax.ppermute(own, ("tgt", "rep"), perm) if k + r else own)

    lhs = pl.pallas_call(
        functools.partial(gather_kernel, n),
        out_shape=shape(rows, 2 * groups * block),
        in_specs=[vmem] * len(codes),
        out_specs=vmem,
        compiler_params=params,
        cost_estimate=weight(20),
        name="gather",
    )(*codes)

    part = pl.pallas_call(
        functools.partial(part_kernel, fetched[1]),
        out_shape=shape(len(fetched[1][0]), groups, block, fetched[1][2]),
        in_specs=[anywhere] * 3,
        out_specs=vmem,
        scratch_shapes=[pltpu.SemaphoreType.DMA((layers * groups,))],
        compiler_params=params,
        cost_estimate=weight(0),
        name="part",
    )(parts[0], dec_w, own)

    got = [lax.ppermute(parts[0], "src", pair)]
    got.append(lax.ppermute(got[0], "parts", [(0, 1), (1, 0)]))
    got.append(lax.ppermute(part, "src", pair))

    def add(some, begun, billions):
        operands = [value for i in some for value in sums[i]]
        count = 2 * sum(len(pieces[i][0]) for i in some)
        widest = max(piece[2] for piece in pieces)
        return pl.pallas_call(
            functools.partial(add_kernel, n, [pieces[i] for i in some]),
            out_shape=shape(layers, share, cols),
            in_specs=[vmem] * (2 + len(operands)) + [anywhere] * len(begun),
            out_specs=anywhere,
            scratch_shapes=[
                pltpu.VMEM((count, share, widest), jnp.bfloat16),
                pltpu.SemaphoreType.DMA((count,)),
            ],
            input_output_aliases={2 + len(operands): 0} if begun else {},
            compiler_params=params,
            cost_estimate=weight(billions),
            name="add",
        )(dec_b, targets, *operands, *begun)

    sums, after = [], []
    for i, piece in enumerate(pieces):
        offsets, _, width, _ = piece
        shapes = [shape(len(offsets), share, width)] * (2 * half)
        shapes[0] = shape(len(offsets), share, width, kind=jnp.float32)
        terms = pl.pallas_call(
            functools.partial(decode_kernel, n, piece),
            out_shape=shapes,
            in_specs=[vmem] * 3 + [anywhere] * len(after),
            out_specs=[vmem] * len(shapes),
            compiler_params=params,
            cost_estimate=weight(0),
            name="decode",
        )(dec_rows, lhs, got[i], *after)
        after = [terms[0]]
        sums.append([])
        for r, j in [(r, j) for r in range(2) for j in range(1, half)] + [(1, 0)]:
            perm = [(d * 2 + c, (d + 2 * j) % n * 2 + (c ^ r)) for d in range(n) for c in range(2)]
            sums[i].append(lax.ppermute(terms[2 * j + r], ("src", "rep"), perm))
        sums[i].append(terms[0])

    begun = []
    begun = [add([0, 1], begun, 20)]
    return add([2], begun, 0)


def solution(mesh):
    in_specs = (
        P(("parts", "rep"), "src"),
        P("src", "tgt"),
        P("tgt"),
        P(None, None, "src", "tgt"),
        P(None, "tgt"),
        P(None, ("parts", "rep", "src"), "tgt"),
        P(("parts", "rep"), None),
    )
    out_specs = P(None, ("parts", "rep", "src"), "tgt")
    return jax.shard_map(body, mesh=mesh, in_specs=in_specs, out_specs=out_specs, check_vma=False)
```

```python
import functools

import jax
import jax.numpy as jnp
from jax import lax
from jax.experimental import pallas as pl
from jax.experimental.pallas import tpu as pltpu
from jax.sharding import PartitionSpec as P

VMEM_BYTES = 32 * 1024 * 1024
LANES = 128
FIRST = 6
PIECES = (((0,), 0, False), ((1,), 0, True), ((0, 1), 1, False))


def cut_pieces(columns):
    middle = columns // LANES * FIRST // 8 * LANES
    bounds = ((0, middle), (middle, columns))
    return [
        (layers, bounds[side][0], bounds[side][1] - bounds[side][0], across)
        for layers, side, across in PIECES
    ]


def layer_of(offset, layers):
    return lax.rem(lax.axis_index("parts") + offset, layers)


def peer(index, k, n):
    return index ^ k if n & (n - 1) == 0 else (index + k) % n


def part_copies(piece, dec_hbm, part_ref, sems):
    offsets, first, width, _ = piece
    layers, groups, _, cols = dec_hbm.shape
    start = pl.multiple_of(lax.axis_index("rep") * (cols // 2) + first, LANES)
    copies = []
    for i, offset in enumerate(offsets):
        for group in range(groups):
            source = dec_hbm.at[layer_of(offset, layers), group, :, pl.ds(start, width)]
            sem = sems.at[i * groups + group]
            copies.append(pltpu.make_async_copy(source, part_ref.at[i, group], sem))
            copies[-1].start()
    return copies


def encode_kernel(n, pieces, acts_hbm, w_hbm, dec_hbm, *refs):
    term_refs, part_refs, refs = refs[:n], refs[n:-5], refs[-5:]
    acts_ref, w_ref, part_sems, acts_sems, w_sems = refs
    half = n // 2
    width = w_ref.shape[1] // half
    depth = w_ref.shape[0] // 8
    copies = []
    for i in range(2):
        for j in range(half):
            copies.append(
                pltpu.make_async_copy(
                    acts_hbm.at[j, i], acts_ref.at[i, j], acts_sems.at[i * half + j]
                )
            )
    for i in range(8):
        rows = slice(i * depth, (i + 1) * depth)
        copies.append(pltpu.make_async_copy(w_hbm.at[rows], w_ref.at[rows], w_sems.at[i]))
    for copy in copies:
        copy.start()
    copies_part = []
    for i, piece in enumerate(pieces):
        copies_part += part_copies(piece, dec_hbm, part_refs[i], part_sems.at[i])
    for copy in copies:
        copy.wait()
    src = lax.axis_index("src")
    for k in range(n):
        dest = peer(src, k, n)
        rows = acts_ref[lax.rem(dest, 2)]
        rows = rows.reshape(rows.shape[0] * rows.shape[1], rows.shape[2])
        columns = pl.ds(pl.multiple_of((dest // 2) * width, width), width)
        term_refs[k][...] = jnp.dot(
            rows, w_ref[:, columns], preferred_element_type=jnp.float32
        ).astype(jnp.bfloat16)
    for copy in copies_part:
        copy.wait()


def part_kernel(piece, before_ref, dec_hbm, after_ref, part_ref, sems):
    for copy in part_copies(piece, dec_hbm, part_ref, sems):
        copy.wait()


def codes_kernel(n, share, tile_rows, active_ref, bias_ref, *refs):
    term_refs, out_ref = refs[:n], refs[n]
    src = lax.axis_index("src")
    tgt = lax.axis_index("tgt")
    parity, half = lax.rem(src, 2), src // 2
    block = out_ref.shape[2] // 2
    pre = term_refs[0][...].astype(jnp.float32)
    for ref in term_refs[1:]:
        pre = pre + ref[...].astype(jnp.float32)
    tiles, slots = active_ref.shape
    for piece in range(2):
        columns = slice(piece * block, (piece + 1) * block)
        bias = bias_ref[pl.ds(half * 2 + piece, 1), :]
        wanted = tgt * n + half * 2 + piece
        flags = []
        for tile in range(tiles):
            flags.append(
                lax.fori_loop(
                    0,
                    slots,
                    lambda i, total: total + (active_ref[tile, i] == wanted).astype(jnp.int32),
                    jnp.int32(0),
                    unroll=slots <= 16,
                )
            )
        for group in range(n // 2):
            tile = ((group * 2 + parity) * share) // tile_rows
            flag = flags[0]
            for i in range(1, tiles):
                flag = jnp.where(tile == i, flags[i], flag)
            live = jnp.where(flag > 0, 1.0, 0.0).astype(jnp.float32)
            rows = slice(group * share, (group + 1) * share)
            value = live * jnp.maximum(pre[rows, columns] + bias, 0.0)
            out_ref[group, :, columns] = value.astype(jnp.bfloat16)


def gather_kernel(n, *refs):
    half = n // 2
    code_refs, out_ref = refs[:-1], refs[-1]
    groups = len(code_refs) // 2
    src, tgt = lax.axis_index("src"), lax.axis_index("tgt")
    parity = lax.rem(src, 2)
    share, block = code_refs[0].shape[1], code_refs[0].shape[2] // 2
    for k in range(groups):
        place = lax.rem(tgt - k + groups, groups)
        for side in range(2):
            latents = parity if side == 0 else 1 - parity
            latents = pl.ds(pl.multiple_of(latents * block, block), block)
            columns = pl.ds(pl.multiple_of((side * groups + place) * block, block), block)
            for j in range(half):
                group = lax.rem(src // 2 + j, half)
                for r in range(2):
                    rows = slice((2 * j + r) * share, (2 * j + r + 1) * share)
                    out_ref[rows, columns] = code_refs[2 * k + r][group, :, latents]


def decode_kernel(n, piece, splits, dec_ref, lhs_ref, *refs):
    offsets, first, width = piece[:3]
    layers, groups, block, cols = dec_ref.shape
    got_refs, out_refs = refs[:splits], refs[-2 * (n // 2) :]
    depth, part = groups * block, width // splits
    share = lhs_ref.shape[0] // len(out_refs)
    for i, offset in enumerate(offsets):
        for c, ref in enumerate(got_refs):
            start = lax.axis_index("rep") * (cols // 2) + first + c * part
            columns = pl.ds(pl.multiple_of(start, LANES), part)
            own = dec_ref[layer_of(offset, layers), :, :, columns].reshape(depth, part)
            got = ref[i].reshape(depth, part)
            total = jnp.dot(lhs_ref[:, :depth], own, preferred_element_type=jnp.float32)
            total += jnp.dot(lhs_ref[:, depth:], got, preferred_element_type=jnp.float32)
            for j, out_ref in enumerate(out_refs):
                value = total[j * share : (j + 1) * share].astype(out_ref.dtype)
                out_ref[i, :, c * part : (c + 1) * part] = value


def add_kernel(n, pieces, bias_ref, target_ref, *refs):
    out_hbm, out_ref, sems = refs[-3:]
    half = n // 2
    layers, _, cols = target_ref.shape
    rep = lax.axis_index("rep")
    copies = []
    for i, (offsets, first, width, _) in enumerate(pieces):
        for side in range(2):
            core = rep if side == 0 else 1 - rep
            columns = pl.ds(pl.multiple_of(core * (cols // 2) + first, LANES), width)
            for j, offset in enumerate(offsets):
                layer = layer_of(offset, layers)
                total = bias_ref[0:1, columns]
                for other in range(1, layers):
                    total = jnp.where(layer == other, bias_ref[other : other + 1, columns], total)
                total = total - target_ref[layer, :, columns].astype(jnp.float32)
                mine = refs[2 * half * i : 2 * half * (i + 1)]
                first_sum = side * (half - 1)
                for ref in (*mine[first_sum : first_sum + half - 1], mine[-1 - side]):
                    total = total + ref[j].astype(jnp.float32)
                place = len(copies)
                out_ref[place, :, :width] = total.astype(jnp.bfloat16)
                copies.append(
                    pltpu.make_async_copy(
                        out_ref.at[place, :, :width], out_hbm.at[layer, :, columns], sems.at[place]
                    )
                )
                copies[-1].start()
    for copy in copies:
        copy.wait()


def body(acts, enc_w, enc_b, dec_w, dec_b, targets, active):
    n = lax.axis_size("src")
    rows, features = acts.shape
    layers, groups, block, cols = dec_w.shape
    share = rows // n
    half = n // 2
    pieces = cut_pieces(cols // 2)
    offsets, first, width, _ = pieces[0]
    splits = 2 if width % (2 * LANES) == 0 else 1
    width //= splits
    fetched = [(offsets, first + c * width, width, False) for c in range(splits)] + [pieces[2]]
    tile_rows = rows // active.shape[0]
    pair = [(i, i ^ 1) for i in range(n)]
    params = pltpu.CompilerParams(vmem_limit_bytes=VMEM_BYTES)
    vmem = pl.BlockSpec(memory_space=pltpu.VMEM)
    smem = pl.BlockSpec(memory_space=pltpu.SMEM)
    anywhere = pl.BlockSpec(memory_space=pl.ANY)
    def weight(billions):
        return pl.CostEstimate(
            flops=int(billions * 1e9), bytes_accessed=0, transcendentals=0
        )

    cost = weight(0)

    dec_rows = dec_w
    acts, enc_w, dec_w = (
        pltpu.with_memory_space_constraint(value, pltpu.HBM)
        for value in (acts.reshape(half, 2, share, features), enc_w, dec_w)
    )

    def shape(*extent, kind=jnp.bfloat16):
        return jax.ShapeDtypeStruct(extent, kind)

    results = pl.pallas_call(
        functools.partial(encode_kernel, n, fetched[:-1]),
        out_shape=[shape(half * share, 2 * block)] * n
        + [shape(len(offsets), groups, block, width) for offsets, _, width, _ in fetched[:-1]],
        in_specs=[anywhere] * 3,
        out_specs=[vmem] * (n + splits),
        scratch_shapes=[
            pltpu.VMEM((2, half, share, features), jnp.bfloat16),
            pltpu.VMEM(enc_w.shape, jnp.bfloat16),
            pltpu.SemaphoreType.DMA((splits, layers * groups)),
            pltpu.SemaphoreType.DMA((2 * half,)),
            pltpu.SemaphoreType.DMA((8,)),
        ],
        compiler_params=params,
        cost_estimate=cost,
        name="encode",
    )(acts, enc_w, dec_w)
    terms, parts = list(results[:n]), list(results[n:])
    for k in range(1, n):
        terms[k] = lax.ppermute(terms[k], "src", [(i, peer(i, k, n)) for i in range(n)])
    order = range(n)
    own = pl.pallas_call(
        functools.partial(codes_kernel, n, share, tile_rows),
        out_shape=shape(half, share, 2 * block),
        in_specs=[smem] + [vmem] * (1 + n),
        out_specs=vmem,
        compiler_params=params,
        cost_estimate=weight(20),
        name="codes",
    )(active, enc_b.reshape(n, block), *[terms[k] for k in order])
    codes = []
    for k in range(groups):
        for r in range(2):
            perm = [
                (i * 2 + c, (i + k) % groups * 2 + (c ^ r)) for i in range(groups) for c in range(2)
            ]
            codes.append(lax.ppermute(own, ("tgt", "rep"), perm) if k + r else own)

    lhs = pl.pallas_call(
        functools.partial(gather_kernel, n),
        out_shape=shape(rows, 2 * groups * block),
        in_specs=[vmem] * len(codes),
        out_specs=vmem,
        compiler_params=params,
        cost_estimate=weight(20),
        name="gather",
    )(*codes)

    part = pl.pallas_call(
        functools.partial(part_kernel, fetched[-1]),
        out_shape=shape(len(fetched[-1][0]), groups, block, fetched[-1][2]),
        in_specs=[anywhere] * 3,
        out_specs=vmem,
        scratch_shapes=[pltpu.SemaphoreType.DMA((layers * groups,))],
        compiler_params=params,
        cost_estimate=weight(0),
        name="part",
    )(parts[0], dec_w, own)

    got = [[lax.ppermute(value, "src", pair) for value in parts]]
    got.append([lax.ppermute(value, "parts", [(0, 1), (1, 0)]) for value in got[0]])
    got.append([lax.ppermute(part, "src", pair)])

    def add(some, begun, billions):
        operands = [value for i in some for value in sums[i]]
        count = 2 * sum(len(pieces[i][0]) for i in some)
        widest = max(piece[2] for piece in pieces)
        return pl.pallas_call(
            functools.partial(add_kernel, n, [pieces[i] for i in some]),
            out_shape=shape(layers, share, cols),
            in_specs=[vmem] * (2 + len(operands)) + [anywhere] * len(begun),
            out_specs=anywhere,
            scratch_shapes=[
                pltpu.VMEM((count, share, widest), jnp.bfloat16),
                pltpu.SemaphoreType.DMA((count,)),
            ],
            input_output_aliases={2 + len(operands): 0} if begun else {},
            compiler_params=params,
            cost_estimate=weight(billions),
            name="add",
        )(dec_b, targets, *operands, *begun)

    sums, after = [], []
    for i, piece in enumerate(pieces):
        offsets, _, width, _ = piece
        shapes = [shape(len(offsets), share, width)] * (2 * half)
        shapes[0] = shape(len(offsets), share, width, kind=jnp.float32)
        terms = pl.pallas_call(
            functools.partial(decode_kernel, n, piece, len(got[i])),
            out_shape=shapes,
            in_specs=[vmem] * (2 + len(got[i])) + [anywhere] * len(after),
            out_specs=[vmem] * len(shapes),
            compiler_params=params,
            cost_estimate=weight(0),
            name="decode",
        )(dec_rows, lhs, *got[i], *after)
        after = [terms[0]]
        sums.append([])
        for r, j in [(r, j) for r in range(2) for j in range(1, half)] + [(1, 0)]:
            perm = [(d * 2 + c, (d + 2 * j) % n * 2 + (c ^ r)) for d in range(n) for c in range(2)]
            sums[i].append(lax.ppermute(terms[2 * j + r], ("src", "rep"), perm))
        sums[i].append(terms[0])

    begun = []
    begun = [add([0, 1], begun, 20)]
    return add([2], begun, 0)


def solution(mesh):
    in_specs = (
        P(("parts", "rep"), "src"),
        P("src", "tgt"),
        P("tgt"),
        P(None, None, "src", "tgt"),
        P(None, "tgt"),
        P(None, ("parts", "rep", "src"), "tgt"),
        P(("parts", "rep"), None),
    )
    out_specs = P(None, ("parts", "rep", "src"), "tgt")
    return jax.shard_map(body, mesh=mesh, in_specs=in_specs, out_specs=out_specs, check_vma=False)
```

```python
import functools

import jax
import jax.numpy as jnp
from jax import lax
from jax.experimental import pallas as pl
from jax.experimental.pallas import tpu as pltpu
from jax.sharding import PartitionSpec as P

VMEM_BYTES = 32 * 1024 * 1024
LANES = 128
FIRST = 5
PIECES = (((0,), 0, False), ((1,), 0, True), ((0, 1), 1, False))


def cut_pieces(columns):
    middle = columns // LANES * FIRST // 8 * LANES
    bounds = ((0, middle), (middle, columns))
    return [
        (layers, bounds[side][0], bounds[side][1] - bounds[side][0], across)
        for layers, side, across in PIECES
    ]


def layer_of(offset, layers):
    return lax.rem(lax.axis_index("parts") + offset, layers)


def peer(index, k, n):
    return index ^ k if n & (n - 1) == 0 else (index + k) % n


def part_copies(piece, dec_hbm, part_ref, sems):
    offsets, first, width, _ = piece
    layers, groups, _, cols = dec_hbm.shape
    start = pl.multiple_of(lax.axis_index("rep") * (cols // 2) + first, LANES)
    copies = []
    for i, offset in enumerate(offsets):
        for group in range(groups):
            source = dec_hbm.at[layer_of(offset, layers), group, :, pl.ds(start, width)]
            sem = sems.at[i * groups + group]
            copies.append(pltpu.make_async_copy(source, part_ref.at[i, group], sem))
            copies[-1].start()
    return copies


def encode_kernel(n, pieces, acts_hbm, w_hbm, dec_hbm, *refs):
    term_refs, part_refs, refs = refs[:n], refs[n:-5], refs[-5:]
    acts_ref, w_ref, part_sems, acts_sems, w_sems = refs
    half = n // 2
    width = w_ref.shape[1] // half
    depth = w_ref.shape[0] // 8
    copies = []
    for i in range(2):
        for j in range(half):
            copies.append(
                pltpu.make_async_copy(
                    acts_hbm.at[j, i], acts_ref.at[i, j], acts_sems.at[i * half + j]
                )
            )
    for i in range(8):
        rows = slice(i * depth, (i + 1) * depth)
        copies.append(pltpu.make_async_copy(w_hbm.at[rows], w_ref.at[rows], w_sems.at[i]))
    for copy in copies:
        copy.start()
    copies_part = []
    for i, piece in enumerate(pieces):
        copies_part += part_copies(piece, dec_hbm, part_refs[i], part_sems.at[i])
    for copy in copies:
        copy.wait()
    src = lax.axis_index("src")
    for k in range(n):
        dest = peer(src, k, n)
        rows = acts_ref[lax.rem(dest, 2)]
        rows = rows.reshape(rows.shape[0] * rows.shape[1], rows.shape[2])
        columns = pl.ds(pl.multiple_of((dest // 2) * width, width), width)
        term_refs[k][...] = jnp.dot(
            rows, w_ref[:, columns], preferred_element_type=jnp.float32
        ).astype(jnp.bfloat16)
    for copy in copies_part:
        copy.wait()


def part_kernel(piece, before_ref, dec_hbm, after_ref, part_ref, sems):
    for copy in part_copies(piece, dec_hbm, part_ref, sems):
        copy.wait()


def codes_kernel(n, share, tile_rows, active_ref, bias_ref, *refs):
    term_refs, out_ref = refs[:n], refs[n]
    src = lax.axis_index("src")
    tgt = lax.axis_index("tgt")
    parity, half = lax.rem(src, 2), src // 2
    block = out_ref.shape[2] // 2
    pre = term_refs[0][...].astype(jnp.float32)
    for ref in term_refs[1:]:
        pre = pre + ref[...].astype(jnp.float32)
    tiles, slots = active_ref.shape
    for piece in range(2):
        columns = slice(piece * block, (piece + 1) * block)
        bias = bias_ref[pl.ds(half * 2 + piece, 1), :]
        wanted = tgt * n + half * 2 + piece
        flags = []
        for tile in range(tiles):
            flags.append(
                lax.fori_loop(
                    0,
                    slots,
                    lambda i, total: total + (active_ref[tile, i] == wanted).astype(jnp.int32),
                    jnp.int32(0),
                    unroll=slots <= 16,
                )
            )
        for group in range(n // 2):
            tile = ((group * 2 + parity) * share) // tile_rows
            flag = flags[0]
            for i in range(1, tiles):
                flag = jnp.where(tile == i, flags[i], flag)
            live = jnp.where(flag > 0, 1.0, 0.0).astype(jnp.float32)
            rows = slice(group * share, (group + 1) * share)
            value = live * jnp.maximum(pre[rows, columns] + bias, 0.0)
            out_ref[group, :, columns] = value.astype(jnp.bfloat16)


def gather_kernel(n, *refs):
    half = n // 2
    code_refs, out_ref = refs[:-1], refs[-1]
    groups = len(code_refs) // 2
    src, tgt = lax.axis_index("src"), lax.axis_index("tgt")
    parity = lax.rem(src, 2)
    share, block = code_refs[0].shape[1], code_refs[0].shape[2] // 2
    for k in range(groups):
        place = lax.rem(tgt - k + groups, groups)
        for side in range(2):
            latents = parity if side == 0 else 1 - parity
            latents = pl.ds(pl.multiple_of(latents * block, block), block)
            columns = pl.ds(pl.multiple_of((side * groups + place) * block, block), block)
            for j in range(half):
                group = lax.rem(src // 2 + j, half)
                for r in range(2):
                    rows = slice((2 * j + r) * share, (2 * j + r + 1) * share)
                    out_ref[rows, columns] = code_refs[2 * k + r][group, :, latents]


def decode_kernel(n, piece, dec_ref, lhs_ref, got_ref, *refs):
    offsets, first, width, _ = piece
    layers, groups, block, cols = dec_ref.shape
    out_refs = refs[-2 * (n // 2) :]
    depth = groups * block
    share = lhs_ref.shape[0] // len(out_refs)
    start = pl.multiple_of(lax.axis_index("rep") * (cols // 2) + first, LANES)
    for i, offset in enumerate(offsets):
        own = dec_ref[layer_of(offset, layers), :, :, pl.ds(start, width)].reshape(depth, width)
        got = got_ref[i].reshape(depth, width)
        total = jnp.dot(lhs_ref[:, :depth], own, preferred_element_type=jnp.float32)
        total += jnp.dot(lhs_ref[:, depth:], got, preferred_element_type=jnp.float32)
        for j, ref in enumerate(out_refs):
            ref[i] = total[j * share : (j + 1) * share].astype(ref.dtype)


def add_kernel(n, pieces, bias_ref, target_ref, *refs):
    out_hbm, out_ref, sems = refs[-3:]
    half = n // 2
    layers, _, cols = target_ref.shape
    rep = lax.axis_index("rep")
    copies = []
    for i, (offsets, first, width, _) in enumerate(pieces):
        for side in range(2):
            core = rep if side == 0 else 1 - rep
            columns = pl.ds(pl.multiple_of(core * (cols // 2) + first, LANES), width)
            for j, offset in enumerate(offsets):
                layer = layer_of(offset, layers)
                total = bias_ref[0:1, columns]
                for other in range(1, layers):
                    total = jnp.where(layer == other, bias_ref[other : other + 1, columns], total)
                total = total - target_ref[layer, :, columns].astype(jnp.float32)
                mine = refs[2 * half * i : 2 * half * (i + 1)]
                first_sum = side * (half - 1)
                for ref in (*mine[first_sum : first_sum + half - 1], mine[-1 - side]):
                    total = total + ref[j].astype(jnp.float32)
                place = len(copies)
                out_ref[place, :, :width] = total.astype(jnp.bfloat16)
                copies.append(
                    pltpu.make_async_copy(
                        out_ref.at[place, :, :width], out_hbm.at[layer, :, columns], sems.at[place]
                    )
                )
                copies[-1].start()
    for copy in copies:
        copy.wait()


def body(acts, enc_w, enc_b, dec_w, dec_b, targets, active):
    n = lax.axis_size("src")
    rows, features = acts.shape
    layers, groups, block, cols = dec_w.shape
    share = rows // n
    half = n // 2
    pieces = cut_pieces(cols // 2)
    fetched = [piece for piece in pieces if not piece[3]]
    tile_rows = rows // active.shape[0]
    pair = [(i, i ^ 1) for i in range(n)]
    params = pltpu.CompilerParams(vmem_limit_bytes=VMEM_BYTES)
    vmem = pl.BlockSpec(memory_space=pltpu.VMEM)
    smem = pl.BlockSpec(memory_space=pltpu.SMEM)
    anywhere = pl.BlockSpec(memory_space=pl.ANY)
    def weight(billions):
        return pl.CostEstimate(
            flops=int(billions * 1e9), bytes_accessed=0, transcendentals=0
        )

    cost = weight(0)

    dec_rows = dec_w
    acts, enc_w, dec_w = (
        pltpu.with_memory_space_constraint(value, pltpu.HBM)
        for value in (acts.reshape(half, 2, share, features), enc_w, dec_w)
    )

    def shape(*extent, kind=jnp.bfloat16):
        return jax.ShapeDtypeStruct(extent, kind)

    results = pl.pallas_call(
        functools.partial(encode_kernel, n, fetched[:1]),
        out_shape=[shape(half * share, 2 * block)] * n
        + [shape(len(offsets), groups, block, width) for offsets, _, width, _ in fetched[:1]],
        in_specs=[anywhere] * 3,
        out_specs=[vmem] * (n + 1),
        scratch_shapes=[
            pltpu.VMEM((2, half, share, features), jnp.bfloat16),
            pltpu.VMEM(enc_w.shape, jnp.bfloat16),
            pltpu.SemaphoreType.DMA((1, layers * groups)),
            pltpu.SemaphoreType.DMA((2 * half,)),
            pltpu.SemaphoreType.DMA((8,)),
        ],
        compiler_params=params,
        cost_estimate=cost,
        name="encode",
    )(acts, enc_w, dec_w)
    terms, parts = list(results[:n]), list(results[n:])
    for k in range(1, n):
        terms[k] = lax.ppermute(terms[k], "src", [(i, peer(i, k, n)) for i in range(n)])
    order = range(n)
    own = pl.pallas_call(
        functools.partial(codes_kernel, n, share, tile_rows),
        out_shape=shape(half, share, 2 * block),
        in_specs=[smem] + [vmem] * (1 + n),
        out_specs=vmem,
        compiler_params=params,
        cost_estimate=weight(20),
        name="codes",
    )(active, enc_b.reshape(n, block), *[terms[k] for k in order])
    codes = []
    for k in range(groups):
        for r in range(2):
            perm = [
                (i * 2 + c, (i + k) % groups * 2 + (c ^ r)) for i in range(groups) for c in range(2)
            ]
            codes.append(lax.ppermute(own, ("tgt", "rep"), perm) if k + r else own)

    lhs = pl.pallas_call(
        functools.partial(gather_kernel, n),
        out_shape=shape(rows, 2 * groups * block),
        in_specs=[vmem] * len(codes),
        out_specs=vmem,
        compiler_params=params,
        cost_estimate=weight(20),
        name="gather",
    )(*codes)

    part = pl.pallas_call(
        functools.partial(part_kernel, fetched[1]),
        out_shape=shape(len(fetched[1][0]), groups, block, fetched[1][2]),
        in_specs=[anywhere] * 3,
        out_specs=vmem,
        scratch_shapes=[pltpu.SemaphoreType.DMA((layers * groups,))],
        compiler_params=params,
        cost_estimate=weight(0),
        name="part",
    )(parts[0], dec_w, own)

    got = [lax.ppermute(parts[0], "src", pair)]
    got.append(lax.ppermute(got[0], "parts", [(0, 1), (1, 0)]))
    got.append(lax.ppermute(part, "src", pair))

    def add(some, begun, billions):
        operands = [value for i in some for value in sums[i]]
        count = 2 * sum(len(pieces[i][0]) for i in some)
        widest = max(piece[2] for piece in pieces)
        return pl.pallas_call(
            functools.partial(add_kernel, n, [pieces[i] for i in some]),
            out_shape=shape(layers, share, cols),
            in_specs=[vmem] * (2 + len(operands)) + [anywhere] * len(begun),
            out_specs=anywhere,
            scratch_shapes=[
                pltpu.VMEM((count, share, widest), jnp.bfloat16),
                pltpu.SemaphoreType.DMA((count,)),
            ],
            input_output_aliases={2 + len(operands): 0} if begun else {},
            compiler_params=params,
            cost_estimate=weight(billions),
            name="add",
        )(dec_b, targets, *operands, *begun)

    sums, after = [], []
    for i, piece in enumerate(pieces):
        offsets, _, width, _ = piece
        shapes = [shape(len(offsets), share, width)] * (2 * half)
        shapes[0] = shape(len(offsets), share, width, kind=jnp.float32)
        terms = pl.pallas_call(
            functools.partial(decode_kernel, n, piece),
            out_shape=shapes,
            in_specs=[vmem] * 3 + [anywhere] * len(after),
            out_specs=[vmem] * len(shapes),
            compiler_params=params,
            cost_estimate=weight(0),
            name="decode",
        )(dec_rows, lhs, got[i], *after)
        after = [terms[0]]
        sums.append([])
        for r, j in [(r, j) for r in range(2) for j in range(1, half)] + [(1, 0)]:
            perm = [(d * 2 + c, (d + 2 * j) % n * 2 + (c ^ r)) for d in range(n) for c in range(2)]
            sums[i].append(lax.ppermute(terms[2 * j + r], ("src", "rep"), perm))
        sums[i].append(terms[0])

    begun = []
    begun = [add([0, 1], begun, 20)]
    return add([2], begun, 0)


def solution(mesh):
    in_specs = (
        P(("parts", "rep"), "src"),
        P("src", "tgt"),
        P("tgt"),
        P(None, None, "src", "tgt"),
        P(None, "tgt"),
        P(None, ("parts", "rep", "src"), "tgt"),
        P(("parts", "rep"), None),
    )
    out_specs = P(None, ("parts", "rep", "src"), "tgt")
    return jax.shard_map(body, mesh=mesh, in_specs=in_specs, out_specs=out_specs, check_vma=False)
```

```python
import functools

import jax
import jax.numpy as jnp
from jax import lax
from jax.experimental import pallas as pl
from jax.experimental.pallas import tpu as pltpu
from jax.sharding import PartitionSpec as P

VMEM_BYTES = 32 * 1024 * 1024
LANES = 128
FIRST = 6
PIECES = (((0,), 0, False), ((1,), 0, True), ((0, 1), 1, False))


def cut_pieces(columns):
    middle = columns // LANES * FIRST // 8 * LANES
    bounds = ((0, middle), (middle, columns))
    return [
        (layers, bounds[side][0], bounds[side][1] - bounds[side][0], across)
        for layers, side, across in PIECES
    ]


def layer_of(offset, layers):
    return lax.rem(lax.axis_index("parts") + offset, layers)


def peer(index, k, n):
    return index ^ k if n & (n - 1) == 0 else (index + k) % n


def part_copies(piece, dec_hbm, part_ref, sems):
    offsets, first, width, _ = piece
    layers, groups, _, cols = dec_hbm.shape
    start = pl.multiple_of(lax.axis_index("rep") * (cols // 2) + first, LANES)
    copies = []
    for i, offset in enumerate(offsets):
        for group in range(groups):
            source = dec_hbm.at[layer_of(offset, layers), group, :, pl.ds(start, width)]
            sem = sems.at[i * groups + group]
            copies.append(pltpu.make_async_copy(source, part_ref.at[i, group], sem))
            copies[-1].start()
    return copies


def encode_kernel(n, pieces, acts_hbm, w_hbm, dec_hbm, *refs):
    term_refs, part_refs, refs = refs[:n], refs[n:-5], refs[-5:]
    acts_ref, w_ref, part_sems, acts_sems, w_sems = refs
    half = n // 2
    width = w_ref.shape[1] // half
    depth = w_ref.shape[0] // 8
    copies = []
    for i in range(2):
        for j in range(half):
            copies.append(
                pltpu.make_async_copy(
                    acts_hbm.at[j, i], acts_ref.at[i, j], acts_sems.at[i * half + j]
                )
            )
    for i in range(8):
        rows = slice(i * depth, (i + 1) * depth)
        copies.append(pltpu.make_async_copy(w_hbm.at[rows], w_ref.at[rows], w_sems.at[i]))
    for copy in copies:
        copy.start()
    copies_part = []
    for i, piece in enumerate(pieces):
        copies_part += part_copies(piece, dec_hbm, part_refs[i], part_sems.at[i])
    for copy in copies:
        copy.wait()
    src = lax.axis_index("src")
    for k in range(n):
        dest = peer(src, k, n)
        rows = acts_ref[lax.rem(dest, 2)]
        rows = rows.reshape(rows.shape[0] * rows.shape[1], rows.shape[2])
        columns = pl.ds(pl.multiple_of((dest // 2) * width, width), width)
        term_refs[k][...] = jnp.dot(
            rows, w_ref[:, columns], preferred_element_type=jnp.float32
        ).astype(jnp.bfloat16)
    for copy in copies_part:
        copy.wait()


def part_kernel(piece, before_ref, dec_hbm, after_ref, part_ref, sems):
    for copy in part_copies(piece, dec_hbm, part_ref, sems):
        copy.wait()


def codes_kernel(n, share, tile_rows, active_ref, bias_ref, *refs):
    term_refs, out_ref = refs[:n], refs[n]
    src = lax.axis_index("src")
    tgt = lax.axis_index("tgt")
    parity, half = lax.rem(src, 2), src // 2
    block = out_ref.shape[2] // 2
    pre = term_refs[0][...].astype(jnp.float32)
    for ref in term_refs[1:]:
        pre = pre + ref[...].astype(jnp.float32)
    tiles = active_ref.shape[0]
    for piece in range(2):
        columns = slice(piece * block, (piece + 1) * block)
        bias = bias_ref[pl.ds(half * 2 + piece, 1), :]
        wanted = tgt * n + half * 2 + piece
        found = jnp.where(active_ref[...] == wanted, 1.0, 0.0).astype(jnp.float32)
        flags = jnp.max(found, axis=1, keepdims=True)
        for group in range(n // 2):
            tile = ((group * 2 + parity) * share) // tile_rows
            live = flags[0:1]
            for i in range(1, tiles):
                live = jnp.where(tile == i, flags[i : i + 1], live)
            rows = slice(group * share, (group + 1) * share)
            value = live * jnp.maximum(pre[rows, columns] + bias, 0.0)
            out_ref[group, :, columns] = value.astype(jnp.bfloat16)


def gather_kernel(n, *refs):
    half = n // 2
    code_refs, out_ref = refs[:-1], refs[-1]
    groups = len(code_refs) // 2
    src, tgt = lax.axis_index("src"), lax.axis_index("tgt")
    parity = lax.rem(src, 2)
    share, block = code_refs[0].shape[1], code_refs[0].shape[2] // 2
    for k in range(groups):
        place = lax.rem(tgt - k + groups, groups)
        for side in range(2):
            latents = parity if side == 0 else 1 - parity
            latents = pl.ds(pl.multiple_of(latents * block, block), block)
            columns = pl.ds(pl.multiple_of((side * groups + place) * block, block), block)
            for j in range(half):
                group = lax.rem(src // 2 + j, half)
                for r in range(2):
                    rows = slice((2 * j + r) * share, (2 * j + r + 1) * share)
                    out_ref[rows, columns] = code_refs[2 * k + r][group, :, latents]


def decode_kernel(n, piece, dec_ref, lhs_ref, got_ref, *refs):
    offsets, first, width, _ = piece
    layers, groups, block, cols = dec_ref.shape
    out_refs = refs[-2 * (n // 2) :]
    depth = groups * block
    share = lhs_ref.shape[0] // len(out_refs)
    start = pl.multiple_of(lax.axis_index("rep") * (cols // 2) + first, LANES)
    for i, offset in enumerate(offsets):
        own = dec_ref[layer_of(offset, layers), :, :, pl.ds(start, width)].reshape(depth, width)
        got = got_ref[i].reshape(depth, width)
        total = jnp.dot(lhs_ref[:, :depth], own, preferred_element_type=jnp.float32)
        total += jnp.dot(lhs_ref[:, depth:], got, preferred_element_type=jnp.float32)
        for j, ref in enumerate(out_refs):
            ref[i] = total[j * share : (j + 1) * share].astype(ref.dtype)


def add_kernel(n, pieces, bias_ref, target_ref, *refs):
    out_hbm, out_ref, sems = refs[-3:]
    half = n // 2
    layers, _, cols = target_ref.shape
    rep = lax.axis_index("rep")
    copies = []
    for i, (offsets, first, width, _) in enumerate(pieces):
        for side in range(2):
            core = rep if side == 0 else 1 - rep
            columns = pl.ds(pl.multiple_of(core * (cols // 2) + first, LANES), width)
            for j, offset in enumerate(offsets):
                layer = layer_of(offset, layers)
                total = bias_ref[0:1, columns]
                for other in range(1, layers):
                    total = jnp.where(layer == other, bias_ref[other : other + 1, columns], total)
                total = total - target_ref[layer, :, columns].astype(jnp.float32)
                mine = refs[2 * half * i : 2 * half * (i + 1)]
                first_sum = side * (half - 1)
                for ref in (*mine[first_sum : first_sum + half - 1], mine[-1 - side]):
                    total = total + ref[j].astype(jnp.float32)
                place = len(copies)
                out_ref[place, :, :width] = total.astype(jnp.bfloat16)
                copies.append(
                    pltpu.make_async_copy(
                        out_ref.at[place, :, :width], out_hbm.at[layer, :, columns], sems.at[place]
                    )
                )
                copies[-1].start()
    for copy in copies:
        copy.wait()


def body(acts, enc_w, enc_b, dec_w, dec_b, targets, active):
    n = lax.axis_size("src")
    rows, features = acts.shape
    layers, groups, block, cols = dec_w.shape
    share = rows // n
    half = n // 2
    pieces = cut_pieces(cols // 2)
    fetched = [piece for piece in pieces if not piece[3]]
    tile_rows = rows // active.shape[0]
    pair = [(i, i ^ 1) for i in range(n)]
    params = pltpu.CompilerParams(vmem_limit_bytes=VMEM_BYTES)
    vmem = pl.BlockSpec(memory_space=pltpu.VMEM)
    anywhere = pl.BlockSpec(memory_space=pl.ANY)
    def weight(billions):
        return pl.CostEstimate(
            flops=int(billions * 1e9), bytes_accessed=0, transcendentals=0
        )

    cost = weight(0)

    dec_rows = dec_w
    acts, enc_w, dec_w = (
        pltpu.with_memory_space_constraint(value, pltpu.HBM)
        for value in (acts.reshape(half, 2, share, features), enc_w, dec_w)
    )

    def shape(*extent, kind=jnp.bfloat16):
        return jax.ShapeDtypeStruct(extent, kind)

    results = pl.pallas_call(
        functools.partial(encode_kernel, n, fetched[:1]),
        out_shape=[shape(half * share, 2 * block)] * n
        + [shape(len(offsets), groups, block, width) for offsets, _, width, _ in fetched[:1]],
        in_specs=[anywhere] * 3,
        out_specs=[vmem] * (n + 1),
        scratch_shapes=[
            pltpu.VMEM((2, half, share, features), jnp.bfloat16),
            pltpu.VMEM(enc_w.shape, jnp.bfloat16),
            pltpu.SemaphoreType.DMA((1, layers * groups)),
            pltpu.SemaphoreType.DMA((2 * half,)),
            pltpu.SemaphoreType.DMA((8,)),
        ],
        compiler_params=params,
        cost_estimate=cost,
        name="encode",
    )(acts, enc_w, dec_w)
    terms, parts = list(results[:n]), list(results[n:])
    for k in range(1, n):
        terms[k] = lax.ppermute(terms[k], "src", [(i, peer(i, k, n)) for i in range(n)])
    order = range(n)
    own = pl.pallas_call(
        functools.partial(codes_kernel, n, share, tile_rows),
        out_shape=shape(half, share, 2 * block),
        in_specs=[vmem] * (2 + n),
        out_specs=vmem,
        compiler_params=params,
        cost_estimate=weight(20),
        name="codes",
    )(active, enc_b.reshape(n, block), *[terms[k] for k in order])
    codes = []
    for k in range(groups):
        for r in range(2):
            perm = [
                (i * 2 + c, (i + k) % groups * 2 + (c ^ r)) for i in range(groups) for c in range(2)
            ]
            codes.append(lax.ppermute(own, ("tgt", "rep"), perm) if k + r else own)

    lhs = pl.pallas_call(
        functools.partial(gather_kernel, n),
        out_shape=shape(rows, 2 * groups * block),
        in_specs=[vmem] * len(codes),
        out_specs=vmem,
        compiler_params=params,
        cost_estimate=weight(20),
        name="gather",
    )(*codes)

    part = pl.pallas_call(
        functools.partial(part_kernel, fetched[1]),
        out_shape=shape(len(fetched[1][0]), groups, block, fetched[1][2]),
        in_specs=[anywhere] * 3,
        out_specs=vmem,
        scratch_shapes=[pltpu.SemaphoreType.DMA((layers * groups,))],
        compiler_params=params,
        cost_estimate=weight(0),
        name="part",
    )(parts[0], dec_w, own)

    got = [lax.ppermute(parts[0], "src", pair)]
    got.append(lax.ppermute(got[0], "parts", [(0, 1), (1, 0)]))
    got.append(lax.ppermute(part, "src", pair))

    def add(some, begun, billions):
        operands = [value for i in some for value in sums[i]]
        count = 2 * sum(len(pieces[i][0]) for i in some)
        widest = max(piece[2] for piece in pieces)
        return pl.pallas_call(
            functools.partial(add_kernel, n, [pieces[i] for i in some]),
            out_shape=shape(layers, share, cols),
            in_specs=[vmem] * (2 + len(operands)) + [anywhere] * len(begun),
            out_specs=anywhere,
            scratch_shapes=[
                pltpu.VMEM((count, share, widest), jnp.bfloat16),
                pltpu.SemaphoreType.DMA((count,)),
            ],
            input_output_aliases={2 + len(operands): 0} if begun else {},
            compiler_params=params,
            cost_estimate=weight(billions),
            name="add",
        )(dec_b, targets, *operands, *begun)

    sums, after = [], []
    for i, piece in enumerate(pieces):
        offsets, _, width, _ = piece
        shapes = [shape(len(offsets), share, width)] * (2 * half)
        shapes[0] = shape(len(offsets), share, width, kind=jnp.float32)
        terms = pl.pallas_call(
            functools.partial(decode_kernel, n, piece),
            out_shape=shapes,
            in_specs=[vmem] * 3 + [anywhere] * len(after),
            out_specs=[vmem] * len(shapes),
            compiler_params=params,
            cost_estimate=weight(0),
            name="decode",
        )(dec_rows, lhs, got[i], *after)
        after = [terms[0]]
        sums.append([])
        for r, j in [(r, j) for r in range(2) for j in range(1, half)] + [(1, 0)]:
            perm = [(d * 2 + c, (d + 2 * j) % n * 2 + (c ^ r)) for d in range(n) for c in range(2)]
            sums[i].append(lax.ppermute(terms[2 * j + r], ("src", "rep"), perm))
        sums[i].append(terms[0])

    begun = []
    begun = [add([0, 1], begun, 20)]
    return add([2], begun, 0)


def solution(mesh):
    in_specs = (
        P(("parts", "rep"), "src"),
        P("src", "tgt"),
        P("tgt"),
        P(None, None, "src", "tgt"),
        P(None, "tgt"),
        P(None, ("parts", "rep", "src"), "tgt"),
        P(("parts", "rep"), None),
    )
    out_specs = P(None, ("parts", "rep", "src"), "tgt")
    return jax.shard_map(body, mesh=mesh, in_specs=in_specs, out_specs=out_specs, check_vma=False)
```
